32 devices in a mesh: ctx: 16 (over z, x, core), fsdp: 2 (over y).
Axes of the slice: x: 2, y: 2, z: 4, core: 2. Of those that a mesh axis runs over, the one named last changes fastest.
Arguments:
- tokens: bfloat16 [12, 2048, 576], P('fsdp', 'ctx'), may hold values from -6 to 6
- cotangent: bfloat16 [12, 2048, 576], P('fsdp', 'ctx'), may hold values from -8 to 8
- pair_order: int32 [12, 16], P('fsdp'), may hold values from 0 to 15, each once within a row
- query_weight: float32 [576, 576], P('fsdp', 'ctx'), may hold values from -0.5 to 0.5
- key_master_weight: float32 [576, 192], P('fsdp', 'ctx'), may hold values from -0.25 to 0.25
- value_master_weight: float32 [576, 192], P('fsdp', 'ctx'), may hold values from -0.25 to 0.25
- output_weight: float32 [576, 576], P('fsdp', 'ctx'), may hold values from -1.5 to 1.5
- gate_weight: float32 [576, 1536], P('fsdp', 'ctx'), may hold values from -0.25 to 0.25
- up_weight: float32 [576, 1536], P('fsdp', 'ctx'), may hold values from -0.25 to 0.25
- down_weight: float32 [1536, 576], P('fsdp', 'ctx'), may hold values from -0.21875 to 0.21875
- norm_gains: float32 [576, 2], P('fsdp'), may hold values from 0.5 to 1.5
- query_first: float32 [576, 576], P('fsdp', 'ctx'), may hold values from -224 to 224
- key_first_moment: float32 [576, 192], P('fsdp', 'ctx'), may hold values from -448 to 448
- value_first_moment: float32 [576, 192], P('fsdp', 'ctx'), may hold values from -320 to 320
- output_first: float32 [576, 576], P('fsdp', 'ctx'), may hold values from -20 to 20
- gate_first: float32 [576, 1536], P('fsdp', 'ctx'), may hold values from -56 to 56
- up_first: float32 [576, 1536], P('fsdp', 'ctx'), may hold values from -56 to 56
- down_first: float32 [1536, 576], P('fsdp', 'ctx'), may hold values from -64 to 64
- gains_first: float32 [576, 2], P('fsdp'), may hold values from -256 to 256
- query_second: float32 [576, 576], P('fsdp', 'ctx'), may hold values from 5160.96 to 20643.84
- key_second_moment: float32 [576, 192], P('fsdp', 'ctx'), may hold values from 20643.84 to 82821.12
- value_second_moment: float32 [576, 192], P('fsdp', 'ctx'), may hold values from 11550.72 to 46448.64
- output_second: float32 [576, 576], P('fsdp', 'ctx'), may hold values from 51.6096 to 206.4384
- gate_second: float32 [576, 1536], P('fsdp', 'ctx'), may hold values from 321.9456 to 1292.6976
- up_second: float32 [576, 1536], P('fsdp', 'ctx'), may hold values from 321.9456 to 1292.6976
- down_second: float32 [1536, 576], P('fsdp', 'ctx'), may hold values from 464.4864 to 1862.8608
- gains_second: float32 [576, 2], P('fsdp'), may hold values from 454.656 to 1818.624
Outputs:
- block_output: float32 [12, 2048, 576], P('fsdp', 'ctx')
- input_gradient: float32 [12, 2048, 576], P('fsdp', 'ctx')
- query_next: float32 [576, 576], P('fsdp', 'ctx')
- key_next: float32 [576, 192], P('fsdp', 'ctx')
- value_next: float32 [576, 192], P('fsdp', 'ctx')
- output_next: float32 [576, 576], P('fsdp', 'ctx')
- gate_next: float32 [576, 1536], P('fsdp', 'ctx')
- up_next: float32 [576, 1536], P('fsdp', 'ctx')
- down_next: float32 [1536, 576], P('fsdp', 'ctx')
- gains_next: float32 [576, 2], P('fsdp')
- query_first_next: float32 [576, 576], P('fsdp', 'ctx')
- key_first_next: float32 [576, 192], P('fsdp', 'ctx')
- value_first_next: float32 [576, 192], P('fsdp', 'ctx')
- output_first_next: float32 [576, 576], P('fsdp', 'ctx')
- gate_first_next: float32 [576, 1536], P('fsdp', 'ctx')
- up_first_next: float32 [576, 1536], P('fsdp', 'ctx')
- down_first_next: float32 [1536, 576], P('fsdp', 'ctx')
- gains_first_next: float32 [576, 2], P('fsdp')
- query_second_next: float32 [576, 576], P('fsdp', 'ctx')
- key_second_next: float32 [576, 192], P('fsdp', 'ctx')
- value_second_next: float32 [576, 192], P('fsdp', 'ctx')
- output_second_next: float32 [576, 576], P('fsdp', 'ctx')
- gate_second_next: float32 [576, 1536], P('fsdp', 'ctx')
- up_second_next: float32 [576, 1536], P('fsdp', 'ctx')
- down_second_next: float32 [1536, 576], P('fsdp', 'ctx')
- gains_second_next: float32 [576, 2], P('fsdp')
The draws below stay inside these ranges and needn't reach their ends.
Inputs may be any that keep to these rules, and one draw needn't show every extreme that they name: `pair_order`: each row is a permutation of 0 to 15.
All inputs are finite; a program needn't handle non-finite values.
Results may differ from the reference program's by a relative error of at most 0.024.
Values may be sent and summed in bfloat16 or wider, within the bound.
No kernel may reach another device: no remote copies, remote signals or barrier semaphores. Data moves between devices by JAX's collectives and lax.ppermute only.
A program may use at most 192 MiB of HBM per device.

```python
import math
import jax
import jax.numpy as jnp
from jax import lax

MODEL_WIDTH = 576
FF = 1536
HEADS = 9
KV_HEADS = 3
HEAD_DIM = 64
BLK = 64
STEP = 10
LEN = 2048
SEQS = 12
TOTAL_TOKENS = 24576
HQ = 576
KEY_VALUE_WIDTH = 192
N_CTX = 16


def with_spikes(result, stream_key, source, target, shards_of, factor):
    def block_of(axis_at):
        return (jnp.arange(result.shape[axis_at]) // (result.shape[axis_at] // shards_of)).reshape((-1,) + (1,) * (result.ndim - 1 - axis_at))

    near = jax.random.permutation(stream_key, shards_of)[block_of(target)]
    other_side = (block_of(target) + shards_of // 2) % shards_of
    return jnp.where((block_of(source) == near) | (block_of(source) == other_side), factor * result, result)


def shard_levels(own_key, shape, cuts, least, top_value):
    level = 1.0
    for dim, blocks in cuts:
        draws = jax.random.uniform(jax.random.fold_in(jax.random.fold_in(own_key, 6), dim), (blocks,), jnp.float32, least / len(cuts), top_value / len(cuts))
        level = level * jnp.repeat(jnp.exp(draws), shape[dim] // blocks).reshape((-1,) + (1,) * (len(shape) - 1 - dim))
    return level


def centred(stream_key, dims, spread, most, shards=(), kind=jnp.bfloat16):
    level = shard_levels(stream_key, dims, shards, -0.22, 0.18) if shards else 1.0
    array = jax.random.normal(stream_key, dims, jnp.float32) * spread * level
    return jnp.minimum(jnp.maximum(array, -most), most).astype(kind)


def bell_draw_with(stream_key, shape, width, most, cuts, heavy, kind=jnp.bfloat16):
    array = width * jax.random.normal(stream_key, shape, jnp.float32)
    if cuts:
        array = array * shard_levels(stream_key, shape, cuts, -0.22, 0.18)
    return jnp.clip(with_spikes(array, jax.random.fold_in(stream_key, 3), *heavy), -most, most).astype(kind)


def setup_inputs(seed: int = 0) -> dict:
    arg_keys = jax.random.split(jax.random.key(seed), 28)
    return {
        "tokens": centred(arg_keys[0], (SEQS, LEN, MODEL_WIDTH), 1.0, 6.0, ((0, 2), (1, 16))),
        "cotangent": bell_draw_with(arg_keys[1], (SEQS, LEN, MODEL_WIDTH), 1.0, 8.0, ((0, 2), (1, 16)), (1, 2, 16, 2.0)),
        "pair_order": jax.vmap(lambda own: jax.random.permutation(own, N_CTX))(jax.random.split(arg_keys[2], SEQS)).reshape((SEQS, N_CTX)).astype(jnp.int32),
        "query_weight": centred(arg_keys[3], (MODEL_WIDTH, HQ), (MODEL_WIDTH // 4) ** -0.5, 0.5, ((0, 2), (1, 16)), jnp.float32),
        "key_master_weight": centred(arg_keys[4], (MODEL_WIDTH, KEY_VALUE_WIDTH), MODEL_WIDTH ** -0.5, 0.25, ((0, 2), (1, 16)), jnp.float32),
        "value_master_weight": centred(arg_keys[5], (MODEL_WIDTH, KEY_VALUE_WIDTH), MODEL_WIDTH ** -0.5, 0.25, ((0, 2), (1, 16)), jnp.float32),
        "output_weight": centred(arg_keys[6], (HQ, MODEL_WIDTH), (MODEL_WIDTH // 32) ** -0.5, 1.5, ((0, 2), (1, 16)), jnp.float32),
        "gate_weight": centred(arg_keys[7], (MODEL_WIDTH, FF), MODEL_WIDTH ** -0.5, 0.25, ((0, 2), (1, 16)), jnp.float32),
        "up_weight": centred(arg_keys[8], (MODEL_WIDTH, FF), MODEL_WIDTH ** -0.5, 0.25, ((0, 2), (1, 16)), jnp.float32),
        "down_weight": centred(arg_keys[9], (FF, MODEL_WIDTH), (FF // 2) ** -0.5, 0.21875, ((0, 2), (1, 16)), jnp.float32),
        "norm_gains": jnp.clip(1.0 + 0.1 * jax.random.normal(arg_keys[10], (MODEL_WIDTH, 2), jnp.float32), 0.5, 1.5),
        "query_first": centred(arg_keys[11], (MODEL_WIDTH, HQ), (0.222 * TOTAL_TOKENS ** 0.5), 224.0, ((0, 2), (1, 16)), jnp.float32),
        "key_first_moment": centred(arg_keys[12], (MODEL_WIDTH, KEY_VALUE_WIDTH), (0.444 * TOTAL_TOKENS ** 0.5), 448.0, ((0, 2), (1, 16)), jnp.float32),
        "value_first_moment": centred(arg_keys[13], (MODEL_WIDTH, KEY_VALUE_WIDTH), (0.333 * TOTAL_TOKENS ** 0.5), 320.0, ((0, 2), (1, 16)), jnp.float32),
        "output_first": centred(arg_keys[14], (HQ, MODEL_WIDTH), (0.0222 * TOTAL_TOKENS ** 0.5), 20.0, ((0, 2), (1, 16)), jnp.float32),
        "gate_first": centred(arg_keys[15], (MODEL_WIDTH, FF), (0.0555 * TOTAL_TOKENS ** 0.5), 56.0, ((0, 2), (1, 16)), jnp.float32),
        "up_first": centred(arg_keys[16], (MODEL_WIDTH, FF), (0.0555 * TOTAL_TOKENS ** 0.5), 56.0, ((0, 2), (1, 16)), jnp.float32),
        "down_first": centred(arg_keys[17], (FF, MODEL_WIDTH), (0.0666 * TOTAL_TOKENS ** 0.5), 64.0, ((0, 2), (1, 16)), jnp.float32),
        "gains_first": centred(arg_keys[18], (MODEL_WIDTH, 2), (0.2775 * TOTAL_TOKENS ** 0.5), 256.0, ((0, 2),), jnp.float32),
        "query_second": jnp.clip(jnp.exp(math.log(20643.84) - 1.3862944 * jax.random.uniform(arg_keys[19], (MODEL_WIDTH, HQ), jnp.float32) ** shard_levels(arg_keys[19], (MODEL_WIDTH, HQ), ((0, 2), (1, 16)), -0.2, 0.2)), 5160.96, 20643.84),
        "key_second_moment": jnp.clip(jnp.exp(math.log(82821.12) - 1.3892661 * jax.random.uniform(arg_keys[20], (MODEL_WIDTH, KEY_VALUE_WIDTH), jnp.float32) ** shard_levels(arg_keys[20], (MODEL_WIDTH, KEY_VALUE_WIDTH), ((0, 2), (1, 16)), -0.2, 0.2)), 20643.84, 82821.12),
        "value_second_moment": jnp.clip(jnp.exp(math.log(46448.64) - 1.39159945 * jax.random.uniform(arg_keys[21], (MODEL_WIDTH, KEY_VALUE_WIDTH), jnp.float32) ** shard_levels(arg_keys[21], (MODEL_WIDTH, KEY_VALUE_WIDTH), ((0, 2), (1, 16)), -0.2, 0.2)), 11550.72, 46448.64),
        "output_second": jnp.clip(jnp.exp(math.log(206.4384) - 1.3862944 * jax.random.uniform(arg_keys[22], (HQ, MODEL_WIDTH), jnp.float32) ** shard_levels(arg_keys[22], (HQ, MODEL_WIDTH), ((0, 2), (1, 16)), -0.2, 0.2)), 51.6096, 206.4384),
        "gate_second": jnp.clip(jnp.exp(math.log(1292.6976) - 1.39010395 * jax.random.uniform(arg_keys[23], (MODEL_WIDTH, FF), jnp.float32) ** shard_levels(arg_keys[23], (MODEL_WIDTH, FF), ((0, 2), (1, 16)), -0.2, 0.2)), 321.9456, 1292.6976),
        "up_second": jnp.clip(jnp.exp(math.log(1292.6976) - 1.39010395 * jax.random.uniform(arg_keys[24], (MODEL_WIDTH, FF), jnp.float32) ** shard_levels(arg_keys[24], (MODEL_WIDTH, FF), ((0, 2), (1, 16)), -0.2, 0.2)), 321.9456, 1292.6976),
        "down_second": jnp.clip(jnp.exp(math.log(1862.8608) - 1.3889364 * jax.random.uniform(arg_keys[25], (FF, MODEL_WIDTH), jnp.float32) ** shard_levels(arg_keys[25], (FF, MODEL_WIDTH), ((0, 2), (1, 16)), -0.2, 0.2)), 464.4864, 1862.8608),
        "gains_second": jnp.clip(jnp.exp(math.log(1818.624) - 1.3862944 * jax.random.uniform(arg_keys[26], (MODEL_WIDTH, 2), jnp.float32) ** shard_levels(arg_keys[26], (MODEL_WIDTH, 2), ((0, 2),), -0.2, 0.2)), 454.656, 1818.624),
    }


@jax.custom_vjp
def low(v):
    return lax.optimization_barrier(v.astype(jnp.bfloat16)).astype(jnp.float32)

@jax.custom_vjp
def low_back(v):
    return v

def low_keep(v):
    return (low(v), None)

def low_pass(kept, grad):
    return (grad,)

def back_keep(v):
    return (v, None)

def back_low(kept, grad):
    return (low(grad),)
low.defvjp(low_keep, low_pass)
low_back.defvjp(back_keep, back_low)
NORM_EPS = 1e-05
ROPE_BASE = 100000.0
BETA_ONE = 0.9
BETA_TWO = 0.95
ADAM_EPS = 1e-08
DECAY = 0.1
GAIN_RATE = 0.5
MASKED = -1e+30
HIGH = lax.Precision.HIGHEST

def rotate(field, cosine, sine):
    half_dim = field.shape[-1] // 2
    first_half = field[..., :half_dim]
    second_half = field[..., half_dim:]
    return jnp.concatenate([first_half * cosine - second_half * sine, second_half * cosine + first_half * sine], axis=-1)

def tables(places):
    half_dim = HEAD_DIM // 2
    inverse = ROPE_BASE ** (-jnp.arange(half_dim, dtype=jnp.float32) * 2.0 / HEAD_DIM)
    angle = places.astype(jnp.float32)[..., None] * inverse
    return (jnp.cos(angle), jnp.sin(angle))

def positions(pair_order):
    within = jnp.arange(BLK, dtype=jnp.int32)
    early = pair_order[:, :, None] * BLK + within[None, None, :]
    late = (2 * N_CTX - 1 - pair_order)[:, :, None] * BLK + within[None, None, :]
    return jnp.concatenate([early, late], axis=2).reshape(pair_order.shape[0], LEN).astype(jnp.int32)

def sequence_forward(inputs, places, weights):
    full_query, full_key, full_value, full_output, full_gate, full_up, full_down, gains = weights
    group = HEADS // KV_HEADS
    factor = HEAD_DIM ** (-0.5)
    inv_one = lax.rsqrt(lax.optimization_barrier(jnp.mean(inputs * inputs, axis=-1, keepdims=True)) + NORM_EPS)
    normed_one = low(inputs * inv_one * gains[:, 0])
    query_raw = low_back(jnp.dot(normed_one, full_query, precision=HIGH))
    key_raw = low_back(jnp.dot(normed_one, full_key, precision=HIGH))
    value_low = low_back(low(jnp.dot(normed_one, full_value, precision=HIGH)))
    cosine, sine = tables(places)
    cosine = cosine[:, None, :]
    sine = sine[:, None, :]
    query_rot = low(rotate(query_raw.reshape(LEN, HEADS, HEAD_DIM), cosine, sine)).reshape(LEN, KV_HEADS, group, HEAD_DIM)
    key_rot = low(rotate(key_raw.reshape(LEN, KV_HEADS, HEAD_DIM), cosine, sine))
    value_heads = value_low.reshape(LEN, KV_HEADS, HEAD_DIM)
    block_rows = min(512, LEN)

    def attend(block_index):
        begin_row = block_index * block_rows
        query_block = lax.dynamic_slice_in_dim(query_rot, begin_row, block_rows, 0)
        query_places = lax.dynamic_slice_in_dim(places, begin_row, block_rows, 0)
        scores = low_back(jnp.einsum('rjgd,tjd->jgrt', query_block, key_rot, precision=HIGH) * factor)
        allowed = places[None, :] <= query_places[:, None]
        scores = jnp.where(allowed[None, None], scores, MASKED)
        row_top = lax.optimization_barrier(jnp.max(scores, axis=-1, keepdims=True))
        weight = jnp.exp(scores - row_top)
        prob_low = low(weight / lax.optimization_barrier(jnp.sum(weight, axis=-1, keepdims=True)))
        mixed = jnp.einsum('jgrt,tjd->rjgd', prob_low, value_heads, precision=HIGH)
        return mixed.reshape(block_rows, HEADS * HEAD_DIM)
    attended = lax.map(jax.checkpoint(attend), jnp.arange(LEN // block_rows)).reshape(LEN, HEADS * HEAD_DIM)
    attn_low = low_back(low(attended))
    resid_one = inputs + low_back(jnp.dot(attn_low, full_output, precision=HIGH))
    inv_two = lax.rsqrt(lax.optimization_barrier(jnp.mean(resid_one * resid_one, axis=-1, keepdims=True)) + NORM_EPS)
    normed_two = low(resid_one * inv_two * gains[:, 1])
    gate_raw = low_back(jnp.dot(normed_two, full_gate, precision=HIGH))
    up_raw = low_back(jnp.dot(normed_two, full_up, precision=HIGH))
    hidden_low = low(jax.nn.silu(gate_raw) * up_raw)
    return resid_one + low_back(jnp.dot(hidden_low, full_down, precision=HIGH))

def adam_update(weight, first, second, grad, rate, decay):
    first_next = BETA_ONE * first + (1.0 - BETA_ONE) * grad
    second_next = BETA_TWO * second + (1.0 - BETA_TWO) * grad * grad
    first_fix = first_next / (1.0 - BETA_ONE ** STEP)
    second_fix = second_next / (1.0 - BETA_TWO ** STEP)
    update = first_fix / (jnp.sqrt(second_fix) + ADAM_EPS) + decay * weight
    return (weight - rate * update, first_next, second_next)

def reference(tokens, cotangent, pair_order, query_weight, key_master_weight, value_master_weight, output_weight, gate_weight, up_weight, down_weight, norm_gains, query_first, key_first_moment, value_first_moment, output_first, gate_first, up_first, down_first, gains_first, query_second, key_second_moment, value_second_moment, output_second, gate_second, up_second, down_second, gains_second):
    places_all = positions(pair_order)

    def forward(inputs_all, *masters_in):
        weights = tuple((low(matrix) for matrix in masters_in))

        def one_sequence(paired):
            return sequence_forward(paired[0], paired[1], weights)
        return lax.map(jax.checkpoint(one_sequence), (inputs_all, places_all))
    masters = (query_weight, key_master_weight, value_master_weight, output_weight, gate_weight, up_weight, down_weight, norm_gains)
    block_output, pull = jax.vjp(forward, tokens.astype(jnp.float32), *masters)
    grads = pull(cotangent.astype(jnp.float32))
    rates = ((MODEL_WIDTH // 4) ** (-0.5), MODEL_WIDTH ** (-0.5), MODEL_WIDTH ** (-0.5), (MODEL_WIDTH // 32) ** (-0.5), MODEL_WIDTH ** (-0.5), MODEL_WIDTH ** (-0.5), (FF // 2) ** (-0.5), GAIN_RATE)
    decays = (DECAY, DECAY, DECAY, DECAY, DECAY, DECAY, DECAY, 0.0)
    firsts = (query_first, key_first_moment, value_first_moment, output_first, gate_first, up_first, down_first, gains_first)
    seconds = (query_second, key_second_moment, value_second_moment, output_second, gate_second, up_second, down_second, gains_second)
    updated = [adam_update(masters[member], firsts[member], seconds[member], grads[member + 1], rates[member], decays[member]) for member in range(8)]
    return (block_output, grads[0], updated[0][0], updated[1][0], updated[2][0], updated[3][0], updated[4][0], updated[5][0], updated[6][0], updated[7][0], updated[0][1], updated[1][1], updated[2][1], updated[3][1], updated[4][1], updated[5][1], updated[6][1], updated[7][1], updated[0][2], updated[1][2], updated[2][2], updated[3][2], updated[4][2], updated[5][2], updated[6][2], updated[7][2])
```

```python
import functools

import jax
import jax.numpy as jnp
from jax import lax
from jax.experimental import pallas as pl
from jax.experimental.pallas import tpu as pltpu
from jax.sharding import PartitionSpec as P

MODEL_WIDTH = 576
FF = 1536
HEADS = 9
KV_HEADS = 3
HEAD_DIM = 64
STEP = 10
GROUP = HEADS // KV_HEADS
KEY_WIDTH = KV_HEADS * HEAD_DIM
QUERY_WIDTH = HEADS * HEAD_DIM
PACK = 2 * HEAD_DIM
KV_PACKED = KV_HEADS * PACK
TILE = 256
FF_CHUNK = 512

NORM_EPS = 1e-05
ROPE_BASE = 100000.0
BETA_ONE = 0.9
BETA_TWO = 0.95
ADAM_EPS = 1e-08
DECAY = 0.1
GAIN_RATE = 0.5
MASKED = -1e30
VMEM_BYTES = 56 * 1024 * 1024

f32 = jnp.float32
bf16 = jnp.bfloat16


def dot_nt(a, b):
    return lax.dot_general(a, b, (((1,), (1,)), ((), ())), preferred_element_type=f32)


def dot_nn(a, b):
    return lax.dot_general(a, b, (((1,), (0,)), ((), ())), preferred_element_type=f32)


def lanes_of(shape):
    return lax.broadcasted_iota(jnp.int32, shape, len(shape) - 1)


def turned(v, first):
    lane = lanes_of(v.shape) % HEAD_DIM
    ahead = pltpu.roll(v, PACK - HEAD_DIM // 2, 1)
    behind = pltpu.roll(v, HEAD_DIM // 2, 1)
    if first:
        return jnp.where(lane < HEAD_DIM // 2, -ahead, behind)
    return jnp.where(lane < HEAD_DIM // 2, ahead, -behind)


def project_kernel(x_ref, gain_ref, weight_ref, cos_ref, sin_ref, normed_ref, query_ref, kv_ref):
    rows = x_ref.shape[1]
    blk = query_ref.shape[3] // GROUP
    x = x_ref[0].astype(f32)
    inv = lax.rsqrt(jnp.mean(x * x, axis=-1, keepdims=True) + NORM_EPS)
    normed = (x * inv * gain_ref[...]).astype(bf16)
    normed_ref[0] = normed
    raw = dot_nt(normed, weight_ref[...])
    cosine, sine = cos_ref[0], sin_ref[0]
    low_half = lanes_of((rows, PACK)) < HEAD_DIM
    for j in range(KV_HEADS):
        part = raw[:, j * PACK : (j + 1) * PACK]
        spun = part * cosine + turned(part, True) * sine
        kv_ref[0, :, j * PACK : (j + 1) * PACK] = jnp.where(low_half, spun, part).astype(bf16)
    for i in range((HEADS + 1) // 2):
        begin = KV_PACKED + i * PACK
        if 2 * i + 1 < HEADS:
            part = raw[:, begin : begin + PACK]
        else:
            tail = raw[:, begin : begin + HEAD_DIM]
            part = jnp.concatenate([tail, tail], axis=1)
        spun = part * cosine + turned(part, True) * sine
        spun = spun.astype(bf16).astype(f32) * (HEAD_DIM**-0.5)
        pair = [jnp.where(low_half, spun, 0.0)]
        if 2 * i + 1 < HEADS:
            pair.append(jnp.where(low_half, pltpu.roll(spun, HEAD_DIM, 1), 0.0))
        for offset, value in enumerate(pair):
            head = 2 * i + offset
            j, member = head // GROUP, head % GROUP
            value = value.astype(bf16)
            for b in range(rows // blk):
                query_ref[0, b, j, member * blk : (member + 1) * blk, :] = value[
                    b * blk : (b + 1) * blk
                ]


def sort_blocks(blocks_ref, s, kv_ref, sorted_ref, blk):
    chunks, _, rows, _ = kv_ref.shape
    per = rows // blk
    for g in range(chunks):
        for b in range(per):
            place = pl.multiple_of(blocks_ref[s, g * per + b] * blk, blk)
            sorted_ref[pl.ds(place, blk), :] = kv_ref[g, 0, b * blk : (b + 1) * blk, :]


def allowed_mask(place, tile_begin, blk, rows):
    row = lax.broadcasted_iota(jnp.int32, (rows, TILE), 0) % blk
    col = lax.broadcasted_iota(jnp.int32, (rows, TILE), 1)
    return col <= row + (place * blk - tile_begin)


def attend_kernel(
    blocks_ref, own_ref, query_ref, kv_ref, out_ref, log_ref, sorted_ref, score_ref, top_ref, acc_ref
):
    s = pl.program_id(0)
    per, rows = query_ref.shape[1], query_ref.shape[3]
    blk = rows // GROUP
    sort_blocks(blocks_ref, s, kv_ref, sorted_ref, blk)
    lane = lanes_of((TILE, PACK))
    for b in range(per):
        place = own_ref[s, b]
        full = (place * blk) // TILE

        def score_tile(t, masked):
            begin = pl.multiple_of(t * TILE, TILE)
            for j in range(KV_HEADS):
                kv = sorted_ref[pl.ds(begin, TILE), j * PACK : (j + 1) * PACK]
                score = dot_nt(query_ref[0, b, j], kv)
                if masked:
                    score = jnp.where(allowed_mask(place, begin, blk, rows), score, MASKED)
                score_ref[j, t] = score
                best = jnp.maximum(score[:, :PACK], score[:, PACK:])
                top_ref[j] = jnp.maximum(top_ref[j], best)

        top_ref[...] = jnp.full(top_ref.shape, MASKED, f32)
        acc_ref[...] = jnp.zeros(acc_ref.shape, f32)

        @pl.loop(0, full)
        def _(t):
            score_tile(t, False)

        score_tile(full, True)
        for j in range(KV_HEADS):
            top = jnp.max(top_ref[j], axis=-1, keepdims=True)
            top_ref[j] = jnp.broadcast_to(top, (rows, PACK))

        @pl.loop(0, full + 1)
        def _(t):
            begin = pl.multiple_of(t * TILE, TILE)
            for j in range(KV_HEADS):
                kv = sorted_ref[pl.ds(begin, TILE), j * PACK : (j + 1) * PACK]
                ones_v = jnp.where(lane < HEAD_DIM, jnp.ones((), bf16), kv)
                top = top_ref[j]
                score = score_ref[j, t]
                prob = jnp.concatenate(
                    [jnp.exp(score[:, :PACK] - top), jnp.exp(score[:, PACK:] - top)], axis=1
                )
                acc_ref[j] += dot_nn(prob.astype(bf16), ones_v)

        for j in range(KV_HEADS):
            acc = acc_ref[j]
            low_half = lanes_of(acc.shape) < HEAD_DIM
            total = jnp.where(low_half, acc, pltpu.roll(acc, HEAD_DIM, 1))
            log_ref[0, b, j] = top_ref[j] + jnp.log(total)
            attended = (acc / total).astype(bf16)
            for member in range(GROUP):
                head = j * GROUP + member
                out_ref[0, b * blk : (b + 1) * blk, head * HEAD_DIM : (head + 1) * HEAD_DIM] = (
                    attended[member * blk : (member + 1) * blk, HEAD_DIM:]
                )


def middle_kernel(
    x_ref,
    attn_ref,
    cot_ref,
    gain_ref,
    out_w_ref,
    gate_w_ref,
    up_w_ref,
    down_w_ref,
    block_ref,
    normed_ref,
    hidden_ref,
    dgate_ref,
    dup_ref,
    dattn_ref,
    dout_ref,
    dresid_ref,
    gain_grad_ref,
):
    attn = attn_ref[0]
    cot = cot_ref[0]
    resid = x_ref[0].astype(f32) + dot_nt(attn, out_w_ref[...])
    inv = lax.rsqrt(jnp.mean(resid * resid, axis=-1, keepdims=True) + NORM_EPS)
    hat = resid * inv
    gain = gain_ref[...]
    normed = (hat * gain).astype(bf16)
    normed_ref[0] = normed
    block = resid
    dnormed = jnp.zeros(resid.shape, f32)
    for begin in range(0, FF, FF_CHUNK):
        span = slice(begin, begin + FF_CHUNK)
        gate = dot_nt(normed, gate_w_ref[span, :])
        up = dot_nt(normed, up_w_ref[span, :])
        sig = 1.0 / (1.0 + jnp.exp(-gate))
        act = gate * sig
        hidden = (act * up).astype(bf16)
        hidden_ref[0, :, span] = hidden
        block = block + dot_nt(hidden, down_w_ref[:, span])
        dhidden = dot_nn(cot, down_w_ref[:, span])
        dgate = (dhidden * up * (sig * (1.0 + gate * (1.0 - sig)))).astype(bf16)
        dup = (dhidden * act).astype(bf16)
        dgate_ref[0, :, span] = dgate
        dup_ref[0, :, span] = dup
        dnormed = dnormed + dot_nn(dgate, gate_w_ref[span, :]) + dot_nn(dup, up_w_ref[span, :])
    block_ref[0] = block
    gain_grad_ref[0] = jnp.sum(dnormed * hat, axis=0, keepdims=True)
    scaled = dnormed * gain
    dresid = cot.astype(f32) + inv * (scaled - hat * jnp.mean(scaled * hat, axis=-1, keepdims=True))
    dresid_ref[0] = dresid
    dattn = dresid.astype(bf16)
    dattn_ref[0] = dattn
    dout_ref[0] = dot_nn(dattn, out_w_ref[...]).astype(bf16)


def attend_back_kernel(
    blocks_ref,
    own_ref,
    query_ref,
    kv_ref,
    out_ref,
    dout_ref,
    log_ref,
    cos_ref,
    sin_ref,
    dquery_ref,
    dkv_ref,
    sorted_ref,
    both_ref,
    flip_ref,
    delta_ref,
    dq_ref,
    dkv_t_ref,
    dkv_s_ref,
):
    s = pl.program_id(0)
    per, rows = query_ref.shape[1], query_ref.shape[3]
    blk = rows // GROUP
    length = sorted_ref.shape[0]
    sort_blocks(blocks_ref, s, kv_ref, sorted_ref, blk)
    dkv_t_ref[...] = jnp.zeros(dkv_t_ref.shape, f32)
    for b in range(per):
        place = own_ref[s, b]
        full = (place * blk) // TILE
        span = slice(b * blk, (b + 1) * blk)
        for j in range(KV_HEADS):
            both_ref[j, :rows] = query_ref[0, b, j]
            for member in range(GROUP):
                head = j * GROUP + member
                lanes = slice(head * HEAD_DIM, (head + 1) * HEAD_DIM)
                dout = dout_ref[0, span, lanes]
                delta = jnp.sum(
                    dout.astype(f32) * out_ref[0, span, lanes].astype(f32), axis=-1, keepdims=True
                )
                here = slice(member * blk, (member + 1) * blk)
                delta_ref[j, here] = jnp.broadcast_to(delta, (blk, PACK))
                both_ref[j, rows + member * blk : rows + (member + 1) * blk] = jnp.concatenate(
                    [jnp.zeros_like(dout), dout], axis=1
                )
            flip_ref[j] = both_ref[j].T
        dq_ref[...] = jnp.zeros(dq_ref.shape, f32)

        def tile_step(t, masked):
            begin = pl.multiple_of(t * TILE, TILE)
            for j in range(KV_HEADS):
                kv = sorted_ref[pl.ds(begin, TILE), j * PACK : (j + 1) * PACK]
                score = dot_nt(both_ref[j, :rows], kv)
                dprob = dot_nt(both_ref[j, rows:], kv)
                log_total = log_ref[0, b, j]
                delta = delta_ref[j]
                prob = jnp.concatenate(
                    [jnp.exp(score[:, :PACK] - log_total), jnp.exp(score[:, PACK:] - log_total)],
                    axis=1,
                )
                if masked:
                    prob = jnp.where(allowed_mask(place, begin, blk, rows), prob, 0.0)
                dscore = prob * jnp.concatenate(
                    [dprob[:, :PACK] - delta, dprob[:, PACK:] - delta], axis=1
                )
                dscore = dscore.astype(bf16)
                dq_ref[j] += dot_nn(dscore, kv)
                joint = jnp.concatenate([dscore, prob.astype(bf16)], axis=0)
                dkv_t_ref[j * PACK : (j + 1) * PACK, pl.ds(begin, TILE)] += dot_nn(
                    flip_ref[j], joint
                )

        @pl.loop(0, full)
        def _(t):
            tile_step(t, False)

        tile_step(full, True)
        cosine, sine = cos_ref[0, span, :], sin_ref[0, span, :]
        for j in range(KV_HEADS):
            for member in range(GROUP):
                head = j * GROUP + member
                grad = dq_ref[j, member * blk : (member + 1) * blk]
                back = (grad * cosine + turned(grad, False) * sine) * (HEAD_DIM**-0.5)
                dquery_ref[0, span, head * HEAD_DIM : (head + 1) * HEAD_DIM] = back[
                    :, :HEAD_DIM
                ].astype(bf16)
    for begin in range(0, length, TILE):
        dkv_s_ref[begin : begin + TILE, :] = dkv_t_ref[:, begin : begin + TILE].T.astype(bf16)
    for g in range(kv_ref.shape[0]):
        for b in range(per):
            place = pl.multiple_of(blocks_ref[s, g * per + b] * blk, blk)
            dkv_ref[g, 0, b * blk : (b + 1) * blk, :] = dkv_s_ref[pl.ds(place, blk), :]


def final_kernel(
    x_ref,
    gain_ref,
    dquery_ref,
    dkv_ref,
    dresid_ref,
    cos_ref,
    sin_ref,
    weight_ref,
    dinput_ref,
    dall_ref,
    gain_grad_ref,
):
    rows = x_ref.shape[1]
    cosine, sine = cos_ref[0], sin_ref[0]
    low_half = lanes_of((rows, PACK)) < HEAD_DIM
    for j in range(KV_HEADS):
        part = dkv_ref[0, :, j * PACK : (j + 1) * PACK].astype(f32)
        back = part * cosine + turned(part, False) * sine
        dall_ref[0, :, j * PACK : (j + 1) * PACK] = jnp.where(low_half, back, part).astype(bf16)
    dall_ref[0, :, KV_PACKED:] = dquery_ref[0]
    dnormed = dot_nn(dall_ref[0], weight_ref[...])
    x = x_ref[0].astype(f32)
    inv = lax.rsqrt(jnp.mean(x * x, axis=-1, keepdims=True) + NORM_EPS)
    hat = x * inv
    gain_grad_ref[0] = jnp.sum(dnormed * hat, axis=0, keepdims=True)
    scaled = dnormed * gain_ref[...]
    dinput_ref[0] = dresid_ref[0] + inv * (
        scaled - hat * jnp.mean(scaled * hat, axis=-1, keepdims=True)
    )


def one(shape):
    rest = tuple(shape[1:])
    return pl.BlockSpec((1,) + rest, lambda s, *_: (s,) + (0,) * len(rest))


def whole(shape):
    return pl.BlockSpec(tuple(shape), lambda s, *_: (0,) * len(shape))


def second(shape):
    rest = tuple(shape[2:])
    return pl.BlockSpec((shape[0], 1) + rest, lambda s, *_: (0, s) + (0,) * len(rest))


def call(kernel, seqs, inputs, outputs, scalars=(), scratch=(), flops=0):
    in_specs = [make(array.shape) for make, array in inputs]
    out_specs = [make(shape) for make, shape, _ in outputs]
    moved = sum(array.size * array.dtype.itemsize for _, array in inputs)
    for _, shape, kind in outputs:
        count = 1
        for size in shape:
            count *= size
        moved += count * jnp.dtype(kind).itemsize
    return pl.pallas_call(
        kernel,
        grid_spec=pltpu.PrefetchScalarGridSpec(
            num_scalar_prefetch=len(scalars),
            grid=(seqs,),
            in_specs=in_specs,
            out_specs=out_specs,
            scratch_shapes=list(scratch),
        ),
        out_shape=[jax.ShapeDtypeStruct(shape, kind) for _, shape, kind in outputs],
        compiler_params=pltpu.CompilerParams(vmem_limit_bytes=VMEM_BYTES),
        cost_estimate=pl.CostEstimate(
            flops=int(flops), bytes_accessed=int(moved), transcendentals=0
        ),
    )(*scalars, *[array for _, array in inputs])


def adam_update(weight, first, second, grad, rate, decay):
    first_next = BETA_ONE * first + (1.0 - BETA_ONE) * grad
    second_next = BETA_TWO * second + (1.0 - BETA_TWO) * grad * grad
    first_fix = first_next / (1.0 - BETA_ONE**STEP)
    second_fix = second_next / (1.0 - BETA_TWO**STEP)
    update = first_fix / (jnp.sqrt(second_fix) + ADAM_EPS) + decay * weight
    return (weight - rate * update, first_next, second_next)


def gather_packed(packed):
    ctx, fsdp = lax.axis_size("ctx"), lax.axis_size("fsdp")
    rows, lanes = packed.shape
    every = lax.all_gather(packed, ("ctx", "fsdp"), axis=0, tiled=False)
    every = every.reshape(ctx, fsdp, rows, lanes).transpose(0, 2, 1, 3)
    return every.reshape(ctx, rows, fsdp * lanes)


def scatter_packed(grads):
    ctx, fsdp = lax.axis_size("ctx"), lax.axis_size("fsdp")
    rows, lanes = grads.shape[1], grads.shape[2] // fsdp
    split = grads.astype(bf16).reshape(ctx, rows, fsdp, lanes).transpose(0, 2, 1, 3)
    split = split.reshape(ctx * fsdp, rows, lanes)
    return lax.psum_scatter(split, ("ctx", "fsdp"), scatter_dimension=0, tiled=False).astype(f32)


def weight_grad(left, right):
    return lax.dot_general(left, right, (((0, 1), (0, 1)), ((), ())), preferred_element_type=f32)


def body(
    tokens,
    cotangent,
    pair_order,
    query_weight,
    key_master_weight,
    value_master_weight,
    output_weight,
    gate_weight,
    up_weight,
    down_weight,
    norm_gains,
    query_first,
    key_first_moment,
    value_first_moment,
    output_first,
    gate_first,
    up_first,
    down_first,
    gains_first,
    query_second,
    key_second_moment,
    value_second_moment,
    output_second,
    gate_second,
    up_second,
    down_second,
    gains_second,
):
    masters = (
        query_weight,
        key_master_weight,
        value_master_weight,
        output_weight,
        gate_weight,
        up_weight,
        down_weight,
    )
    ctx = lax.axis_size("ctx")
    index = lax.axis_index("ctx")
    chunks = ctx // 2
    core = index % 2
    seqs = tokens.shape[0] // 2
    part_rows = tokens.shape[1]
    rows = 2 * part_rows
    blk = part_rows // 2
    per = rows // blk
    length = part_rows * ctx
    mine, other = core * seqs, (1 - core) * seqs
    partners = [(i, i ^ 1) for i in range(ctx)]
    cores = [list(range(0, ctx, 2)), list(range(1, ctx, 2))]

    def take(array):
        own = lax.dynamic_slice_in_dim(array, mine, seqs, 0)
        got = lax.ppermute(lax.dynamic_slice_in_dim(array, other, seqs, 0), "ctx", partners)
        return jnp.concatenate([own, got], axis=1)

    def give(array):
        got = lax.ppermute(array[:, part_rows:], "ctx", partners)
        result = jnp.zeros((2 * seqs, part_rows) + array.shape[2:], array.dtype)
        result = lax.dynamic_update_slice_in_dim(result, array[:, :part_rows], mine, 0)
        return lax.dynamic_update_slice_in_dim(result, got, other, 0)

    turned_low = [matrix.astype(bf16).T for matrix in masters]
    gains_low = norm_gains.astype(bf16).T
    first_pack = gather_packed(jnp.concatenate(turned_low[:3] + [gains_low], axis=0))
    second_pack = gather_packed(jnp.concatenate(turned_low[3:6], axis=0))
    down_t = gather_packed(turned_low[6]).reshape(MODEL_WIDTH, FF)
    q_cols, kv_cols = QUERY_WIDTH // ctx, KEY_WIDTH // ctx
    query_t = first_pack[:, :q_cols].reshape(QUERY_WIDTH, MODEL_WIDTH)
    key_t = first_pack[:, q_cols : q_cols + kv_cols].reshape(KV_HEADS, HEAD_DIM, MODEL_WIDTH)
    value_t = first_pack[:, q_cols + kv_cols : q_cols + 2 * kv_cols].reshape(
        KV_HEADS, HEAD_DIM, MODEL_WIDTH
    )
    gains = first_pack[0, q_cols + 2 * kv_cols :].astype(f32)
    gain_one, gain_two = gains[0:1], gains[1:2]
    inward = jnp.concatenate(
        [jnp.stack([key_t, value_t], axis=1).reshape(KV_PACKED, MODEL_WIDTH), query_t], axis=0
    )
    o_cols, f_cols = MODEL_WIDTH // ctx, FF // ctx
    output_t = second_pack[:, :o_cols].reshape(MODEL_WIDTH, QUERY_WIDTH)
    gate_t = second_pack[:, o_cols : o_cols + f_cols].reshape(FF, MODEL_WIDTH)
    up_t = second_pack[:, o_cols + f_cols :].reshape(FF, MODEL_WIDTH)

    x = take(tokens)
    cot = take(cotangent)
    order = lax.dynamic_slice_in_dim(pair_order, mine, seqs, 0)
    ends = jnp.stack([order, 2 * ctx - 1 - order], axis=2).reshape(seqs, chunks, 2, 2)
    ends = jnp.where(core == 0, ends, ends[:, :, ::-1])
    own = lax.dynamic_slice_in_dim(ends, index // 2, 1, 1).reshape(seqs, per)
    blocks = ends.reshape(seqs, chunks * per)
    places = (own[:, :, None] * blk + jnp.arange(blk, dtype=jnp.int32)).reshape(seqs, rows)
    half_dim = HEAD_DIM // 2
    inverse = ROPE_BASE ** (-jnp.arange(half_dim, dtype=f32) * 2.0 / HEAD_DIM)
    angle = places.astype(f32)[..., None] * inverse
    cosine = jnp.tile(jnp.cos(angle), (1, 1, PACK // half_dim))
    sine = jnp.tile(jnp.sin(angle), (1, 1, PACK // half_dim))

    wide = (seqs, rows, MODEL_WIDTH)
    heads = (seqs, per, KV_HEADS, GROUP * blk, PACK)
    normed_one, query, kv = call(
        project_kernel,
        seqs,
        [(one, x), (whole, gain_one), (whole, inward), (one, cosine), (one, sine)],
        [(one, wide, bf16), (one, heads, bf16), (one, (seqs, rows, KV_PACKED), bf16)],
        flops=2 * seqs * rows * MODEL_WIDTH * (KV_PACKED + QUERY_WIDTH),
    )
    kv_all = lax.all_gather(kv, "ctx", axis=0, tiled=False, axis_index_groups=cores)
    pairs = seqs * HEADS * rows * length * HEAD_DIM
    tile_rows = (KV_HEADS, GROUP * blk, PACK)
    attn, logs = call(
        attend_kernel,
        seqs,
        [(one, query), (second, kv_all)],
        [(one, wide, bf16), (one, heads, f32)],
        scalars=(blocks, own),
        scratch=[
            pltpu.VMEM((length, KV_PACKED), bf16),
            pltpu.VMEM((KV_HEADS, length // TILE, GROUP * blk, TILE), f32),
            pltpu.VMEM(tile_rows, f32),
            pltpu.VMEM(tile_rows, f32),
        ],
        flops=4 * pairs,
    )
    ff_wide = (seqs, rows, FF)
    (
        block_local,
        normed_two,
        hidden,
        dgate,
        dup,
        dattn,
        dout,
        dresid,
        gain_two_grad,
    ) = call(
        middle_kernel,
        seqs,
        [
            (one, x),
            (one, attn),
            (one, cot),
            (whole, gain_two),
            (whole, output_t),
            (whole, gate_t),
            (whole, up_t),
            (whole, down_t),
        ],
        [
            (one, wide, f32),
            (one, wide, bf16),
            (one, ff_wide, bf16),
            (one, ff_wide, bf16),
            (one, ff_wide, bf16),
            (one, wide, bf16),
            (one, wide, bf16),
            (one, wide, f32),
            (one, (seqs, 1, MODEL_WIDTH), f32),
        ],
        flops=2 * seqs * rows * MODEL_WIDTH * (6 * FF + 2 * MODEL_WIDTH),
    )
    block_output = give(block_local)
    down_grad = weight_grad(cot, hidden).reshape(ctx, o_cols, FF)
    gate_grad = weight_grad(dgate, normed_two).reshape(ctx, f_cols, MODEL_WIDTH)
    up_grad = weight_grad(dup, normed_two).reshape(ctx, f_cols, MODEL_WIDTH)
    output_grad = weight_grad(dattn, attn).reshape(ctx, o_cols, QUERY_WIDTH)
    down_sum = scatter_packed(down_grad)
    second_sum = scatter_packed(jnp.concatenate([output_grad, gate_grad, up_grad], axis=1))

    dquery, dkv = call(
        attend_back_kernel,
        seqs,
        [
            (one, query),
            (second, kv_all),
            (one, attn),
            (one, dout),
            (one, logs),
            (one, cosine),
            (one, sine),
        ],
        [(one, wide, bf16), (second, kv_all.shape, bf16)],
        scalars=(blocks, own),
        scratch=[
            pltpu.VMEM((length, KV_PACKED), bf16),
            pltpu.VMEM((KV_HEADS, 2 * GROUP * blk, PACK), bf16),
            pltpu.VMEM((KV_HEADS, PACK, 2 * GROUP * blk), bf16),
            pltpu.VMEM(tile_rows, f32),
            pltpu.VMEM(tile_rows, f32),
            pltpu.VMEM((KV_PACKED, length), f32),
            pltpu.VMEM((length, KV_PACKED), bf16),
        ],
        flops=10 * pairs,
    )
    dkv_own = lax.psum_scatter(
        dkv, "ctx", scatter_dimension=0, tiled=False, axis_index_groups=cores
    )
    inner = KV_PACKED + QUERY_WIDTH
    dinput, dall, gain_one_grad = call(
        final_kernel,
        seqs,
        [
            (one, x),
            (whole, gain_one),
            (one, dquery),
            (one, dkv_own),
            (one, dresid),
            (one, cosine),
            (one, sine),
            (whole, inward),
        ],
        [
            (one, wide, f32),
            (one, (seqs, rows, inner), bf16),
            (one, (seqs, 1, MODEL_WIDTH), f32),
        ],
        flops=2 * seqs * rows * MODEL_WIDTH * inner,
    )
    input_gradient = give(dinput)
    inward_grad = weight_grad(dall, normed_one)
    kv_grad = inward_grad[:KV_PACKED].reshape(KV_HEADS, 2, HEAD_DIM, MODEL_WIDTH)
    key_grad = kv_grad[:, 0].reshape(ctx, kv_cols, MODEL_WIDTH)
    value_grad = kv_grad[:, 1].reshape(ctx, kv_cols, MODEL_WIDTH)
    query_grad = inward_grad[KV_PACKED:].reshape(ctx, q_cols, MODEL_WIDTH)
    gains_grad = jnp.concatenate(
        [jnp.sum(gain_one_grad, axis=0), jnp.sum(gain_two_grad, axis=0)], axis=0
    )
    gains_grad = jnp.broadcast_to(gains_grad[None], (ctx, 2, MODEL_WIDTH))
    first_sum = scatter_packed(
        jnp.concatenate([query_grad, key_grad, value_grad, gains_grad], axis=1)
    )
    reduced = (
        first_sum[:q_cols],
        first_sum[q_cols : q_cols + kv_cols],
        first_sum[q_cols + kv_cols : q_cols + 2 * kv_cols],
        second_sum[:o_cols],
        second_sum[o_cols : o_cols + f_cols],
        second_sum[o_cols + f_cols :],
        down_sum,
    )
    gains_total = first_sum[q_cols + 2 * kv_cols :].T
    rates = (
        (MODEL_WIDTH // 4) ** (-0.5),
        MODEL_WIDTH ** (-0.5),
        MODEL_WIDTH ** (-0.5),
        (MODEL_WIDTH // 32) ** (-0.5),
        MODEL_WIDTH ** (-0.5),
        MODEL_WIDTH ** (-0.5),
        (FF // 2) ** (-0.5),
    )
    firsts = (
        query_first,
        key_first_moment,
        value_first_moment,
        output_first,
        gate_first,
        up_first,
        down_first,
    )
    seconds = (
        query_second,
        key_second_moment,
        value_second_moment,
        output_second,
        gate_second,
        up_second,
        down_second,
    )
    results = [
        adam_update(
            masters[member], firsts[member], seconds[member], reduced[member].T, rates[member], DECAY
        )
        for member in range(7)
    ]
    results.append(adam_update(norm_gains, gains_first, gains_second, gains_total, GAIN_RATE, 0.0))
    new_weights = [result[0] for result in results]
    new_firsts = [result[1] for result in results]
    new_seconds = [result[2] for result in results]
    return tuple([block_output, input_gradient] + new_weights + new_firsts + new_seconds)


def solution(mesh):
    sequences = P("fsdp", "ctx", None)
    matrix = P("fsdp", "ctx")
    gains = P("fsdp", None)
    state = (matrix,) * 7 + (gains,)
    return jax.shard_map(
        body,
        mesh=mesh,
        in_specs=(sequences, sequences, P("fsdp", None)) + state * 3,
        out_specs=(sequences, sequences) + state * 3,
        check_vma=False,
    )
```

```python
import functools

import jax
import jax.numpy as jnp
from jax import lax
from jax.experimental import pallas as pl
from jax.experimental.pallas import tpu as pltpu
from jax.sharding import PartitionSpec as P

MODEL_WIDTH = 576
FF = 1536
HEADS = 9
KV_HEADS = 3
HEAD_DIM = 64
STEP = 10
GROUP = HEADS // KV_HEADS
KEY_WIDTH = KV_HEADS * HEAD_DIM
QUERY_WIDTH = HEADS * HEAD_DIM
PACK = 2 * HEAD_DIM
KV_PACKED = KV_HEADS * PACK
TILE = 256
FF_CHUNK = 640
LANES = 640

NORM_EPS = 1e-05
ROPE_BASE = 100000.0
BETA_ONE = 0.9
BETA_TWO = 0.95
ADAM_EPS = 1e-08
DECAY = 0.1
GAIN_RATE = 0.5
MASKED = -1e30
VMEM_BYTES = 56 * 1024 * 1024

f32 = jnp.float32
bf16 = jnp.bfloat16


def dot_nt(a, b):
    return lax.dot_general(a, b, (((1,), (1,)), ((), ())), preferred_element_type=f32)


def dot_nn(a, b):
    return lax.dot_general(a, b, (((1,), (0,)), ((), ())), preferred_element_type=f32)


def lanes_of(shape):
    return lax.broadcasted_iota(jnp.int32, shape, len(shape) - 1)


def turned(v, first):
    lane = lanes_of(v.shape) % HEAD_DIM
    ahead = pltpu.roll(v, PACK - HEAD_DIM // 2, 1)
    behind = pltpu.roll(v, HEAD_DIM // 2, 1)
    if first:
        return jnp.where(lane < HEAD_DIM // 2, -ahead, behind)
    return jnp.where(lane < HEAD_DIM // 2, ahead, -behind)


def project_kernel(x_ref, gain_ref, weight_ref, cos_ref, sin_ref, normed_ref, query_ref, kv_ref):
    rows = x_ref.shape[1]
    blk = query_ref.shape[3] // GROUP
    x = x_ref[0].astype(f32)
    inv = lax.rsqrt(jnp.mean(x * x, axis=-1, keepdims=True) + NORM_EPS)
    normed = (x * inv * gain_ref[...]).astype(bf16)
    normed_ref[0] = normed
    raw = dot_nt(normed, weight_ref[...])
    cosine, sine = cos_ref[0], sin_ref[0]
    low_half = lanes_of((rows, PACK)) < HEAD_DIM
    for j in range(KV_HEADS):
        part = raw[:, j * PACK : (j + 1) * PACK]
        spun = part * cosine + turned(part, True) * sine
        kv_ref[0, :, j * PACK : (j + 1) * PACK] = jnp.where(low_half, spun, part).astype(bf16)
    for i in range((HEADS + 1) // 2):
        begin = KV_PACKED + i * PACK
        if 2 * i + 1 < HEADS:
            part = raw[:, begin : begin + PACK]
        else:
            tail = raw[:, begin : begin + HEAD_DIM]
            part = jnp.concatenate([tail, tail], axis=1)
        spun = part * cosine + turned(part, True) * sine
        spun = spun.astype(bf16).astype(f32) * (HEAD_DIM**-0.5)
        pair = [jnp.where(low_half, spun, 0.0)]
        if 2 * i + 1 < HEADS:
            pair.append(jnp.where(low_half, pltpu.roll(spun, HEAD_DIM, 1), 0.0))
        for offset, value in enumerate(pair):
            head = 2 * i + offset
            j, member = head // GROUP, head % GROUP
            value = value.astype(bf16)
            for b in range(rows // blk):
                query_ref[0, b, j, member * blk : (member + 1) * blk, :] = value[
                    b * blk : (b + 1) * blk
                ]


def sort_blocks(blocks_ref, kv_refs, sorted_ref, blk):
    per = kv_refs[0].shape[0] // blk
    for g, kv_ref in enumerate(kv_refs):
        for b in range(per):
            place = pl.multiple_of(blocks_ref[g * per + b] * blk, blk)
            sorted_ref[pl.ds(place, blk), :] = kv_ref[b * blk : (b + 1) * blk, :]


def allowed_mask(place, tile_begin, blk, rows):
    row = lax.broadcasted_iota(jnp.int32, (rows, TILE), 0) % blk
    col = lax.broadcasted_iota(jnp.int32, (rows, TILE), 1)
    return col <= row + (place * blk - tile_begin)


def attend_kernel(chunks, blocks_ref, query_ref, *refs):
    kv_refs = refs[:chunks]
    out_ref, log_ref, sorted_ref, score_ref, top_ref, acc_ref = refs[chunks:]
    per, rows = query_ref.shape[1], query_ref.shape[3]
    blk = rows // GROUP
    sort_blocks(blocks_ref, kv_refs, sorted_ref, blk)
    lane = lanes_of((TILE, PACK))
    for b in range(per):
        place = blocks_ref[b]
        full = (place * blk) // TILE

        def score_tile(t, masked):
            begin = pl.multiple_of(t * TILE, TILE)
            for j in range(KV_HEADS):
                kv = sorted_ref[pl.ds(begin, TILE), j * PACK : (j + 1) * PACK]
                score = dot_nt(query_ref[0, b, j], kv)
                if masked:
                    score = jnp.where(allowed_mask(place, begin, blk, rows), score, MASKED)
                score_ref[j, t] = score
                best = jnp.maximum(score[:, :PACK], score[:, PACK:])
                top_ref[j] = jnp.maximum(top_ref[j], best)

        top_ref[...] = jnp.full(top_ref.shape, MASKED, f32)
        acc_ref[...] = jnp.zeros(acc_ref.shape, f32)

        @pl.loop(0, full)
        def _(t):
            score_tile(t, False)

        score_tile(full, True)
        for j in range(KV_HEADS):
            top = jnp.max(top_ref[j], axis=-1, keepdims=True)
            top_ref[j] = jnp.broadcast_to(top, (rows, PACK))

        @pl.loop(0, full + 1)
        def _(t):
            begin = pl.multiple_of(t * TILE, TILE)
            for j in range(KV_HEADS):
                kv = sorted_ref[pl.ds(begin, TILE), j * PACK : (j + 1) * PACK]
                ones_v = jnp.where(lane < HEAD_DIM, jnp.ones((), bf16), kv)
                top = top_ref[j]
                score = score_ref[j, t]
                prob = jnp.concatenate(
                    [jnp.exp(score[:, :PACK] - top), jnp.exp(score[:, PACK:] - top)], axis=1
                )
                acc_ref[j] += dot_nn(prob.astype(bf16), ones_v)

        for j in range(KV_HEADS):
            acc = acc_ref[j]
            low_half = lanes_of(acc.shape) < HEAD_DIM
            total = jnp.where(low_half, acc, pltpu.roll(acc, HEAD_DIM, 1))
            log_ref[0, b, j] = top_ref[j] + jnp.log(total)
            attended = (acc / total).astype(bf16)
            for member in range(GROUP):
                head = j * GROUP + member
                out_ref[0, b * blk : (b + 1) * blk, head * HEAD_DIM : (head + 1) * HEAD_DIM] = (
                    attended[member * blk : (member + 1) * blk, HEAD_DIM:]
                )


def middle_kernel(
    x_ref,
    attn_ref,
    cot_ref,
    gain_ref,
    out_w_ref,
    gate_w_ref,
    up_w_ref,
    down_w_ref,
    block_ref,
    normed_ref,
    hidden_ref,
    dgate_ref,
    dup_ref,
    dattn_ref,
    dout_ref,
    dresid_ref,
    gain_grad_ref,
):
    attn = attn_ref[0]
    cot = cot_ref[0]
    resid = x_ref[0].astype(f32) + dot_nt(attn, out_w_ref[...])
    inv = lax.rsqrt(jnp.mean(resid * resid, axis=-1, keepdims=True) + NORM_EPS)
    hat = resid * inv
    gain = gain_ref[...]
    normed = (hat * gain).astype(bf16)
    normed_ref[0] = normed
    block = resid
    dnormed = jnp.zeros(resid.shape, f32)
    for begin in range(0, FF, FF_CHUNK):
        span = slice(begin, min(begin + FF_CHUNK, FF))
        gate = dot_nt(normed, gate_w_ref[span, :])
        up = dot_nt(normed, up_w_ref[span, :])
        sig = 1.0 / (1.0 + jnp.exp(-gate))
        act = gate * sig
        hidden = (act * up).astype(bf16)
        hidden_ref[0, :, span] = hidden
        block = block + dot_nt(hidden, down_w_ref[:, span])
        dhidden = dot_nn(cot, down_w_ref[:, span])
        dgate = (dhidden * up * (sig * (1.0 + gate * (1.0 - sig)))).astype(bf16)
        dup = (dhidden * act).astype(bf16)
        dgate_ref[0, :, span] = dgate
        dup_ref[0, :, span] = dup
        dnormed = dnormed + dot_nn(dgate, gate_w_ref[span, :]) + dot_nn(dup, up_w_ref[span, :])
    block_ref[0] = block
    gain_grad_ref[0] = jnp.sum(dnormed * hat, axis=0, keepdims=True)
    scaled = dnormed * gain
    dresid = cot.astype(f32) + inv * (scaled - hat * jnp.mean(scaled * hat, axis=-1, keepdims=True))
    dresid_ref[0] = dresid
    dattn = dresid.astype(bf16)
    dattn_ref[0] = dattn
    dout_ref[0] = dot_nn(dattn, out_w_ref[...]).astype(bf16)


def attend_back_kernel(chunks, blocks_ref, query_ref, *refs):
    kv_refs = refs[:chunks]
    out_ref, dout_ref, log_ref, cos_ref, sin_ref, dquery_ref = refs[chunks : chunks + 6]
    dkv_refs = refs[chunks + 6 : 2 * chunks + 6]
    sorted_ref, both_ref, flip_ref, delta_ref, dq_ref, dkv_t_ref, dkv_s_ref = refs[2 * chunks + 6 :]
    per, rows = query_ref.shape[1], query_ref.shape[3]
    blk = rows // GROUP
    length = sorted_ref.shape[0]
    sort_blocks(blocks_ref, kv_refs, sorted_ref, blk)
    dkv_t_ref[...] = jnp.zeros(dkv_t_ref.shape, f32)
    for b in range(per):
        place = blocks_ref[b]
        full = (place * blk) // TILE
        span = slice(b * blk, (b + 1) * blk)
        for j in range(KV_HEADS):
            both_ref[j, :rows] = query_ref[0, b, j]
            for member in range(GROUP):
                head = j * GROUP + member
                lanes = slice(head * HEAD_DIM, (head + 1) * HEAD_DIM)
                dout = dout_ref[0, span, lanes]
                delta = jnp.sum(
                    dout.astype(f32) * out_ref[0, span, lanes].astype(f32), axis=-1, keepdims=True
                )
                here = slice(member * blk, (member + 1) * blk)
                delta_ref[j, here] = jnp.broadcast_to(delta, (blk, PACK))
                both_ref[j, rows + member * blk : rows + (member + 1) * blk] = jnp.concatenate(
                    [jnp.zeros_like(dout), dout], axis=1
                )
            flip_ref[j] = both_ref[j].T
        dq_ref[...] = jnp.zeros(dq_ref.shape, f32)

        def tile_step(t, masked):
            begin = pl.multiple_of(t * TILE, TILE)
            for j in range(KV_HEADS):
                kv = sorted_ref[pl.ds(begin, TILE), j * PACK : (j + 1) * PACK]
                score = dot_nt(both_ref[j, :rows], kv)
                dprob = dot_nt(both_ref[j, rows:], kv)
                log_total = log_ref[0, b, j]
                delta = delta_ref[j]
                prob = jnp.concatenate(
                    [jnp.exp(score[:, :PACK] - log_total), jnp.exp(score[:, PACK:] - log_total)],
                    axis=1,
                )
                if masked:
                    prob = jnp.where(allowed_mask(place, begin, blk, rows), prob, 0.0)
                dscore = prob * jnp.concatenate(
                    [dprob[:, :PACK] - delta, dprob[:, PACK:] - delta], axis=1
                )
                dscore = dscore.astype(bf16)
                dq_ref[j] += dot_nn(dscore, kv)
                joint = jnp.concatenate([dscore, prob.astype(bf16)], axis=0)
                dkv_t_ref[j * PACK : (j + 1) * PACK, pl.ds(begin, TILE)] += dot_nn(
                    flip_ref[j], joint
                )

        @pl.loop(0, full)
        def _(t):
            tile_step(t, False)

        tile_step(full, True)
        cosine, sine = cos_ref[0, span, :], sin_ref[0, span, :]
        for j in range(KV_HEADS):
            for member in range(GROUP):
                head = j * GROUP + member
                grad = dq_ref[j, member * blk : (member + 1) * blk]
                back = (grad * cosine + turned(grad, False) * sine) * (HEAD_DIM**-0.5)
                dquery_ref[0, span, head * HEAD_DIM : (head + 1) * HEAD_DIM] = back[
                    :, :HEAD_DIM
                ].astype(bf16)
    for begin in range(0, length, TILE):
        dkv_s_ref[begin : begin + TILE, :] = dkv_t_ref[:, begin : begin + TILE].T.astype(bf16)
    for g, dkv_ref in enumerate(dkv_refs):
        for b in range(per):
            place = pl.multiple_of(blocks_ref[g * per + b] * blk, blk)
            dkv_ref[b * blk : (b + 1) * blk, :] = dkv_s_ref[pl.ds(place, blk), :]


def final_kernel(
    x_ref,
    gain_ref,
    dquery_ref,
    dkv_ref,
    dresid_ref,
    cos_ref,
    sin_ref,
    weight_ref,
    dinput_ref,
    dall_ref,
    gain_grad_ref,
):
    rows = x_ref.shape[1]
    cosine, sine = cos_ref[0], sin_ref[0]
    low_half = lanes_of((rows, PACK)) < HEAD_DIM
    for j in range(KV_HEADS):
        part = dkv_ref[0, :, j * PACK : (j + 1) * PACK].astype(f32)
        back = part * cosine + turned(part, False) * sine
        dall_ref[0, :, j * PACK : (j + 1) * PACK] = jnp.where(low_half, back, part).astype(bf16)
    dall_ref[0, :, KV_PACKED:] = dquery_ref[0]
    dnormed = dot_nn(dall_ref[0], weight_ref[...])
    x = x_ref[0].astype(f32)
    inv = lax.rsqrt(jnp.mean(x * x, axis=-1, keepdims=True) + NORM_EPS)
    hat = x * inv
    gain_grad_ref[0] = jnp.sum(dnormed * hat, axis=0, keepdims=True)
    scaled = dnormed * gain_ref[...]
    dinput_ref[0] = dresid_ref[0] + inv * (
        scaled - hat * jnp.mean(scaled * hat, axis=-1, keepdims=True)
    )


def natural_pieces(where_ref, own_ref, other_ref, begin, size):
    zero = where_ref[0] == 0
    pieces = []
    for g in range(own_ref.shape[0]):
        slot = where_ref[1 + g]
        mine = own_ref[slot, begin : begin + size, :].astype(f32)
        theirs = other_ref[slot, begin : begin + size, :].astype(f32)
        pieces.append(jnp.where(zero, mine, theirs))
        pieces.append(jnp.where(zero, theirs, mine))
    return jnp.concatenate(pieces, axis=0).astype(bf16)


def unpack_first_kernel(q_cols, kv_cols, where_ref, own_ref, other_ref, inward_ref):
    width = inward_ref.shape[1]
    query = natural_pieces(where_ref, own_ref, other_ref, 0, q_cols)
    inward_ref[KV_PACKED:, :] = query[:, :width]
    for offset in range(2):
        part = natural_pieces(where_ref, own_ref, other_ref, q_cols + offset * kv_cols, kv_cols)
        for j in range(KV_HEADS):
            begin = j * PACK + offset * HEAD_DIM
            inward_ref[begin : begin + HEAD_DIM, :] = part[
                j * HEAD_DIM : (j + 1) * HEAD_DIM, :width
            ]


def unpack_second_kernel(
    o_cols, f_cols, where_ref, own_ref, other_ref, out_w_ref, gate_w_ref, up_w_ref, down_w_ref
):
    width = MODEL_WIDTH
    out_w_ref[...] = natural_pieces(where_ref, own_ref, other_ref, 0, o_cols)[:, :width]
    gate_w_ref[...] = natural_pieces(where_ref, own_ref, other_ref, o_cols, f_cols)[:, :width]
    up_w_ref[...] = natural_pieces(where_ref, own_ref, other_ref, o_cols + f_cols, f_cols)[
        :, :width
    ]
    base = o_cols + 2 * f_cols
    for begin in range(0, FF, LANES):
        size = min(LANES, FF - begin)
        part = natural_pieces(where_ref, own_ref, other_ref, base, o_cols)
        down_w_ref[:, begin : begin + size] = part[:, :size]
        base += o_cols


def pack_rows(where_ref, own_ref, other_ref, source, begin, size):
    zero = where_ref[0] == 0
    lanes = source.shape[1]
    for g in range(own_ref.shape[0]):
        slot = where_ref[1 + g]
        even = source[2 * g * size : (2 * g + 1) * size]
        odd = source[(2 * g + 1) * size : (2 * g + 2) * size]
        own_ref[slot, begin : begin + size, :lanes] = jnp.where(zero, even, odd).astype(bf16)
        other_ref[slot, begin : begin + size, :lanes] = jnp.where(zero, odd, even).astype(bf16)


def pack_first_kernel(q_cols, kv_cols, where_ref, grad_ref, gains_ref, own_ref, other_ref):
    width = grad_ref.shape[1]
    own_ref[...] = jnp.zeros(own_ref.shape, bf16)
    other_ref[...] = jnp.zeros(other_ref.shape, bf16)
    pack_rows(where_ref, own_ref, other_ref, grad_ref[KV_PACKED:, :].astype(f32), 0, q_cols)
    for offset in range(2):
        part = jnp.concatenate(
            [
                grad_ref[j * PACK + offset * HEAD_DIM : j * PACK + (offset + 1) * HEAD_DIM, :]
                for j in range(KV_HEADS)
            ],
            axis=0,
        ).astype(f32)
        pack_rows(where_ref, own_ref, other_ref, part, q_cols + offset * kv_cols, kv_cols)
    begin = q_cols + 2 * kv_cols
    for g in range(own_ref.shape[0]):
        own_ref[g, begin : begin + 2, :width] = gains_ref[...].astype(bf16)
        other_ref[g, begin : begin + 2, :width] = gains_ref[...].astype(bf16)


def pack_second_kernel(
    o_cols, f_cols, where_ref, out_g_ref, gate_g_ref, up_g_ref, down_g_ref, own_ref, other_ref
):
    own_ref[...] = jnp.zeros(own_ref.shape, bf16)
    other_ref[...] = jnp.zeros(other_ref.shape, bf16)
    pack_rows(where_ref, own_ref, other_ref, out_g_ref[...].astype(f32), 0, o_cols)
    pack_rows(where_ref, own_ref, other_ref, gate_g_ref[...].astype(f32), o_cols, f_cols)
    pack_rows(where_ref, own_ref, other_ref, up_g_ref[...].astype(f32), o_cols + f_cols, f_cols)
    base = o_cols + 2 * f_cols
    for begin in range(0, FF, LANES):
        size = min(LANES, FF - begin)
        part = down_g_ref[:, begin : begin + size].astype(f32)
        pack_rows(where_ref, own_ref, other_ref, part, base, o_cols)
        base += o_cols


def one(shape):
    rest = tuple(shape[1:])
    return pl.BlockSpec((1,) + rest, lambda s, *_: (s,) + (0,) * len(rest))


def whole(shape):
    return pl.BlockSpec(tuple(shape), lambda s, *_: (0,) * len(shape))


def call(kernel, seqs, inputs, outputs, scalars=(), scratch=(), flops=0):
    in_specs = [make(array.shape) for make, array in inputs]
    out_specs = [make(shape) for make, shape, _ in outputs]
    moved = sum(array.size * array.dtype.itemsize for _, array in inputs)
    for _, shape, kind in outputs:
        count = 1
        for size in shape:
            count *= size
        moved += count * jnp.dtype(kind).itemsize
    return pl.pallas_call(
        kernel,
        grid_spec=pltpu.PrefetchScalarGridSpec(
            num_scalar_prefetch=len(scalars),
            grid=(seqs,),
            in_specs=in_specs,
            out_specs=out_specs,
            scratch_shapes=list(scratch),
        ),
        out_shape=[jax.ShapeDtypeStruct(shape, kind) for _, shape, kind in outputs],
        compiler_params=pltpu.CompilerParams(vmem_limit_bytes=VMEM_BYTES),
        cost_estimate=pl.CostEstimate(
            flops=int(flops), bytes_accessed=int(moved), transcendentals=0
        ),
    )(*scalars, *[array for _, array in inputs])


def adam_update(weight, first, second, grad, rate, decay):
    first_next = BETA_ONE * first + (1.0 - BETA_ONE) * grad
    second_next = BETA_TWO * second + (1.0 - BETA_TWO) * grad * grad
    first_fix = first_next / (1.0 - BETA_ONE**STEP)
    second_fix = second_next / (1.0 - BETA_TWO**STEP)
    update = first_fix / (jnp.sqrt(second_fix) + ADAM_EPS) + decay * weight
    return (weight - rate * update, first_next, second_next)


def ring_of(chips):
    if chips == 8:
        return [0, 2, 4, 6, 7, 5, 3, 1]
    return list(range(chips))


def ring_pairs(chips, step):
    ring = ring_of(chips)
    return [
        (2 * ring[p] + core, 2 * ring[(p + step) % chips] + core)
        for p in range(chips)
        for core in range(2)
    ]


def ring_gather(mine, flip):
    chips = lax.axis_size("ctx") // 2
    steps = (chips // 2, (chips - 1) // 2)
    if flip:
        steps = steps[::-1]
    result = [mine] * chips
    ahead = behind = mine
    for t in range(1, max(steps) + 1):
        if t <= steps[0]:
            ahead = lax.ppermute(ahead, "ctx", ring_pairs(chips, 1))
            result[-t % chips] = ahead
        if t <= steps[1]:
            behind = lax.ppermute(behind, "ctx", ring_pairs(chips, -1))
            result[t] = behind
    return result


def plus(*terms):
    total = terms[0].astype(f32)
    for term in terms[1:]:
        total = total + term.astype(f32)
    return total


def ring_scatter(terms, flip):
    chips = lax.axis_size("ctx") // 2
    steps = (chips // 2, (chips - 1) // 2)
    if flip:
        steps = steps[::-1]
    moving = [terms[steps[0]]().astype(bf16), terms[-steps[1] % chips]().astype(bf16)]
    for t in range(max(steps)):
        for way in range(2):
            left = steps[way] - 1 - t
            if left < 0:
                continue
            sign = 1 - 2 * way
            got = lax.ppermute(moving[way], "ctx", ring_pairs(chips, sign))
            if left:
                got = plus(got, terms[sign * left % chips]()).astype(bf16)
            moving[way] = got
    return plus(terms[0](), moving[0], moving[1])


def rows_gather(part):
    if lax.axis_size("fsdp") != 2:
        return lax.all_gather(part, "fsdp", axis=1, tiled=True)
    first = lax.axis_index("fsdp") == 0
    got = lax.ppermute(part, "fsdp", [(0, 1), (1, 0)])
    return jnp.concatenate([jnp.where(first, part, got), jnp.where(first, got, part)], axis=1)


def rows_scatter(grads):
    fsdp = lax.axis_size("fsdp")
    if fsdp != 2:
        return lax.psum_scatter(
            grads.astype(bf16), "fsdp", scatter_dimension=1, tiled=True
        ).astype(f32)
    first = lax.axis_index("fsdp") == 0
    half = grads.shape[1] // 2
    low, high = grads[:, :half], grads[:, half:]
    got = lax.ppermute(jnp.where(first, high, low).astype(bf16), "fsdp", [(0, 1), (1, 0)])
    return jnp.where(first, low, high) + got.astype(f32)


def widen(array):
    return jnp.pad(array, ((0, 0), (0, LANES - array.shape[1])))


def weight_grad(left, right):
    return lax.dot_general(left, right, (((0, 1), (0, 1)), ((), ())), preferred_element_type=f32)


def body(
    tokens,
    cotangent,
    pair_order,
    query_weight,
    key_master_weight,
    value_master_weight,
    output_weight,
    gate_weight,
    up_weight,
    down_weight,
    norm_gains,
    query_first,
    key_first_moment,
    value_first_moment,
    output_first,
    gate_first,
    up_first,
    down_first,
    gains_first,
    query_second,
    key_second_moment,
    value_second_moment,
    output_second,
    gate_second,
    up_second,
    down_second,
    gains_second,
):
    masters = (
        query_weight,
        key_master_weight,
        value_master_weight,
        output_weight,
        gate_weight,
        up_weight,
        down_weight,
    )
    ctx = lax.axis_size("ctx")
    index = lax.axis_index("ctx")
    chunks = ctx // 2
    core = index % 2
    seqs = tokens.shape[0] // 2
    part_rows = tokens.shape[1]
    rows = 2 * part_rows
    blk = part_rows // 2
    per = rows // blk
    length = part_rows * ctx
    mine, other = core * seqs, (1 - core) * seqs
    partners = [(i, i ^ 1) for i in range(ctx)]

    def take(array):
        own = lax.dynamic_slice_in_dim(array, mine, seqs, 0)
        got = lax.ppermute(lax.dynamic_slice_in_dim(array, other, seqs, 0), "ctx", partners)
        return jnp.concatenate([own, got], axis=1)

    def give(array):
        got = lax.ppermute(array[:, part_rows:], "ctx", partners)
        result = jnp.zeros((2 * seqs, part_rows) + array.shape[2:], array.dtype)
        result = lax.dynamic_update_slice_in_dim(result, array[:, :part_rows], mine, 0)
        return lax.dynamic_update_slice_in_dim(result, got, other, 0)

    ring = ring_of(chunks)
    position_of = [ring.index(g) for g in range(chunks)]
    position = jnp.array(position_of, jnp.int32)[index // 2]
    slots = (jnp.array(position_of, jnp.int32) - position) % chunks
    where = jnp.concatenate([core[None].astype(jnp.int32), slots])

    turned_low = [matrix.astype(bf16).T for matrix in masters]
    q_cols, kv_cols = QUERY_WIDTH // ctx, KEY_WIDTH // ctx
    o_cols, f_cols = MODEL_WIDTH // ctx, FF // ctx

    def both_packs(pack, flip):
        stack = jnp.stack(ring_gather(pack, flip), axis=0)
        return stack, lax.ppermute(stack, "ctx", partners)

    first_part = rows_gather(jnp.concatenate(turned_low[:3] + [norm_gains.astype(bf16).T], axis=0))
    gains = first_part[q_cols + 2 * kv_cols :].astype(f32)
    gain_one, gain_two = gains[0:1], gains[1:2]
    first_own, first_other = both_packs(widen(first_part), False)
    (inward,) = call(
        functools.partial(unpack_first_kernel, q_cols, kv_cols),
        1,
        [(whole, first_own), (whole, first_other)],
        [(whole, (KV_PACKED + QUERY_WIDTH, MODEL_WIDTH), bf16)],
        scalars=(where,),
    )
    down_part = rows_gather(turned_low[6])
    second_part = jnp.concatenate(
        [widen(rows_gather(jnp.concatenate(turned_low[3:6], axis=0)))]
        + [widen(down_part[:, begin : begin + LANES]) for begin in range(0, FF, LANES)],
        axis=0,
    )
    second_own, second_other = both_packs(second_part, True)
    output_t, gate_t, up_t, down_t = call(
        functools.partial(unpack_second_kernel, o_cols, f_cols),
        1,
        [(whole, second_own), (whole, second_other)],
        [
            (whole, (MODEL_WIDTH, QUERY_WIDTH), bf16),
            (whole, (FF, MODEL_WIDTH), bf16),
            (whole, (FF, MODEL_WIDTH), bf16),
            (whole, (MODEL_WIDTH, FF), bf16),
        ],
        scalars=(where,),
    )

    x = take(tokens)
    cot = take(cotangent)
    order = lax.dynamic_slice_in_dim(pair_order, mine, seqs, 0)
    ends = jnp.stack([order, 2 * ctx - 1 - order], axis=2).reshape(seqs, chunks, 2, 2)
    ends = jnp.where(core == 0, ends, ends[:, :, ::-1])
    ends = ends.reshape(seqs, chunks, per)
    reached = jnp.array(ring, jnp.int32)[(position + jnp.arange(chunks)) % chunks]
    blocks = jnp.take(ends, reached, axis=1).reshape(seqs, chunks * per)
    own = blocks[:, :per]
    places = (own[:, :, None] * blk + jnp.arange(blk, dtype=jnp.int32)).reshape(seqs, rows)
    half_dim = HEAD_DIM // 2
    inverse = ROPE_BASE ** (-jnp.arange(half_dim, dtype=f32) * 2.0 / HEAD_DIM)
    angle = places.astype(f32)[..., None] * inverse
    cosine = jnp.tile(jnp.cos(angle), (1, 1, PACK // half_dim))
    sine = jnp.tile(jnp.sin(angle), (1, 1, PACK // half_dim))

    wide = (seqs, rows, MODEL_WIDTH)
    heads = (seqs, per, KV_HEADS, GROUP * blk, PACK)
    normed_one, query, kv = call(
        project_kernel,
        seqs,
        [(one, x), (whole, gain_one), (whole, inward), (one, cosine), (one, sine)],
        [(one, wide, bf16), (one, heads, bf16), (one, (seqs, rows, KV_PACKED), bf16)],
        flops=2 * seqs * rows * MODEL_WIDTH * (KV_PACKED + QUERY_WIDTH),
    )
    pairs = HEADS * rows * length * HEAD_DIM
    tile_rows = (KV_HEADS, GROUP * blk, PACK)
    kv_alls, attns, logs = [], [], []
    for s in range(seqs):
        kv_all = ring_gather(kv[s], s % 2 == 0)
        attn_one, log_one = call(
            functools.partial(attend_kernel, chunks),
            1,
            [(whole, query[s : s + 1])] + [(whole, chunk) for chunk in kv_all],
            [(whole, (1,) + wide[1:], bf16), (whole, (1,) + heads[1:], f32)],
            scalars=(blocks[s],),
            scratch=[
                pltpu.VMEM((length, KV_PACKED), bf16),
                pltpu.VMEM((KV_HEADS, length // TILE, GROUP * blk, TILE), f32),
                pltpu.VMEM(tile_rows, f32),
                pltpu.VMEM(tile_rows, f32),
            ],
            flops=4 * pairs,
        )
        kv_alls.append(kv_all)
        attns.append(attn_one)
        logs.append(log_one)
    attn = jnp.concatenate(attns, axis=0)
    ff_wide = (seqs, rows, FF)
    (
        block_local,
        normed_two,
        hidden,
        dgate,
        dup,
        dattn,
        dout,
        dresid,
        gain_two_grad,
    ) = call(
        middle_kernel,
        seqs,
        [
            (one, x),
            (one, attn),
            (one, cot),
            (whole, gain_two),
            (whole, output_t),
            (whole, gate_t),
            (whole, up_t),
            (whole, down_t),
        ],
        [
            (one, wide, f32),
            (one, wide, bf16),
            (one, ff_wide, bf16),
            (one, ff_wide, bf16),
            (one, ff_wide, bf16),
            (one, wide, bf16),
            (one, wide, bf16),
            (one, wide, f32),
            (one, (seqs, 1, MODEL_WIDTH), f32),
        ],
        flops=2 * seqs * rows * MODEL_WIDTH * (6 * FF + 2 * MODEL_WIDTH),
    )
    block_output = give(block_local)
    def reduced_packs(own_packs, other_packs, flip):
        got = lax.ppermute(other_packs, "ctx", partners)
        terms = [lambda k=k: plus(own_packs[k], got[k]) for k in range(chunks)]
        return ring_scatter(terms, flip)

    second_rows = second_part.shape[0]
    packs = (chunks, second_rows, LANES)
    second_packs = call(
        functools.partial(pack_second_kernel, o_cols, f_cols),
        1,
        [
            (whole, weight_grad(dattn, attn).astype(bf16)),
            (whole, weight_grad(dgate, normed_two).astype(bf16)),
            (whole, weight_grad(dup, normed_two).astype(bf16)),
            (whole, weight_grad(cot, hidden).astype(bf16)),
        ],
        [(whole, packs, bf16), (whole, packs, bf16)],
        scalars=(where,),
    )
    second_sum = reduced_packs(*second_packs, True)
    base = o_cols + 2 * f_cols
    down_sum = rows_scatter(
        jnp.concatenate(
            [
                second_sum[base + i * o_cols : base + (i + 1) * o_cols, : min(LANES, FF - begin)]
                for i, begin in enumerate(range(0, FF, LANES))
            ],
            axis=1,
        )
    )
    second_sum = rows_scatter(second_sum[:base, :MODEL_WIDTH])

    inner = KV_PACKED + QUERY_WIDTH
    dinputs, dalls, gain_one_grads = [], [], []
    for s in range(seqs):
        this = slice(s, s + 1)
        dquery, *dkv = call(
            functools.partial(attend_back_kernel, chunks),
            1,
            [(whole, query[this])]
            + [(whole, chunk) for chunk in kv_alls[s]]
            + [(whole, attns[s]), (whole, dout[this]), (whole, logs[s])]
            + [(whole, cosine[this]), (whole, sine[this])],
            [(whole, (1,) + wide[1:], bf16)] + [(whole, (rows, KV_PACKED), bf16)] * chunks,
            scalars=(blocks[s],),
            scratch=[
                pltpu.VMEM((length, KV_PACKED), bf16),
                pltpu.VMEM((KV_HEADS, 2 * GROUP * blk, PACK), bf16),
                pltpu.VMEM((KV_HEADS, PACK, 2 * GROUP * blk), bf16),
                pltpu.VMEM(tile_rows, f32),
                pltpu.VMEM(tile_rows, f32),
                pltpu.VMEM((KV_PACKED, length), f32),
                pltpu.VMEM((length, KV_PACKED), bf16),
            ],
            flops=10 * pairs,
        )
        dkv_own = ring_scatter([lambda k=k: dkv[k] for k in range(chunks)], s % 2 == 0)
        dinput, dall, gain_one_grad = call(
            final_kernel,
            1,
            [
                (whole, x[this]),
                (whole, gain_one),
                (whole, dquery),
                (whole, dkv_own[None]),
                (whole, dresid[this]),
                (whole, cosine[this]),
                (whole, sine[this]),
                (whole, inward),
            ],
            [
                (whole, (1,) + wide[1:], f32),
                (whole, (1, rows, inner), bf16),
                (whole, (1, 1, MODEL_WIDTH), f32),
            ],
            flops=2 * rows * MODEL_WIDTH * inner,
        )
        dinputs.append(dinput)
        dalls.append(dall)
        gain_one_grads.append(gain_one_grad)
    input_gradient = give(jnp.concatenate(dinputs, axis=0))
    inward_grad = weight_grad(jnp.concatenate(dalls, axis=0), normed_one).astype(bf16)
    gains_grad = jnp.concatenate(
        [sum(gain_one_grads)[0], jnp.sum(gain_two_grad, axis=0)], axis=0
    )
    packs = (chunks, first_part.shape[0], LANES)
    first_packs = call(
        functools.partial(pack_first_kernel, q_cols, kv_cols),
        1,
        [(whole, inward_grad), (whole, gains_grad)],
        [(whole, packs, bf16), (whole, packs, bf16)],
        scalars=(where,),
    )
    first_sum = rows_scatter(reduced_packs(*first_packs, False)[:, :MODEL_WIDTH])
    reduced = (
        first_sum[:q_cols],
        first_sum[q_cols : q_cols + kv_cols],
        first_sum[q_cols + kv_cols : q_cols + 2 * kv_cols],
        second_sum[:o_cols],
        second_sum[o_cols : o_cols + f_cols],
        second_sum[o_cols + f_cols :],
        down_sum,
    )
    gains_total = first_sum[q_cols + 2 * kv_cols :].T
    rates = (
        (MODEL_WIDTH // 4) ** (-0.5),
        MODEL_WIDTH ** (-0.5),
        MODEL_WIDTH ** (-0.5),
        (MODEL_WIDTH // 32) ** (-0.5),
        MODEL_WIDTH ** (-0.5),
        MODEL_WIDTH ** (-0.5),
        (FF // 2) ** (-0.5),
    )
    firsts = (
        query_first,
        key_first_moment,
        value_first_moment,
        output_first,
        gate_first,
        up_first,
        down_first,
    )
    seconds = (
        query_second,
        key_second_moment,
        value_second_moment,
        output_second,
        gate_second,
        up_second,
        down_second,
    )
    results = [
        adam_update(
            masters[member], firsts[member], seconds[member], reduced[member].T, rates[member], DECAY
        )
        for member in range(7)
    ]
    results.append(adam_update(norm_gains, gains_first, gains_second, gains_total, GAIN_RATE, 0.0))
    new_weights = [result[0] for result in results]
    new_firsts = [result[1] for result in results]
    new_seconds = [result[2] for result in results]
    return tuple([block_output, input_gradient] + new_weights + new_firsts + new_seconds)


def solution(mesh):
    sequences = P("fsdp", "ctx", None)
    matrix = P("fsdp", "ctx")
    gains = P("fsdp", None)
    state = (matrix,) * 7 + (gains,)
    return jax.shard_map(
        body,
        mesh=mesh,
        in_specs=(sequences, sequences, P("fsdp", None)) + state * 3,
        out_specs=(sequences, sequences) + state * 3,
        check_vma=False,
    )
```

```python
import functools

import jax
import jax.numpy as jnp
from jax import lax
from jax.experimental import pallas as pl
from jax.experimental.pallas import tpu as pltpu
from jax.sharding import PartitionSpec as P

MODEL_WIDTH = 576
FF = 1536
HEADS = 9
KV_HEADS = 3
HEAD_DIM = 64
STEP = 10
GROUP = HEADS // KV_HEADS
KEY_WIDTH = KV_HEADS * HEAD_DIM
QUERY_WIDTH = HEADS * HEAD_DIM
PACK = 2 * HEAD_DIM
KV_PACKED = KV_HEADS * PACK
TILE = 256
FF_CHUNK = 640
LANES = 640

NORM_EPS = 1e-05
ROPE_BASE = 100000.0
BETA_ONE = 0.9
BETA_TWO = 0.95
ADAM_EPS = 1e-08
DECAY = 0.1
GAIN_RATE = 0.5
MASKED = -1e30
VMEM_BYTES = 56 * 1024 * 1024

f32 = jnp.float32
bf16 = jnp.bfloat16


def dot_nt(a, b):
    return lax.dot_general(a, b, (((1,), (1,)), ((), ())), preferred_element_type=f32)


def dot_nn(a, b):
    return lax.dot_general(a, b, (((1,), (0,)), ((), ())), preferred_element_type=f32)


def lanes_of(shape):
    return lax.broadcasted_iota(jnp.int32, shape, len(shape) - 1)


def turned(v, first):
    lane = lanes_of(v.shape) % HEAD_DIM
    ahead = pltpu.roll(v, PACK - HEAD_DIM // 2, 1)
    behind = pltpu.roll(v, HEAD_DIM // 2, 1)
    if first:
        return jnp.where(lane < HEAD_DIM // 2, -ahead, behind)
    return jnp.where(lane < HEAD_DIM // 2, ahead, -behind)


def project_kernel(x_ref, gain_ref, weight_ref, cos_ref, sin_ref, normed_ref, query_ref, kv_ref):
    rows = x_ref.shape[1]
    blk = query_ref.shape[3] // GROUP
    x = x_ref[0].astype(f32)
    inv = lax.rsqrt(jnp.mean(x * x, axis=-1, keepdims=True) + NORM_EPS)
    normed = (x * inv * gain_ref[...]).astype(bf16)
    normed_ref[0] = normed
    raw = dot_nt(normed, weight_ref[...])
    cosine, sine = cos_ref[0], sin_ref[0]
    low_half = lanes_of((rows, PACK)) < HEAD_DIM
    for j in range(KV_HEADS):
        part = raw[:, j * PACK : (j + 1) * PACK]
        spun = part * cosine + turned(part, True) * sine
        kv_ref[0, :, j * PACK : (j + 1) * PACK] = jnp.where(low_half, spun, part).astype(bf16)
    for i in range((HEADS + 1) // 2):
        begin = KV_PACKED + i * PACK
        if 2 * i + 1 < HEADS:
            part = raw[:, begin : begin + PACK]
        else:
            tail = raw[:, begin : begin + HEAD_DIM]
            part = jnp.concatenate([tail, tail], axis=1)
        spun = part * cosine + turned(part, True) * sine
        spun = spun.astype(bf16).astype(f32) * (HEAD_DIM**-0.5)
        pair = [jnp.where(low_half, spun, 0.0)]
        if 2 * i + 1 < HEADS:
            pair.append(jnp.where(low_half, pltpu.roll(spun, HEAD_DIM, 1), 0.0))
        for offset, value in enumerate(pair):
            head = 2 * i + offset
            j, member = head // GROUP, head % GROUP
            value = value.astype(bf16)
            for b in range(rows // blk):
                query_ref[0, b, j, member * blk : (member + 1) * blk, :] = value[
                    b * blk : (b + 1) * blk
                ]


def sort_blocks(blocks_ref, kv_refs, sorted_ref, blk):
    per = kv_refs[0].shape[0] // blk
    for g, kv_ref in enumerate(kv_refs):
        for b in range(per):
            place = pl.multiple_of(blocks_ref[g * per + b] * blk, blk)
            sorted_ref[pl.ds(place, blk), :] = kv_ref[b * blk : (b + 1) * blk, :]


def allowed_mask(place, tile_begin, blk, rows):
    row = lax.broadcasted_iota(jnp.int32, (rows, TILE), 0) % blk
    col = lax.broadcasted_iota(jnp.int32, (rows, TILE), 1)
    return col <= row + (place * blk - tile_begin)


def attend_kernel(chunks, blocks_ref, query_ref, *refs):
    kv_refs = refs[:chunks]
    out_ref, log_ref, sorted_ref, score_ref, top_ref, acc_ref = refs[chunks:]
    per, rows = query_ref.shape[1], query_ref.shape[3]
    blk = rows // GROUP
    sort_blocks(blocks_ref, kv_refs, sorted_ref, blk)
    lane = lanes_of((TILE, PACK))
    for b in range(per):
        place = blocks_ref[b]
        full = (place * blk) // TILE

        def score_tile(t, masked):
            begin = pl.multiple_of(t * TILE, TILE)
            for j in range(KV_HEADS):
                kv = sorted_ref[pl.ds(begin, TILE), j * PACK : (j + 1) * PACK]
                score = dot_nt(query_ref[0, b, j], kv)
                if masked:
                    score = jnp.where(allowed_mask(place, begin, blk, rows), score, MASKED)
                score_ref[j, t] = score
                best = jnp.maximum(score[:, :PACK], score[:, PACK:])
                top_ref[j] = jnp.maximum(top_ref[j], best)

        top_ref[...] = jnp.full(top_ref.shape, MASKED, f32)
        acc_ref[...] = jnp.zeros(acc_ref.shape, f32)

        @pl.loop(0, full)
        def _(t):
            score_tile(t, False)

        score_tile(full, True)
        for j in range(KV_HEADS):
            top = jnp.max(top_ref[j], axis=-1, keepdims=True)
            top_ref[j] = jnp.broadcast_to(top, (rows, PACK))

        @pl.loop(0, full + 1)
        def _(t):
            begin = pl.multiple_of(t * TILE, TILE)
            for j in range(KV_HEADS):
                kv = sorted_ref[pl.ds(begin, TILE), j * PACK : (j + 1) * PACK]
                ones_v = jnp.where(lane < HEAD_DIM, jnp.ones((), bf16), kv)
                top = top_ref[j]
                score = score_ref[j, t]
                prob = jnp.concatenate(
                    [jnp.exp(score[:, :PACK] - top), jnp.exp(score[:, PACK:] - top)], axis=1
                )
                acc_ref[j] += dot_nn(prob.astype(bf16), ones_v)

        for j in range(KV_HEADS):
            acc = acc_ref[j]
            low_half = lanes_of(acc.shape) < HEAD_DIM
            total = jnp.where(low_half, acc, pltpu.roll(acc, HEAD_DIM, 1))
            log_ref[0, b, j] = top_ref[j] + jnp.log(total)
            attended = (acc / total).astype(bf16)
            for member in range(GROUP):
                head = j * GROUP + member
                out_ref[0, b * blk : (b + 1) * blk, head * HEAD_DIM : (head + 1) * HEAD_DIM] = (
                    attended[member * blk : (member + 1) * blk, HEAD_DIM:]
                )


def unpack_second(pack_ref, out_w_ref, gate_w_ref, up_w_ref, down_w_ref):
    ctx = pack_ref.shape[0]
    f_cols, o_cols = FF // ctx, MODEL_WIDTH // ctx
    for c in range(ctx):
        here = slice(c * f_cols, (c + 1) * f_cols)
        gate_w_ref[here, :] = pack_ref[c, :f_cols, :MODEL_WIDTH]
        up_w_ref[here, :] = pack_ref[c, f_cols : 2 * f_cols, :MODEL_WIDTH]

    def natural(base, size):
        pieces = [pack_ref[c, base : base + o_cols, :size].astype(f32) for c in range(ctx)]
        return jnp.concatenate(pieces, axis=0).astype(bf16)

    base = 2 * f_cols
    out_w_ref[...] = natural(base, MODEL_WIDTH)
    for begin in range(0, FF, LANES):
        base += o_cols
        size = min(LANES, FF - begin)
        down_w_ref[:, begin : begin + size] = natural(base, size)


def middle_kernel(
    x_ref,
    attn_ref,
    cot_ref,
    gain_ref,
    pack_ref,
    block_ref,
    normed_ref,
    hidden_ref,
    dgate_ref,
    dup_ref,
    dattn_ref,
    dout_ref,
    dresid_ref,
    gain_grad_ref,
    out_w_ref,
    gate_w_ref,
    up_w_ref,
    down_w_ref,
):
    @pl.when(pl.program_id(0) == 0)
    def _():
        unpack_second(pack_ref, out_w_ref, gate_w_ref, up_w_ref, down_w_ref)

    attn = attn_ref[0]
    cot = cot_ref[0]
    resid = x_ref[0].astype(f32) + dot_nt(attn, out_w_ref[...])
    inv = lax.rsqrt(jnp.mean(resid * resid, axis=-1, keepdims=True) + NORM_EPS)
    hat = resid * inv
    gain = gain_ref[...]
    normed = (hat * gain).astype(bf16)
    normed_ref[0] = normed
    block = resid
    dnormed = jnp.zeros(resid.shape, f32)
    for begin in range(0, FF, FF_CHUNK):
        span = slice(begin, min(begin + FF_CHUNK, FF))
        gate = dot_nt(normed, gate_w_ref[span, :])
        up = dot_nt(normed, up_w_ref[span, :])
        sig = 1.0 / (1.0 + jnp.exp(-gate))
        act = gate * sig
        hidden = (act * up).astype(bf16)
        hidden_ref[0, :, span] = hidden
        block = block + dot_nt(hidden, down_w_ref[:, span])
        dhidden = dot_nn(cot, down_w_ref[:, span])
        dgate = (dhidden * up * (sig * (1.0 + gate * (1.0 - sig)))).astype(bf16)
        dup = (dhidden * act).astype(bf16)
        dgate_ref[0, :, span] = dgate
        dup_ref[0, :, span] = dup
        dnormed = dnormed + dot_nn(dgate, gate_w_ref[span, :]) + dot_nn(dup, up_w_ref[span, :])
    block_ref[0] = block
    gain_grad_ref[0] = jnp.sum(dnormed * hat, axis=0, keepdims=True)
    scaled = dnormed * gain
    dresid = cot.astype(f32) + inv * (scaled - hat * jnp.mean(scaled * hat, axis=-1, keepdims=True))
    dresid_ref[0] = dresid
    dattn = dresid.astype(bf16)
    dattn_ref[0] = dattn
    dout_ref[0] = dot_nn(dattn, out_w_ref[...]).astype(bf16)


def attend_back_kernel(chunks, blocks_ref, query_ref, *refs):
    kv_refs = refs[:chunks]
    out_ref, dout_ref, log_ref, cos_ref, sin_ref, dquery_ref = refs[chunks : chunks + 6]
    dkv_refs = refs[chunks + 6 : 2 * chunks + 6]
    sorted_ref, both_ref, flip_ref, delta_ref, dq_ref, dkv_t_ref, dkv_s_ref = refs[2 * chunks + 6 :]
    per, rows = query_ref.shape[1], query_ref.shape[3]
    blk = rows // GROUP
    length = sorted_ref.shape[0]
    sort_blocks(blocks_ref, kv_refs, sorted_ref, blk)
    dkv_t_ref[...] = jnp.zeros(dkv_t_ref.shape, f32)
    for b in range(per):
        place = blocks_ref[b]
        full = (place * blk) // TILE
        span = slice(b * blk, (b + 1) * blk)
        for j in range(KV_HEADS):
            both_ref[j, :rows] = query_ref[0, b, j]
            for member in range(GROUP):
                head = j * GROUP + member
                lanes = slice(head * HEAD_DIM, (head + 1) * HEAD_DIM)
                dout = dout_ref[0, span, lanes]
                delta = jnp.sum(
                    dout.astype(f32) * out_ref[0, span, lanes].astype(f32), axis=-1, keepdims=True
                )
                here = slice(member * blk, (member + 1) * blk)
                delta_ref[j, here] = jnp.broadcast_to(delta, (blk, PACK))
                both_ref[j, rows + member * blk : rows + (member + 1) * blk] = jnp.concatenate(
                    [jnp.zeros_like(dout), dout], axis=1
                )
            flip_ref[j] = both_ref[j].T
        dq_ref[...] = jnp.zeros(dq_ref.shape, f32)

        def tile_step(t, masked):
            begin = pl.multiple_of(t * TILE, TILE)
            kvs = [
                sorted_ref[pl.ds(begin, TILE), j * PACK : (j + 1) * PACK] for j in range(KV_HEADS)
            ]
            joined = [dot_nt(both_ref[j], kvs[j]) for j in range(KV_HEADS)]
            dscores, joints = [], []
            for j in range(KV_HEADS):
                score, dprob = joined[j][:rows], joined[j][rows:]
                log_total = log_ref[0, b, j]
                delta = delta_ref[j]
                prob = jnp.concatenate(
                    [jnp.exp(score[:, :PACK] - log_total), jnp.exp(score[:, PACK:] - log_total)],
                    axis=1,
                )
                if masked:
                    prob = jnp.where(allowed_mask(place, begin, blk, rows), prob, 0.0)
                dscore = prob * jnp.concatenate(
                    [dprob[:, :PACK] - delta, dprob[:, PACK:] - delta], axis=1
                )
                dscores.append(dscore.astype(bf16))
                joints.append(jnp.concatenate([dscores[j], prob.astype(bf16)], axis=0))
            dqs = [dot_nn(dscores[j], kvs[j]) for j in range(KV_HEADS)]
            dkvs = [dot_nn(flip_ref[j], joints[j]) for j in range(KV_HEADS)]
            for j in range(KV_HEADS):
                dq_ref[j] += dqs[j]
                dkv_t_ref[j * PACK : (j + 1) * PACK, pl.ds(begin, TILE)] += dkvs[j]

        @pl.loop(0, full)
        def _(t):
            tile_step(t, False)

        tile_step(full, True)
        cosine, sine = cos_ref[0, span, :], sin_ref[0, span, :]
        for j in range(KV_HEADS):
            for member in range(GROUP):
                head = j * GROUP + member
                grad = dq_ref[j, member * blk : (member + 1) * blk]
                back = (grad * cosine + turned(grad, False) * sine) * (HEAD_DIM**-0.5)
                dquery_ref[0, span, head * HEAD_DIM : (head + 1) * HEAD_DIM] = back[
                    :, :HEAD_DIM
                ].astype(bf16)
    for begin in range(0, length, TILE):
        dkv_s_ref[begin : begin + TILE, :] = dkv_t_ref[:, begin : begin + TILE].T.astype(bf16)
    for g, dkv_ref in enumerate(dkv_refs):
        for b in range(per):
            place = pl.multiple_of(blocks_ref[g * per + b] * blk, blk)
            dkv_ref[b * blk : (b + 1) * blk, :] = dkv_s_ref[pl.ds(place, blk), :]


def final_kernel(
    x_ref,
    gain_ref,
    dquery_ref,
    dkv_ref,
    dresid_ref,
    cos_ref,
    sin_ref,
    weight_ref,
    dinput_ref,
    dall_ref,
    gain_grad_ref,
):
    rows = x_ref.shape[1]
    cosine, sine = cos_ref[0], sin_ref[0]
    low_half = lanes_of((rows, PACK)) < HEAD_DIM
    for j in range(KV_HEADS):
        part = dkv_ref[0, :, j * PACK : (j + 1) * PACK].astype(f32)
        back = part * cosine + turned(part, False) * sine
        dall_ref[0, :, j * PACK : (j + 1) * PACK] = jnp.where(low_half, back, part).astype(bf16)
    dall_ref[0, :, KV_PACKED:] = dquery_ref[0]
    dnormed = dot_nn(dall_ref[0], weight_ref[...])
    x = x_ref[0].astype(f32)
    inv = lax.rsqrt(jnp.mean(x * x, axis=-1, keepdims=True) + NORM_EPS)
    hat = x * inv
    gain_grad_ref[0] = jnp.sum(dnormed * hat, axis=0, keepdims=True)
    scaled = dnormed * gain_ref[...]
    dinput_ref[0] = dresid_ref[0] + inv * (
        scaled - hat * jnp.mean(scaled * hat, axis=-1, keepdims=True)
    )


def natural_pieces(where_ref, own_ref, other_ref, begin, size):
    zero = where_ref[0] == 0
    pieces = []
    for g in range(own_ref.shape[0]):
        slot = where_ref[1 + g]
        mine = own_ref[slot, begin : begin + size, :].astype(f32)
        theirs = other_ref[slot, begin : begin + size, :].astype(f32)
        pieces.append(jnp.where(zero, mine, theirs))
        pieces.append(jnp.where(zero, theirs, mine))
    return jnp.concatenate(pieces, axis=0).astype(bf16)


def unpack_first_kernel(q_cols, kv_cols, where_ref, own_ref, other_ref, inward_ref):
    width = inward_ref.shape[1]
    query = natural_pieces(where_ref, own_ref, other_ref, 0, q_cols)
    inward_ref[KV_PACKED:, :] = query[:, :width]
    for offset in range(2):
        part = natural_pieces(where_ref, own_ref, other_ref, q_cols + offset * kv_cols, kv_cols)
        for j in range(KV_HEADS):
            begin = j * PACK + offset * HEAD_DIM
            inward_ref[begin : begin + HEAD_DIM, :] = part[
                j * HEAD_DIM : (j + 1) * HEAD_DIM, :width
            ]


def pack_rows(where_ref, own_ref, other_ref, source, begin, size):
    zero = where_ref[0] == 0
    lanes = source.shape[1]
    for g in range(own_ref.shape[0]):
        slot = where_ref[1 + g]
        even = source[2 * g * size : (2 * g + 1) * size]
        odd = source[(2 * g + 1) * size : (2 * g + 2) * size]
        own_ref[slot, begin : begin + size, :lanes] = jnp.where(zero, even, odd).astype(bf16)
        other_ref[slot, begin : begin + size, :lanes] = jnp.where(zero, odd, even).astype(bf16)


def pack_first_kernel(q_cols, kv_cols, where_ref, grad_ref, gains_ref, own_ref, other_ref):
    width = grad_ref.shape[1]
    pack_rows(where_ref, own_ref, other_ref, grad_ref[KV_PACKED:, :].astype(f32), 0, q_cols)
    for offset in range(2):
        part = jnp.concatenate(
            [
                grad_ref[j * PACK + offset * HEAD_DIM : j * PACK + (offset + 1) * HEAD_DIM, :]
                for j in range(KV_HEADS)
            ],
            axis=0,
        ).astype(f32)
        pack_rows(where_ref, own_ref, other_ref, part, q_cols + offset * kv_cols, kv_cols)
    begin = q_cols + 2 * kv_cols
    for g in range(own_ref.shape[0]):
        own_ref[g, begin : begin + 2, :width] = gains_ref[...].astype(bf16)
        other_ref[g, begin : begin + 2, :width] = gains_ref[...].astype(bf16)


def pack_second_kernel(out_g_ref, gate_g_ref, up_g_ref, down_g_ref, pack_ref):
    ctx = pack_ref.shape[0]
    f_cols, o_cols = FF // ctx, MODEL_WIDTH // ctx
    for c in range(ctx):
        here = slice(c * f_cols, (c + 1) * f_cols)
        pack_ref[c, :f_cols, :MODEL_WIDTH] = gate_g_ref[here, :]
        pack_ref[c, f_cols : 2 * f_cols, :MODEL_WIDTH] = up_g_ref[here, :]
    base = 2 * f_cols
    parts = [out_g_ref[...]]
    parts += [down_g_ref[:, begin : min(begin + LANES, FF)] for begin in range(0, FF, LANES)]
    for part in parts:
        wide = part.astype(f32)
        for c in range(ctx):
            piece = wide[c * o_cols : (c + 1) * o_cols].astype(bf16)
            pack_ref[c, base : base + o_cols, : part.shape[1]] = piece
        base += o_cols


def one(shape):
    rest = tuple(shape[1:])
    return pl.BlockSpec((1,) + rest, lambda s, *_: (s,) + (0,) * len(rest))


def whole(shape):
    return pl.BlockSpec(tuple(shape), lambda s, *_: (0,) * len(shape))


def call(kernel, seqs, inputs, outputs, scalars=(), scratch=(), flops=0):
    in_specs = [make(array.shape) for make, array in inputs]
    out_specs = [make(shape) for make, shape, _ in outputs]
    moved = sum(array.size * array.dtype.itemsize for _, array in inputs)
    for _, shape, kind in outputs:
        count = 1
        for size in shape:
            count *= size
        moved += count * jnp.dtype(kind).itemsize
    return pl.pallas_call(
        kernel,
        grid_spec=pltpu.PrefetchScalarGridSpec(
            num_scalar_prefetch=len(scalars),
            grid=(seqs,),
            in_specs=in_specs,
            out_specs=out_specs,
            scratch_shapes=list(scratch),
        ),
        out_shape=[jax.ShapeDtypeStruct(shape, kind) for _, shape, kind in outputs],
        compiler_params=pltpu.CompilerParams(vmem_limit_bytes=VMEM_BYTES),
        cost_estimate=pl.CostEstimate(
            flops=int(flops), bytes_accessed=int(moved), transcendentals=0
        ),
    )(*scalars, *[array for _, array in inputs])


def adam_update(weight, first, second, grad, rate, decay):
    first_next = BETA_ONE * first + (1.0 - BETA_ONE) * grad
    second_next = BETA_TWO * second + (1.0 - BETA_TWO) * grad * grad
    first_fix = first_next / (1.0 - BETA_ONE**STEP)
    second_fix = second_next / (1.0 - BETA_TWO**STEP)
    update = first_fix / (jnp.sqrt(second_fix) + ADAM_EPS) + decay * weight
    return (weight - rate * update, first_next, second_next)


def ring_of(chips):
    if chips == 8:
        return [0, 2, 4, 6, 7, 5, 3, 1]
    return list(range(chips))


def ring_pairs(chips, step):
    ring = ring_of(chips)
    return [
        (2 * ring[p] + core, 2 * ring[(p + step) % chips] + core)
        for p in range(chips)
        for core in range(2)
    ]


def ring_gather(mine, flip):
    chips = lax.axis_size("ctx") // 2
    steps = (chips // 2, (chips - 1) // 2)
    if flip:
        steps = steps[::-1]
    result = [mine] * chips
    ahead = behind = mine
    for t in range(1, max(steps) + 1):
        if t <= steps[0]:
            ahead = lax.ppermute(ahead, "ctx", ring_pairs(chips, 1))
            result[-t % chips] = ahead
        if t <= steps[1]:
            behind = lax.ppermute(behind, "ctx", ring_pairs(chips, -1))
            result[t] = behind
    return result


def plus(*terms):
    total = terms[0].astype(f32)
    for term in terms[1:]:
        total = total + term.astype(f32)
    return total


def ring_scatter(terms, flip):
    chips = lax.axis_size("ctx") // 2
    steps = (chips // 2, (chips - 1) // 2)
    if flip:
        steps = steps[::-1]
    moving = [terms[steps[0]]().astype(bf16), terms[-steps[1] % chips]().astype(bf16)]
    for t in range(max(steps)):
        for way in range(2):
            left = steps[way] - 1 - t
            if left < 0:
                continue
            sign = 1 - 2 * way
            got = lax.ppermute(moving[way], "ctx", ring_pairs(chips, sign))
            if left:
                got = plus(got, terms[sign * left % chips]()).astype(bf16)
            moving[way] = got
    return plus(terms[0](), moving[0], moving[1])


def rows_gather(part):
    if lax.axis_size("fsdp") != 2:
        return lax.all_gather(part, "fsdp", axis=1, tiled=True)
    first = lax.axis_index("fsdp") == 0
    got = lax.ppermute(part, "fsdp", [(0, 1), (1, 0)])
    return jnp.concatenate([jnp.where(first, part, got), jnp.where(first, got, part)], axis=1)


def rows_scatter(grads):
    fsdp = lax.axis_size("fsdp")
    if fsdp != 2:
        return lax.psum_scatter(
            grads.astype(bf16), "fsdp", scatter_dimension=1, tiled=True
        ).astype(f32)
    first = lax.axis_index("fsdp") == 0
    half = grads.shape[1] // 2
    low, high = grads[:, :half], grads[:, half:]
    got = lax.ppermute(jnp.where(first, high, low).astype(bf16), "fsdp", [(0, 1), (1, 0)])
    return jnp.where(first, low, high) + got.astype(f32)


def widen(array):
    return jnp.pad(array, ((0, 0), (0, LANES - array.shape[1])))


def weight_grad(left, right):
    return lax.dot_general(left, right, (((0, 1), (0, 1)), ((), ())), preferred_element_type=f32)


def body(
    tokens,
    cotangent,
    pair_order,
    query_weight,
    key_master_weight,
    value_master_weight,
    output_weight,
    gate_weight,
    up_weight,
    down_weight,
    norm_gains,
    query_first,
    key_first_moment,
    value_first_moment,
    output_first,
    gate_first,
    up_first,
    down_first,
    gains_first,
    query_second,
    key_second_moment,
    value_second_moment,
    output_second,
    gate_second,
    up_second,
    down_second,
    gains_second,
):
    masters = (
        query_weight,
        key_master_weight,
        value_master_weight,
        output_weight,
        gate_weight,
        up_weight,
        down_weight,
    )
    ctx = lax.axis_size("ctx")
    index = lax.axis_index("ctx")
    chunks = ctx // 2
    core = index % 2
    seqs = tokens.shape[0] // 2
    part_rows = tokens.shape[1]
    rows = 2 * part_rows
    blk = part_rows // 2
    per = rows // blk
    length = part_rows * ctx
    mine, other = core * seqs, (1 - core) * seqs
    partners = [(i, i ^ 1) for i in range(ctx)]

    def take(array):
        own = lax.dynamic_slice_in_dim(array, mine, seqs, 0)
        got = lax.ppermute(lax.dynamic_slice_in_dim(array, other, seqs, 0), "ctx", partners)
        return jnp.concatenate([own, got], axis=1)

    def give(array):
        got = lax.ppermute(array[:, part_rows:], "ctx", partners)
        result = jnp.zeros((2 * seqs, part_rows) + array.shape[2:], array.dtype)
        result = lax.dynamic_update_slice_in_dim(result, array[:, :part_rows], mine, 0)
        return lax.dynamic_update_slice_in_dim(result, got, other, 0)

    ring = ring_of(chunks)
    position_of = [ring.index(g) for g in range(chunks)]
    position = jnp.array(position_of, jnp.int32)[index // 2]
    slots = (jnp.array(position_of, jnp.int32) - position) % chunks
    where = jnp.concatenate([core[None].astype(jnp.int32), slots])

    turned_low = [matrix.astype(bf16).T for matrix in masters]
    q_cols, kv_cols = QUERY_WIDTH // ctx, KEY_WIDTH // ctx
    o_cols, f_cols = MODEL_WIDTH // ctx, FF // ctx

    def both_packs(pack, flip):
        stack = jnp.stack(ring_gather(pack, flip), axis=0)
        return stack, lax.ppermute(stack, "ctx", partners)

    first_part = rows_gather(jnp.concatenate(turned_low[:3] + [norm_gains.astype(bf16).T], axis=0))
    gains = first_part[q_cols + 2 * kv_cols :].astype(f32)
    gain_one, gain_two = gains[0:1], gains[1:2]
    first_own, first_other = both_packs(widen(first_part), False)
    (inward,) = call(
        functools.partial(unpack_first_kernel, q_cols, kv_cols),
        1,
        [(whole, first_own), (whole, first_other)],
        [(whole, (KV_PACKED + QUERY_WIDTH, MODEL_WIDTH), bf16)],
        scalars=(where,),
    )
    down_part = rows_gather(turned_low[6])
    second_part = jnp.concatenate(
        [widen(rows_gather(jnp.concatenate(turned_low[4:6] + turned_low[3:4], axis=0)))]
        + [widen(down_part[:, begin : begin + LANES]) for begin in range(0, FF, LANES)],
        axis=0,
    )
    second_all = lax.all_gather(second_part, "ctx", axis=0, tiled=False)

    x = take(tokens)
    cot = take(cotangent)
    order = lax.dynamic_slice_in_dim(pair_order, mine, seqs, 0)
    ends = jnp.stack([order, 2 * ctx - 1 - order], axis=2).reshape(seqs, chunks, 2, 2)
    ends = jnp.where(core == 0, ends, ends[:, :, ::-1])
    ends = ends.reshape(seqs, chunks, per)
    reached = jnp.array(ring, jnp.int32)[(position + jnp.arange(chunks)) % chunks]
    blocks = jnp.take(ends, reached, axis=1).reshape(seqs, chunks * per)
    own = blocks[:, :per]
    places = (own[:, :, None] * blk + jnp.arange(blk, dtype=jnp.int32)).reshape(seqs, rows)
    half_dim = HEAD_DIM // 2
    inverse = ROPE_BASE ** (-jnp.arange(half_dim, dtype=f32) * 2.0 / HEAD_DIM)
    angle = places.astype(f32)[..., None] * inverse
    cosine = jnp.tile(jnp.cos(angle), (1, 1, PACK // half_dim))
    sine = jnp.tile(jnp.sin(angle), (1, 1, PACK // half_dim))

    wide = (seqs, rows, MODEL_WIDTH)
    heads = (seqs, per, KV_HEADS, GROUP * blk, PACK)
    normed_one, query, kv = call(
        project_kernel,
        seqs,
        [(one, x), (whole, gain_one), (whole, inward), (one, cosine), (one, sine)],
        [(one, wide, bf16), (one, heads, bf16), (one, (seqs, rows, KV_PACKED), bf16)],
        flops=2 * seqs * rows * MODEL_WIDTH * (KV_PACKED + QUERY_WIDTH),
    )
    pairs = HEADS * rows * length * HEAD_DIM
    tile_rows = (KV_HEADS, GROUP * blk, PACK)
    kv_alls, attns, logs = [], [], []
    for s in range(seqs):
        kv_all = ring_gather(kv[s], s % 2 == 0)
        attn_one, log_one = call(
            functools.partial(attend_kernel, chunks),
            1,
            [(whole, query[s : s + 1])] + [(whole, chunk) for chunk in kv_all],
            [(whole, (1,) + wide[1:], bf16), (whole, (1,) + heads[1:], f32)],
            scalars=(blocks[s],),
            scratch=[
                pltpu.VMEM((length, KV_PACKED), bf16),
                pltpu.VMEM((KV_HEADS, length // TILE, GROUP * blk, TILE), f32),
                pltpu.VMEM(tile_rows, f32),
                pltpu.VMEM(tile_rows, f32),
            ],
            flops=4 * pairs,
        )
        kv_alls.append(kv_all)
        attns.append(attn_one)
        logs.append(log_one)
    attn = jnp.concatenate(attns, axis=0)
    ff_wide = (seqs, rows, FF)
    (
        block_local,
        normed_two,
        hidden,
        dgate,
        dup,
        dattn,
        dout,
        dresid,
        gain_two_grad,
    ) = call(
        middle_kernel,
        seqs,
        [
            (one, x),
            (one, attn),
            (one, cot),
            (whole, gain_two),
            (whole, second_all),
        ],
        [
            (one, wide, f32),
            (one, wide, bf16),
            (one, ff_wide, bf16),
            (one, ff_wide, bf16),
            (one, ff_wide, bf16),
            (one, wide, bf16),
            (one, wide, bf16),
            (one, wide, f32),
            (one, (seqs, 1, MODEL_WIDTH), f32),
        ],
        scratch=[
            pltpu.VMEM((MODEL_WIDTH, QUERY_WIDTH), bf16),
            pltpu.VMEM((FF, MODEL_WIDTH), bf16),
            pltpu.VMEM((FF, MODEL_WIDTH), bf16),
            pltpu.VMEM((MODEL_WIDTH, FF), bf16),
        ],
        flops=2 * seqs * rows * MODEL_WIDTH * (6 * FF + 2 * MODEL_WIDTH),
    )
    block_output = give(block_local)
    def reduced_packs(own_packs, other_packs, flip):
        got = lax.ppermute(other_packs, "ctx", partners)
        terms = [lambda k=k: plus(own_packs[k], got[k]) for k in range(chunks)]
        return ring_scatter(terms, flip)

    (second_pack,) = call(
        pack_second_kernel,
        1,
        [
            (whole, weight_grad(dattn, attn).astype(bf16)),
            (whole, weight_grad(dgate, normed_two).astype(bf16)),
            (whole, weight_grad(dup, normed_two).astype(bf16)),
            (whole, weight_grad(cot, hidden).astype(bf16)),
        ],
        [(whole, second_all.shape, bf16)],
    )
    second_sum = lax.psum_scatter(second_pack, "ctx", scatter_dimension=0, tiled=False)
    base = 2 * f_cols + o_cols
    down_sum = rows_scatter(
        jnp.concatenate(
            [
                second_sum[base + i * o_cols : base + (i + 1) * o_cols, : min(LANES, FF - begin)]
                for i, begin in enumerate(range(0, FF, LANES))
            ],
            axis=1,
        ).astype(f32)
    )
    second_sum = rows_scatter(second_sum[:base, :MODEL_WIDTH].astype(f32))

    inner = KV_PACKED + QUERY_WIDTH
    dinputs, dalls, gain_one_grads = [], [], []
    for s in range(seqs):
        this = slice(s, s + 1)
        dquery, *dkv = call(
            functools.partial(attend_back_kernel, chunks),
            1,
            [(whole, query[this])]
            + [(whole, chunk) for chunk in kv_alls[s]]
            + [(whole, attns[s]), (whole, dout[this]), (whole, logs[s])]
            + [(whole, cosine[this]), (whole, sine[this])],
            [(whole, (1,) + wide[1:], bf16)] + [(whole, (rows, KV_PACKED), bf16)] * chunks,
            scalars=(blocks[s],),
            scratch=[
                pltpu.VMEM((length, KV_PACKED), bf16),
                pltpu.VMEM((KV_HEADS, 2 * GROUP * blk, PACK), bf16),
                pltpu.VMEM((KV_HEADS, PACK, 2 * GROUP * blk), bf16),
                pltpu.VMEM(tile_rows, f32),
                pltpu.VMEM(tile_rows, f32),
                pltpu.VMEM((KV_PACKED, length), f32),
                pltpu.VMEM((length, KV_PACKED), bf16),
            ],
            flops=10 * pairs,
        )
        dkv_own = ring_scatter([lambda k=k: dkv[k] for k in range(chunks)], s % 2 == 0)
        dinput, dall, gain_one_grad = call(
            final_kernel,
            1,
            [
                (whole, x[this]),
                (whole, gain_one),
                (whole, dquery),
                (whole, dkv_own[None]),
                (whole, dresid[this]),
                (whole, cosine[this]),
                (whole, sine[this]),
                (whole, inward),
            ],
            [
                (whole, (1,) + wide[1:], f32),
                (whole, (1, rows, inner), bf16),
                (whole, (1, 1, MODEL_WIDTH), f32),
            ],
            flops=2 * rows * MODEL_WIDTH * inner,
        )
        dinputs.append(dinput)
        dalls.append(dall)
        gain_one_grads.append(gain_one_grad)
    input_gradient = give(jnp.concatenate(dinputs, axis=0))
    inward_grad = weight_grad(jnp.concatenate(dalls, axis=0), normed_one).astype(bf16)
    gains_grad = jnp.concatenate(
        [sum(gain_one_grads)[0], jnp.sum(gain_two_grad, axis=0)], axis=0
    )
    packs = (chunks, first_part.shape[0], LANES)
    first_packs = call(
        functools.partial(pack_first_kernel, q_cols, kv_cols),
        1,
        [(whole, inward_grad), (whole, gains_grad)],
        [(whole, packs, bf16), (whole, packs, bf16)],
        scalars=(where,),
    )
    first_sum = rows_scatter(reduced_packs(*first_packs, False)[:, :MODEL_WIDTH])
    reduced = (
        first_sum[:q_cols],
        first_sum[q_cols : q_cols + kv_cols],
        first_sum[q_cols + kv_cols : q_cols + 2 * kv_cols],
        second_sum[2 * f_cols :],
        second_sum[:f_cols],
        second_sum[f_cols : 2 * f_cols],
        down_sum,
    )
    gains_total = first_sum[q_cols + 2 * kv_cols :].T
    rates = (
        (MODEL_WIDTH // 4) ** (-0.5),
        MODEL_WIDTH ** (-0.5),
        MODEL_WIDTH ** (-0.5),
        (MODEL_WIDTH // 32) ** (-0.5),
        MODEL_WIDTH ** (-0.5),
        MODEL_WIDTH ** (-0.5),
        (FF // 2) ** (-0.5),
    )
    firsts = (
        query_first,
        key_first_moment,
        value_first_moment,
        output_first,
        gate_first,
        up_first,
        down_first,
    )
    seconds = (
        query_second,
        key_second_moment,
        value_second_moment,
        output_second,
        gate_second,
        up_second,
        down_second,
    )
    results = [
        adam_update(
            masters[member], firsts[member], seconds[member], reduced[member].T, rates[member], DECAY
        )
        for member in range(7)
    ]
    results.append(adam_update(norm_gains, gains_first, gains_second, gains_total, GAIN_RATE, 0.0))
    new_weights = [result[0] for result in results]
    new_firsts = [result[1] for result in results]
    new_seconds = [result[2] for result in results]
    return tuple([block_output, input_gradient] + new_weights + new_firsts + new_seconds)


def solution(mesh):
    sequences = P("fsdp", "ctx", None)
    matrix = P("fsdp", "ctx")
    gains = P("fsdp", None)
    state = (matrix,) * 7 + (gains,)
    return jax.shard_map(
        body,
        mesh=mesh,
        in_specs=(sequences, sequences, P("fsdp", None)) + state * 3,
        out_specs=(sequences, sequences) + state * 3,
        check_vma=False,
    )
```

```python
import functools

import jax
import jax.numpy as jnp
from jax import lax
from jax.experimental import pallas as pl
from jax.experimental.pallas import tpu as pltpu
from jax.sharding import PartitionSpec as P

MODEL_WIDTH = 576
FF = 1536
HEADS = 9
KV_HEADS = 3
HEAD_DIM = 64
STEP = 10
GROUP = HEADS // KV_HEADS
KEY_WIDTH = KV_HEADS * HEAD_DIM
QUERY_WIDTH = HEADS * HEAD_DIM
PACK = 2 * HEAD_DIM
KV_PACKED = KV_HEADS * PACK
TILE = 256
FF_CHUNK = 640
LANES = 640
REST = FF // 2 - LANES

NORM_EPS = 1e-05
ROPE_BASE = 100000.0
BETA_ONE = 0.9
BETA_TWO = 0.95
ADAM_EPS = 1e-08
DECAY = 0.1
GAIN_RATE = 0.5
MASKED = -1e30
VMEM_BYTES = 56 * 1024 * 1024

f32 = jnp.float32
bf16 = jnp.bfloat16


def dot_nt(a, b):
    return lax.dot_general(a, b, (((1,), (1,)), ((), ())), preferred_element_type=f32)


def dot_nn(a, b):
    return lax.dot_general(a, b, (((1,), (0,)), ((), ())), preferred_element_type=f32)


def lanes_of(shape):
    return lax.broadcasted_iota(jnp.int32, shape, len(shape) - 1)


def turned(v, first):
    lane = lanes_of(v.shape) % HEAD_DIM
    ahead = pltpu.roll(v, PACK - HEAD_DIM // 2, 1)
    behind = pltpu.roll(v, HEAD_DIM // 2, 1)
    if first:
        return jnp.where(lane < HEAD_DIM // 2, -ahead, behind)
    return jnp.where(lane < HEAD_DIM // 2, ahead, -behind)


def project_kernel(x_ref, gain_ref, weight_ref, cos_ref, sin_ref, normed_ref, query_ref, kv_ref):
    rows = x_ref.shape[1]
    blk = query_ref.shape[3] // GROUP
    x = x_ref[0].astype(f32)
    inv = lax.rsqrt(jnp.mean(x * x, axis=-1, keepdims=True) + NORM_EPS)
    normed = (x * inv * gain_ref[...]).astype(bf16)
    normed_ref[0] = normed
    raw = dot_nt(normed, weight_ref[...])
    cosine, sine = cos_ref[0], sin_ref[0]
    low_half = lanes_of((rows, PACK)) < HEAD_DIM
    for j in range(KV_HEADS):
        part = raw[:, j * PACK : (j + 1) * PACK]
        spun = part * cosine + turned(part, True) * sine
        kv_ref[0, :, j * PACK : (j + 1) * PACK] = jnp.where(low_half, spun, part).astype(bf16)
    for i in range((HEADS + 1) // 2):
        begin = KV_PACKED + i * PACK
        if 2 * i + 1 < HEADS:
            part = raw[:, begin : begin + PACK]
        else:
            tail = raw[:, begin : begin + HEAD_DIM]
            part = jnp.concatenate([tail, tail], axis=1)
        spun = part * cosine + turned(part, True) * sine
        spun = spun.astype(bf16).astype(f32) * (HEAD_DIM**-0.5)
        pair = [jnp.where(low_half, spun, 0.0)]
        if 2 * i + 1 < HEADS:
            pair.append(jnp.where(low_half, pltpu.roll(spun, HEAD_DIM, 1), 0.0))
        for offset, value in enumerate(pair):
            head = 2 * i + offset
            j, member = head // GROUP, head % GROUP
            value = value.astype(bf16)
            for b in range(rows // blk):
                query_ref[0, b, j, member * blk : (member + 1) * blk, :] = value[
                    b * blk : (b + 1) * blk
                ]


def sort_blocks(blocks_ref, kv_refs, sorted_ref, blk):
    per = kv_refs[0].shape[0] // blk
    for g, kv_ref in enumerate(kv_refs):
        for b in range(per):
            place = pl.multiple_of(blocks_ref[g * per + b] * blk, blk)
            sorted_ref[pl.ds(place, blk), :] = kv_ref[b * blk : (b + 1) * blk, :]


def allowed_mask(place, tile_begin, blk, rows):
    row = lax.broadcasted_iota(jnp.int32, (rows, TILE), 0) % blk
    col = lax.broadcasted_iota(jnp.int32, (rows, TILE), 1)
    return col <= row + (place * blk - tile_begin)


def attend_kernel(chunks, first, blocks_ref, query_ref, *refs):
    kv_refs = refs[:chunks]
    out_ref, log_ref, sorted_ref, score_ref, top_ref, acc_ref = refs[chunks:]
    per, rows = query_ref.shape[1], query_ref.shape[3]
    blk = rows // GROUP
    sort_blocks(blocks_ref, kv_refs, sorted_ref, blk)
    lane = lanes_of((TILE, PACK))
    for b in range(per):
        place = blocks_ref[first + b]
        full = (place * blk) // TILE

        def score_tile(t, masked):
            begin = pl.multiple_of(t * TILE, TILE)
            for j in range(KV_HEADS):
                kv = sorted_ref[pl.ds(begin, TILE), j * PACK : (j + 1) * PACK]
                score = dot_nt(query_ref[0, b, j], kv)
                if masked:
                    score = jnp.where(allowed_mask(place, begin, blk, rows), score, MASKED)
                score_ref[j, t] = score
                best = jnp.maximum(score[:, :PACK], score[:, PACK:])
                top_ref[j] = jnp.maximum(top_ref[j], best)

        top_ref[...] = jnp.full(top_ref.shape, MASKED, f32)
        acc_ref[...] = jnp.zeros(acc_ref.shape, f32)

        @pl.loop(0, full)
        def _(t):
            score_tile(t, False)

        score_tile(full, True)
        for j in range(KV_HEADS):
            top = jnp.max(top_ref[j], axis=-1, keepdims=True)
            top_ref[j] = jnp.broadcast_to(top, (rows, PACK))

        @pl.loop(0, full + 1)
        def _(t):
            begin = pl.multiple_of(t * TILE, TILE)
            for j in range(KV_HEADS):
                kv = sorted_ref[pl.ds(begin, TILE), j * PACK : (j + 1) * PACK]
                ones_v = jnp.where(lane < HEAD_DIM, jnp.ones((), bf16), kv)
                top = top_ref[j]
                score = score_ref[j, t]
                prob = jnp.concatenate(
                    [jnp.exp(score[:, :PACK] - top), jnp.exp(score[:, PACK:] - top)], axis=1
                )
                acc_ref[j] += dot_nn(prob.astype(bf16), ones_v)

        for j in range(KV_HEADS):
            acc = acc_ref[j]
            low_half = lanes_of(acc.shape) < HEAD_DIM
            total = jnp.where(low_half, acc, pltpu.roll(acc, HEAD_DIM, 1))
            log_ref[0, b, j] = top_ref[j] + jnp.log(total)
            attended = (acc / total).astype(bf16)
            for member in range(GROUP):
                head = j * GROUP + member
                out_ref[0, b * blk : (b + 1) * blk, head * HEAD_DIM : (head + 1) * HEAD_DIM] = (
                    attended[member * blk : (member + 1) * blk, HEAD_DIM:]
                )


def unpack_second(place_ref, part_refs, pack_ref, sems, out_w_ref, gate_w_ref, up_w_ref, down_w_ref):
    ctx = pack_ref.shape[1]
    f_cols, o_cols, half = FF // ctx, MODEL_WIDTH // ctx, MODEL_WIDTH // 2
    copies = []
    for part, part_ref in enumerate(part_refs):
        core = jnp.abs(place_ref[0] - part // 2)
        plane = jnp.abs(place_ref[1] - part % 2)
        for k in range(part_ref.shape[0]):
            index = 2 * place_ref[2 + k] + core
            copies.append(
                pltpu.make_async_copy(
                    part_ref.at[k], pack_ref.at[plane, index], sems.at[part, k]
                )
            )
    for copy in copies:
        copy.start()
    for copy in copies:
        copy.wait()
    for c in range(ctx):
        here = slice(c * f_cols, (c + 1) * f_cols)
        low, high = pack_ref[0, c, :f_cols, :], pack_ref[1, c, :f_cols, :]
        gate_w_ref[here, :] = jnp.concatenate([low[:, :half], high[:, :half]], axis=1)
        up_w_ref[here, :] = jnp.concatenate(
            [low[:, half:MODEL_WIDTH], high[:, half:MODEL_WIDTH]], axis=1
        )

    def natural(plane, base, lanes):
        pieces = [
            pack_ref[plane, c, base : base + o_cols, lanes].astype(f32) for c in range(ctx)
        ]
        return jnp.concatenate(pieces, axis=0).astype(bf16)

    base = f_cols + o_cols
    for plane in range(2):
        begin = plane * (FF // 2)
        down_w_ref[:, begin : begin + LANES] = natural(plane, f_cols, slice(0, LANES))
        down_w_ref[:, begin + LANES : begin + FF // 2] = natural(plane, base, slice(0, REST))
    out_w_ref[...] = jnp.concatenate(
        [natural(plane, base, slice(REST, REST + half)) for plane in range(2)], axis=1
    )


def middle_kernel(
    place_ref,
    x_ref,
    attn_ref,
    cot_ref,
    gain_ref,
    part_a_ref,
    part_b_ref,
    part_c_ref,
    part_d_ref,
    block_ref,
    normed_ref,
    hidden_ref,
    dgate_ref,
    dup_ref,
    dattn_ref,
    dout_ref,
    dresid_ref,
    gain_grad_ref,
    out_w_ref,
    gate_w_ref,
    up_w_ref,
    down_w_ref,
    pack_ref,
    sems,
):
    @pl.when(pl.program_id(0) == 0)
    def _():
        parts = (part_a_ref, part_b_ref, part_c_ref, part_d_ref)
        unpack_second(
            place_ref, parts, pack_ref, sems, out_w_ref, gate_w_ref, up_w_ref, down_w_ref
        )

    attn = attn_ref[0]
    cot = cot_ref[0]
    resid = x_ref[0].astype(f32) + dot_nt(attn, out_w_ref[...])
    inv = lax.rsqrt(jnp.mean(resid * resid, axis=-1, keepdims=True) + NORM_EPS)
    hat = resid * inv
    gain = gain_ref[...]
    normed = (hat * gain).astype(bf16)
    normed_ref[0] = normed
    block = resid
    dnormed = jnp.zeros(resid.shape, f32)
    for begin in range(0, FF, FF_CHUNK):
        span = slice(begin, min(begin + FF_CHUNK, FF))
        gate = dot_nt(normed, gate_w_ref[span, :])
        up = dot_nt(normed, up_w_ref[span, :])
        sig = 1.0 / (1.0 + jnp.exp(-gate))
        act = gate * sig
        hidden = (act * up).astype(bf16)
        hidden_ref[0, :, span] = hidden
        block = block + dot_nt(hidden, down_w_ref[:, span])
        dhidden = dot_nn(cot, down_w_ref[:, span])
        dgate = (dhidden * up * (sig * (1.0 + gate * (1.0 - sig)))).astype(bf16)
        dup = (dhidden * act).astype(bf16)
        dgate_ref[0, :, span] = dgate
        dup_ref[0, :, span] = dup
        dnormed = dnormed + dot_nn(dgate, gate_w_ref[span, :]) + dot_nn(dup, up_w_ref[span, :])
    block_ref[0] = block
    gain_grad_ref[0] = jnp.sum(dnormed * hat, axis=0, keepdims=True)
    scaled = dnormed * gain
    dresid = cot.astype(f32) + inv * (scaled - hat * jnp.mean(scaled * hat, axis=-1, keepdims=True))
    dresid_ref[0] = dresid
    dattn = dresid.astype(bf16)
    dattn_ref[0] = dattn
    dout_ref[0] = dot_nn(dattn, out_w_ref[...]).astype(bf16)


def attend_back_kernel(chunks, blocks_ref, query_ref, *refs):
    kv_refs = refs[:chunks]
    out_ref, dout_ref, *log_refs, cos_ref, sin_ref, dquery_ref = refs[chunks : chunks + 7]
    dkv_refs = refs[chunks + 7 : 2 * chunks + 7]
    sorted_ref, both_ref, flip_ref, delta_ref, dq_ref, dkv_t_ref, dkv_s_ref = refs[2 * chunks + 7 :]
    per, rows = query_ref.shape[1], query_ref.shape[3]
    blk = rows // GROUP
    length = sorted_ref.shape[0]
    sort_blocks(blocks_ref, kv_refs, sorted_ref, blk)
    dkv_t_ref[...] = jnp.zeros(dkv_t_ref.shape, f32)
    for b in range(per):
        place = blocks_ref[b]
        full = (place * blk) // TILE
        span = slice(b * blk, (b + 1) * blk)
        for j in range(KV_HEADS):
            both_ref[j, :rows] = query_ref[0, b, j]
            for member in range(GROUP):
                head = j * GROUP + member
                lanes = slice(head * HEAD_DIM, (head + 1) * HEAD_DIM)
                dout = dout_ref[0, span, lanes]
                delta = jnp.sum(
                    dout.astype(f32) * out_ref[0, span, lanes].astype(f32), axis=-1, keepdims=True
                )
                here = slice(member * blk, (member + 1) * blk)
                delta_ref[j, here] = jnp.broadcast_to(delta, (blk, PACK))
                both_ref[j, rows + member * blk : rows + (member + 1) * blk] = jnp.concatenate(
                    [jnp.zeros_like(dout), dout], axis=1
                )
            flip_ref[j] = both_ref[j].T
        dq_ref[...] = jnp.zeros(dq_ref.shape, f32)

        def tile_step(t, masked):
            begin = pl.multiple_of(t * TILE, TILE)
            kvs = [
                sorted_ref[pl.ds(begin, TILE), j * PACK : (j + 1) * PACK] for j in range(KV_HEADS)
            ]
            joined = [dot_nt(both_ref[j], kvs[j]) for j in range(KV_HEADS)]
            dscores, joints = [], []
            for j in range(KV_HEADS):
                score, dprob = joined[j][:rows], joined[j][rows:]
                log_total = log_refs[b // 2][0, b % 2, j]
                delta = delta_ref[j]
                prob = jnp.concatenate(
                    [jnp.exp(score[:, :PACK] - log_total), jnp.exp(score[:, PACK:] - log_total)],
                    axis=1,
                )
                if masked:
                    prob = jnp.where(allowed_mask(place, begin, blk, rows), prob, 0.0)
                dscore = prob * jnp.concatenate(
                    [dprob[:, :PACK] - delta, dprob[:, PACK:] - delta], axis=1
                )
                dscores.append(dscore.astype(bf16))
                joints.append(jnp.concatenate([dscores[j], prob.astype(bf16)], axis=0))
            dqs = [dot_nn(dscores[j], kvs[j]) for j in range(KV_HEADS)]
            dkvs = [dot_nn(flip_ref[j], joints[j]) for j in range(KV_HEADS)]
            for j in range(KV_HEADS):
                dq_ref[j] += dqs[j]
                dkv_t_ref[j * PACK : (j + 1) * PACK, pl.ds(begin, TILE)] += dkvs[j]

        @pl.loop(0, full)
        def _(t):
            tile_step(t, False)

        tile_step(full, True)
        cosine, sine = cos_ref[0, span, :], sin_ref[0, span, :]
        for j in range(KV_HEADS):
            for member in range(GROUP):
                head = j * GROUP + member
                grad = dq_ref[j, member * blk : (member + 1) * blk]
                back = (grad * cosine + turned(grad, False) * sine) * (HEAD_DIM**-0.5)
                dquery_ref[0, span, head * HEAD_DIM : (head + 1) * HEAD_DIM] = back[
                    :, :HEAD_DIM
                ].astype(bf16)
    for begin in range(0, length, TILE):
        dkv_s_ref[begin : begin + TILE, :] = dkv_t_ref[:, begin : begin + TILE].T.astype(bf16)
    for g, dkv_ref in enumerate(dkv_refs):
        for b in range(per):
            place = pl.multiple_of(blocks_ref[g * per + b] * blk, blk)
            dkv_ref[b * blk : (b + 1) * blk, :] = dkv_s_ref[pl.ds(place, blk), :]


def final_kernel(
    x_ref,
    gain_ref,
    dquery_ref,
    dkv_ref,
    dresid_ref,
    cos_ref,
    sin_ref,
    weight_ref,
    dinput_ref,
    dall_ref,
    gain_grad_ref,
):
    rows = x_ref.shape[1]
    cosine, sine = cos_ref[0], sin_ref[0]
    low_half = lanes_of((rows, PACK)) < HEAD_DIM
    for j in range(KV_HEADS):
        part = dkv_ref[0, :, j * PACK : (j + 1) * PACK].astype(f32)
        back = part * cosine + turned(part, False) * sine
        dall_ref[0, :, j * PACK : (j + 1) * PACK] = jnp.where(low_half, back, part).astype(bf16)
    dall_ref[0, :, KV_PACKED:] = dquery_ref[0]
    dnormed = dot_nn(dall_ref[0], weight_ref[...])
    x = x_ref[0].astype(f32)
    inv = lax.rsqrt(jnp.mean(x * x, axis=-1, keepdims=True) + NORM_EPS)
    hat = x * inv
    gain_grad_ref[0] = jnp.sum(dnormed * hat, axis=0, keepdims=True)
    scaled = dnormed * gain_ref[...]
    dinput_ref[0] = dresid_ref[0] + inv * (
        scaled - hat * jnp.mean(scaled * hat, axis=-1, keepdims=True)
    )


def natural_pieces(where_ref, own_ref, other_ref, begin, size):
    zero = where_ref[0] == 0
    pieces = []
    for g in range(own_ref.shape[0]):
        slot = where_ref[1 + g]
        mine = own_ref[slot, begin : begin + size, :].astype(f32)
        theirs = other_ref[slot, begin : begin + size, :].astype(f32)
        pieces.append(jnp.where(zero, mine, theirs))
        pieces.append(jnp.where(zero, theirs, mine))
    return jnp.concatenate(pieces, axis=0).astype(bf16)


def unpack_first_kernel(q_cols, kv_cols, where_ref, own_ref, other_ref, inward_ref):
    width = inward_ref.shape[1]
    query = natural_pieces(where_ref, own_ref, other_ref, 0, q_cols)
    inward_ref[KV_PACKED:, :] = query[:, :width]
    for offset in range(2):
        part = natural_pieces(where_ref, own_ref, other_ref, q_cols + offset * kv_cols, kv_cols)
        for j in range(KV_HEADS):
            begin = j * PACK + offset * HEAD_DIM
            inward_ref[begin : begin + HEAD_DIM, :] = part[
                j * HEAD_DIM : (j + 1) * HEAD_DIM, :width
            ]


def pack_rows(where_ref, own_ref, other_ref, source, begin, size):
    zero = where_ref[0] == 0
    lanes = source.shape[1]
    for g in range(own_ref.shape[0]):
        slot = where_ref[1 + g]
        even = source[2 * g * size : (2 * g + 1) * size]
        odd = source[(2 * g + 1) * size : (2 * g + 2) * size]
        own_ref[slot, begin : begin + size, :lanes] = jnp.where(zero, even, odd).astype(bf16)
        other_ref[slot, begin : begin + size, :lanes] = jnp.where(zero, odd, even).astype(bf16)


def pack_first_kernel(q_cols, kv_cols, where_ref, grad_ref, gains_ref, own_ref, other_ref):
    width = grad_ref.shape[1]
    pack_rows(where_ref, own_ref, other_ref, grad_ref[KV_PACKED:, :].astype(f32), 0, q_cols)
    for offset in range(2):
        part = jnp.concatenate(
            [
                grad_ref[j * PACK + offset * HEAD_DIM : j * PACK + (offset + 1) * HEAD_DIM, :]
                for j in range(KV_HEADS)
            ],
            axis=0,
        ).astype(f32)
        pack_rows(where_ref, own_ref, other_ref, part, q_cols + offset * kv_cols, kv_cols)
    begin = q_cols + 2 * kv_cols
    for g in range(own_ref.shape[0]):
        own_ref[g, begin : begin + 2, :width] = gains_ref[...].astype(bf16)
        other_ref[g, begin : begin + 2, :width] = gains_ref[...].astype(bf16)


def pack_second_kernel(
    place_ref, out_g_ref, gate_g_ref, up_g_ref, down_g_ref, a_ref, b_ref, c_ref, d_ref, pack_ref, sems
):
    ctx = pack_ref.shape[1]
    f_cols, o_cols, half = FF // ctx, MODEL_WIDTH // ctx, MODEL_WIDTH // 2
    base = f_cols + o_cols
    for plane in range(2):
        lanes = slice(plane * half, (plane + 1) * half)
        for c in range(ctx):
            here = slice(c * f_cols, (c + 1) * f_cols)
            pack_ref[plane, c, :f_cols, :MODEL_WIDTH] = jnp.concatenate(
                [gate_g_ref[here, lanes], up_g_ref[here, lanes]], axis=1
            )
        begin = plane * (FF // 2)
        first = down_g_ref[:, begin : begin + LANES].astype(f32)
        rest = down_g_ref[:, begin + LANES : begin + FF // 2]
        second = jnp.concatenate([rest, out_g_ref[:, lanes]], axis=1).astype(f32)
        for c in range(ctx):
            here = slice(c * o_cols, (c + 1) * o_cols)
            pack_ref[plane, c, f_cols:base, :] = first[here].astype(bf16)
            pack_ref[plane, c, base : base + o_cols, : REST + half] = second[here].astype(bf16)
    copies = []
    for part, part_ref in enumerate((a_ref, b_ref, c_ref, d_ref)):
        core = jnp.abs(place_ref[0] - part // 2)
        plane = jnp.abs(place_ref[1] - part % 2)
        for k in range(part_ref.shape[0]):
            index = 2 * place_ref[2 + k] + core
            copies.append(
                pltpu.make_async_copy(
                    pack_ref.at[plane, index], part_ref.at[k], sems.at[part, k]
                )
            )
    for copy in copies:
        copy.start()
    for copy in copies:
        copy.wait()


def one(shape):
    rest = tuple(shape[1:])
    return pl.BlockSpec((1,) + rest, lambda s, *_: (s,) + (0,) * len(rest))


def whole(shape):
    return pl.BlockSpec(tuple(shape), lambda s, *_: (0,) * len(shape))


def anywhere(shape):
    return pl.BlockSpec(memory_space=pl.ANY)


def fixed(block, *index):
    def make(shape):
        full = tuple(index) + (0,) * (len(shape) - len(index))
        sizes = tuple(block) + tuple(shape[len(block) :])
        return pl.BlockSpec(sizes, lambda s, *_: full)

    return make


def call(kernel, seqs, inputs, outputs, scalars=(), scratch=(), flops=0):
    in_specs = [make(array.shape) for make, array in inputs]
    out_specs = [make(shape) for make, shape, _ in outputs]
    moved = sum(array.size * array.dtype.itemsize for _, array in inputs)
    for _, shape, kind in outputs:
        count = 1
        for size in shape:
            count *= size
        moved += count * jnp.dtype(kind).itemsize
    return pl.pallas_call(
        kernel,
        grid_spec=pltpu.PrefetchScalarGridSpec(
            num_scalar_prefetch=len(scalars),
            grid=(seqs,),
            in_specs=in_specs,
            out_specs=out_specs,
            scratch_shapes=list(scratch),
        ),
        out_shape=[jax.ShapeDtypeStruct(shape, kind) for _, shape, kind in outputs],
        compiler_params=pltpu.CompilerParams(vmem_limit_bytes=VMEM_BYTES),
        cost_estimate=pl.CostEstimate(
            flops=int(flops), bytes_accessed=int(moved), transcendentals=0
        ),
    )(*scalars, *[array for _, array in inputs])


def adam_update(weight, first, second, grad, rate, decay):
    first_next = BETA_ONE * first + (1.0 - BETA_ONE) * grad
    second_next = BETA_TWO * second + (1.0 - BETA_TWO) * grad * grad
    first_fix = first_next / (1.0 - BETA_ONE**STEP)
    second_fix = second_next / (1.0 - BETA_TWO**STEP)
    update = first_fix / (jnp.sqrt(second_fix) + ADAM_EPS) + decay * weight
    return (weight - rate * update, first_next, second_next)


def ring_of(chips):
    if chips == 8:
        return [0, 2, 4, 6, 7, 5, 3, 1]
    return list(range(chips))


def ring_pairs(chips, step):
    ring = ring_of(chips)
    return [
        (2 * ring[p] + core, 2 * ring[(p + step) % chips] + core)
        for p in range(chips)
        for core in range(2)
    ]


def ring_gather(mine, flip):
    chips = lax.axis_size("ctx") // 2
    steps = (chips // 2, (chips - 1) // 2)
    if flip:
        steps = steps[::-1]
    result = [mine] * chips
    ahead = behind = mine
    for t in range(1, max(steps) + 1):
        if t <= steps[0]:
            ahead = lax.ppermute(ahead, "ctx", ring_pairs(chips, 1))
            result[-t % chips] = ahead
        if t <= steps[1]:
            behind = lax.ppermute(behind, "ctx", ring_pairs(chips, -1))
            result[t] = behind
    return result


def plus(*terms):
    total = terms[0].astype(f32)
    for term in terms[1:]:
        total = total + term.astype(f32)
    return total


def ring_scatter(terms, flip):
    chips = lax.axis_size("ctx") // 2
    steps = (chips // 2, (chips - 1) // 2)
    if flip:
        steps = steps[::-1]
    moving = [terms[steps[0]]().astype(bf16), terms[-steps[1] % chips]().astype(bf16)]
    for t in range(max(steps)):
        for way in range(2):
            left = steps[way] - 1 - t
            if left < 0:
                continue
            sign = 1 - 2 * way
            got = lax.ppermute(moving[way], "ctx", ring_pairs(chips, sign))
            if left:
                got = plus(got, terms[sign * left % chips]()).astype(bf16)
            moving[way] = got
    return plus(terms[0](), moving[0], moving[1])


def rows_gather(part):
    if lax.axis_size("fsdp") != 2:
        return lax.all_gather(part, "fsdp", axis=1, tiled=True)
    first = lax.axis_index("fsdp") == 0
    got = lax.ppermute(part, "fsdp", [(0, 1), (1, 0)])
    return jnp.concatenate([jnp.where(first, part, got), jnp.where(first, got, part)], axis=1)


def rows_scatter(grads):
    fsdp = lax.axis_size("fsdp")
    if fsdp != 2:
        return lax.psum_scatter(
            grads.astype(bf16), "fsdp", scatter_dimension=1, tiled=True
        ).astype(f32)
    first = lax.axis_index("fsdp") == 0
    half = grads.shape[1] // 2
    low, high = grads[:, :half], grads[:, half:]
    got = lax.ppermute(jnp.where(first, high, low).astype(bf16), "fsdp", [(0, 1), (1, 0)])
    return jnp.where(first, low, high) + got.astype(f32)


def widen(array):
    return jnp.pad(array, ((0, 0), (0, LANES - array.shape[1])))


def weight_grad(left, right):
    return lax.dot_general(left, right, (((0, 1), (0, 1)), ((), ())), preferred_element_type=f32)


def body(
    tokens,
    cotangent,
    pair_order,
    query_weight,
    key_master_weight,
    value_master_weight,
    output_weight,
    gate_weight,
    up_weight,
    down_weight,
    norm_gains,
    query_first,
    key_first_moment,
    value_first_moment,
    output_first,
    gate_first,
    up_first,
    down_first,
    gains_first,
    query_second,
    key_second_moment,
    value_second_moment,
    output_second,
    gate_second,
    up_second,
    down_second,
    gains_second,
):
    masters = (
        query_weight,
        key_master_weight,
        value_master_weight,
        output_weight,
        gate_weight,
        up_weight,
        down_weight,
    )
    ctx = lax.axis_size("ctx")
    index = lax.axis_index("ctx")
    chunks = ctx // 2
    core = index % 2
    seqs = tokens.shape[0] // 2
    part_rows = tokens.shape[1]
    rows = 2 * part_rows
    blk = part_rows // 2
    per = rows // blk
    length = part_rows * ctx
    mine, other = core * seqs, (1 - core) * seqs
    partners = [(i, i ^ 1) for i in range(ctx)]

    def take(array):
        own = lax.dynamic_slice_in_dim(array, mine, seqs, 0)
        got = lax.ppermute(lax.dynamic_slice_in_dim(array, other, seqs, 0), "ctx", partners)
        return jnp.concatenate([own, got], axis=1)

    def give(array):
        got = lax.ppermute(array[:, part_rows:], "ctx", partners)
        result = jnp.zeros((2 * seqs, part_rows) + array.shape[2:], array.dtype)
        result = lax.dynamic_update_slice_in_dim(result, array[:, :part_rows], mine, 0)
        return lax.dynamic_update_slice_in_dim(result, got, other, 0)

    ring = ring_of(chunks)
    position_of = [ring.index(g) for g in range(chunks)]
    position = jnp.array(position_of, jnp.int32)[index // 2]
    slots = (jnp.array(position_of, jnp.int32) - position) % chunks
    where = jnp.concatenate([core[None].astype(jnp.int32), slots])
    reached = jnp.array(ring, jnp.int32)[(position + jnp.arange(chunks)) % chunks]
    two_planes = lax.axis_size("fsdp") == 2
    plane = lax.axis_index("fsdp") if two_planes else jnp.zeros((), jnp.int32)
    place = jnp.concatenate([core[None].astype(jnp.int32), plane[None].astype(jnp.int32), reached])
    planes = [(0, 1), (1, 0)]

    turned_low = [matrix.astype(bf16).T for matrix in masters]
    q_cols, kv_cols = QUERY_WIDTH // ctx, KEY_WIDTH // ctx
    o_cols, f_cols = MODEL_WIDTH // ctx, FF // ctx

    def both_packs(pack, flip):
        stack = jnp.stack(ring_gather(pack, flip), axis=0)
        return stack, lax.ppermute(stack, "ctx", partners)

    first_part = rows_gather(jnp.concatenate(turned_low[:3] + [norm_gains.astype(bf16).T], axis=0))
    gains = first_part[q_cols + 2 * kv_cols :].astype(f32)
    gain_one, gain_two = gains[0:1], gains[1:2]
    first_own, first_other = both_packs(widen(first_part), False)
    (inward,) = call(
        functools.partial(unpack_first_kernel, q_cols, kv_cols),
        1,
        [(whole, first_own), (whole, first_other)],
        [(whole, (KV_PACKED + QUERY_WIDTH, MODEL_WIDTH), bf16)],
        scalars=(where,),
    )
    half = MODEL_WIDTH // 2

    def second_part(gate, up, output, down):
        return jnp.concatenate(
            [
                widen(jnp.concatenate([gate, up], axis=1)),
                down[:, :LANES],
                widen(jnp.concatenate([down[:, LANES:], output], axis=1)),
            ],
            axis=0,
        )

    def later(part):
        return lax.optimization_barrier((part, first_other))[0]

    outer = (turned_low[4], turned_low[5], turned_low[3], turned_low[6])
    if two_planes:
        same = jnp.stack(ring_gather(later(second_part(*outer)), True), axis=0)
        cross = lax.ppermute(same, "fsdp", planes)
    else:
        outer = [rows_gather(part) for part in outer]
        same, cross = [
            jnp.stack(
                ring_gather(
                    second_part(*[jnp.split(part, 2, axis=1)[side] for part in outer]), True
                ),
                axis=0,
            )
            for side in range(2)
        ]
    second_parts = [same, cross] + [lax.ppermute(part, "ctx", partners) for part in (same, cross)]

    x = take(tokens)
    cot = take(cotangent)
    order = lax.dynamic_slice_in_dim(pair_order, mine, seqs, 0)
    ends = jnp.stack([order, 2 * ctx - 1 - order], axis=2).reshape(seqs, chunks, 2, 2)
    ends = jnp.where(core == 0, ends, ends[:, :, ::-1])
    ends = ends.reshape(seqs, chunks, per)
    blocks = jnp.take(ends, reached, axis=1).reshape(seqs, chunks * per)
    own = blocks[:, :per]
    places = (own[:, :, None] * blk + jnp.arange(blk, dtype=jnp.int32)).reshape(seqs, rows)
    half_dim = HEAD_DIM // 2
    inverse = ROPE_BASE ** (-jnp.arange(half_dim, dtype=f32) * 2.0 / HEAD_DIM)
    angle = places.astype(f32)[..., None] * inverse
    cosine = jnp.tile(jnp.cos(angle), (1, 1, PACK // half_dim))
    sine = jnp.tile(jnp.sin(angle), (1, 1, PACK // half_dim))

    wide = (seqs, rows, MODEL_WIDTH)
    heads = (seqs, per, KV_HEADS, GROUP * blk, PACK)
    normed_one, query, kv = call(
        project_kernel,
        seqs,
        [(one, x), (whole, gain_one), (whole, inward), (one, cosine), (one, sine)],
        [(one, wide, bf16), (one, heads, bf16), (one, (seqs, rows, KV_PACKED), bf16)],
        flops=2 * seqs * rows * MODEL_WIDTH * (KV_PACKED + QUERY_WIDTH),
    )
    pairs = HEADS * rows * length * HEAD_DIM
    tile_rows = (KV_HEADS, GROUP * blk, PACK)
    kv_alls, attns, logs = [], [], []
    half_wide = (1, rows // 2, MODEL_WIDTH)
    half_heads = (1, per // 2) + heads[2:]
    for s in range(seqs):
        kv_all = ring_gather(kv[s], s % 2 == 0)
        log_pair = []
        for pair in range(2):
            attn_one, log_one = call(
                functools.partial(attend_kernel, chunks, pair * per // 2),
                1,
                [(fixed((1, per // 2), s, pair), query)] + [(whole, chunk) for chunk in kv_all],
                [(whole, half_wide, bf16), (whole, half_heads, f32)],
                scalars=(blocks[s],),
                scratch=[
                    pltpu.VMEM((length, KV_PACKED), bf16),
                    pltpu.VMEM((KV_HEADS, length // TILE, GROUP * blk, TILE), f32),
                    pltpu.VMEM(tile_rows, f32),
                    pltpu.VMEM(tile_rows, f32),
                ],
                flops=2 * pairs,
            )
            attns.append(attn_one)
            log_pair.append(log_one)
        kv_alls.append(kv_all)
        logs.append(log_pair)
    attn = jnp.concatenate(attns, axis=1).reshape(wide)
    ff_wide = (seqs, rows, FF)
    (
        block_local,
        normed_two,
        hidden,
        dgate,
        dup,
        dattn,
        dout,
        dresid,
        gain_two_grad,
    ) = call(
        middle_kernel,
        seqs,
        [
            (one, x),
            (one, attn),
            (one, cot),
            (whole, gain_two),
        ]
        + [(anywhere, part) for part in second_parts],
        [
            (one, wide, f32),
            (one, wide, bf16),
            (one, ff_wide, bf16),
            (one, ff_wide, bf16),
            (one, ff_wide, bf16),
            (one, wide, bf16),
            (one, wide, bf16),
            (one, wide, f32),
            (one, (seqs, 1, MODEL_WIDTH), f32),
        ],
        scratch=[
            pltpu.VMEM((MODEL_WIDTH, QUERY_WIDTH), bf16),
            pltpu.VMEM((FF, MODEL_WIDTH), bf16),
            pltpu.VMEM((FF, MODEL_WIDTH), bf16),
            pltpu.VMEM((MODEL_WIDTH, FF), bf16),
            pltpu.VMEM((2, ctx) + same.shape[1:], bf16),
            pltpu.SemaphoreType.DMA((4, chunks)),
        ],
        scalars=(place,),
        flops=2 * seqs * rows * MODEL_WIDTH * (6 * FF + 2 * MODEL_WIDTH),
    )
    block_output = give(block_local)
    def reduced_packs(own_packs, other_packs, flip):
        got = lax.ppermute(other_packs, "ctx", partners)
        terms = [lambda k=k: plus(own_packs[k], got[k]) for k in range(chunks)]
        return ring_scatter(terms, flip)

    def outer_sums(after):
        kept = lax.optimization_barrier((dattn, attn, dgate, dup, normed_two, hidden, after))
        dattn_, attn_, dgate_, dup_, normed_, hidden_, _ = kept
        packs = call(
            pack_second_kernel,
            1,
            [
                (whole, weight_grad(dattn_, attn_).astype(bf16)),
                (whole, weight_grad(dgate_, normed_).astype(bf16)),
                (whole, weight_grad(dup_, normed_).astype(bf16)),
                (whole, weight_grad(cot, hidden_).astype(bf16)),
            ],
            [(anywhere, same.shape, bf16)] * 4,
            scalars=(place,),
            scratch=[
                pltpu.VMEM((2, ctx) + same.shape[1:], bf16),
                pltpu.SemaphoreType.DMA((4, chunks)),
            ],
        )
        got = [lax.ppermute(part, "ctx", partners) for part in packs[2:]]
        if two_planes:
            sent = lax.ppermute(plus(packs[1], got[1]).astype(bf16), "fsdp", planes)
            terms = [lambda k=k: plus(packs[0][k], got[0][k], sent[k]) for k in range(chunks)]
            sums = [ring_scatter(terms, True)]
        else:
            sums = [
                ring_scatter([lambda k=k: plus(packs[i][k], got[i][k]) for k in range(chunks)], True)
                for i in range(2)
            ]
        base = f_cols + o_cols
        result = []
        for pick in (
            lambda part: part[base:, REST : REST + half],
            lambda part: part[:f_cols, :half],
            lambda part: part[:f_cols, half:MODEL_WIDTH],
            lambda part: jnp.concatenate([part[f_cols:base], part[base:, :REST]], axis=1),
        ):
            if two_planes:
                result.append(pick(sums[0]))
            else:
                result.append(rows_scatter(jnp.concatenate([pick(part) for part in sums], axis=1)))
        return packs, result

    inner = KV_PACKED + QUERY_WIDTH
    dinputs, dalls, gain_one_grads = [], [], []
    dout_now = dout
    for s in range(seqs):
        this = fixed((1,), s)
        if s == seqs - 1:
            outer_packs, outer_reduced = outer_sums(dquery)
            dout_now = lax.optimization_barrier((dout, outer_packs[0]))[0]
        dquery, *dkv = call(
            functools.partial(attend_back_kernel, chunks),
            1,
            [(this, query)]
            + [(whole, chunk) for chunk in kv_alls[s]]
            + [(this, attn), (this, dout_now), (whole, logs[s][0]), (whole, logs[s][1])]
            + [(this, cosine), (this, sine)],
            [(whole, (1,) + wide[1:], bf16)] + [(whole, (rows, KV_PACKED), bf16)] * chunks,
            scalars=(blocks[s],),
            scratch=[
                pltpu.VMEM((length, KV_PACKED), bf16),
                pltpu.VMEM((KV_HEADS, 2 * GROUP * blk, PACK), bf16),
                pltpu.VMEM((KV_HEADS, PACK, 2 * GROUP * blk), bf16),
                pltpu.VMEM(tile_rows, f32),
                pltpu.VMEM(tile_rows, f32),
                pltpu.VMEM((KV_PACKED, length), f32),
                pltpu.VMEM((length, KV_PACKED), bf16),
            ],
            flops=10 * pairs,
        )
        dkv_own = ring_scatter([lambda k=k: dkv[k] for k in range(chunks)], s % 2 == 0)
        dinput, dall, gain_one_grad = call(
            final_kernel,
            1,
            [
                (this, x),
                (whole, gain_one),
                (whole, dquery),
                (whole, dkv_own[None]),
                (this, dresid),
                (this, cosine),
                (this, sine),
                (whole, inward),
            ],
            [
                (whole, (1,) + wide[1:], f32),
                (whole, (1, rows, inner), bf16),
                (whole, (1, 1, MODEL_WIDTH), f32),
            ],
            flops=2 * rows * MODEL_WIDTH * inner,
        )
        dinputs.append(dinput)
        dalls.append(dall)
        gain_one_grads.append(gain_one_grad)
    input_gradient = give(jnp.concatenate(dinputs, axis=0))
    inward_grad = weight_grad(jnp.concatenate(dalls, axis=0), normed_one).astype(bf16)
    gains_grad = jnp.concatenate(
        [sum(gain_one_grads)[0], jnp.sum(gain_two_grad, axis=0)], axis=0
    )
    packs = (chunks, first_part.shape[0], LANES)
    first_packs = call(
        functools.partial(pack_first_kernel, q_cols, kv_cols),
        1,
        [(whole, inward_grad), (whole, gains_grad)],
        [(whole, packs, bf16), (whole, packs, bf16)],
        scalars=(where,),
    )
    first_sum = rows_scatter(reduced_packs(*first_packs, False)[:, :MODEL_WIDTH])
    reduced = (
        first_sum[:q_cols],
        first_sum[q_cols : q_cols + kv_cols],
        first_sum[q_cols + kv_cols : q_cols + 2 * kv_cols],
        *outer_reduced,
    )
    gains_total = first_sum[q_cols + 2 * kv_cols :].T
    rates = (
        (MODEL_WIDTH // 4) ** (-0.5),
        MODEL_WIDTH ** (-0.5),
        MODEL_WIDTH ** (-0.5),
        (MODEL_WIDTH // 32) ** (-0.5),
        MODEL_WIDTH ** (-0.5),
        MODEL_WIDTH ** (-0.5),
        (FF // 2) ** (-0.5),
    )
    firsts = (
        query_first,
        key_first_moment,
        value_first_moment,
        output_first,
        gate_first,
        up_first,
        down_first,
    )
    seconds = (
        query_second,
        key_second_moment,
        value_second_moment,
        output_second,
        gate_second,
        up_second,
        down_second,
    )
    results = [
        adam_update(
            masters[member], firsts[member], seconds[member], reduced[member].T, rates[member], DECAY
        )
        for member in range(7)
    ]
    results.append(adam_update(norm_gains, gains_first, gains_second, gains_total, GAIN_RATE, 0.0))
    new_weights = [result[0] for result in results]
    new_firsts = [result[1] for result in results]
    new_seconds = [result[2] for result in results]
    return tuple([block_output, input_gradient] + new_weights + new_firsts + new_seconds)


def solution(mesh):
    sequences = P("fsdp", "ctx", None)
    matrix = P("fsdp", "ctx")
    gains = P("fsdp", None)
    state = (matrix,) * 7 + (gains,)
    return jax.shard_map(
        body,
        mesh=mesh,
        in_specs=(sequences, sequences, P("fsdp", None)) + state * 3,
        out_specs=(sequences, sequences) + state * 3,
        check_vma=False,
    )
```

```python
import functools

import jax
import jax.numpy as jnp
from jax import lax
from jax.experimental import pallas as pl
from jax.experimental.pallas import tpu as pltpu
from jax.sharding import PartitionSpec as P

MODEL_WIDTH = 576
FF = 1536
HEADS = 9
KV_HEADS = 3
HEAD_DIM = 64
STEP = 10
GROUP = HEADS // KV_HEADS
KEY_WIDTH = KV_HEADS * HEAD_DIM
QUERY_WIDTH = HEADS * HEAD_DIM
PACK = 2 * HEAD_DIM
KV_PACKED = KV_HEADS * PACK
TILE = 256
FF_CHUNK = 640
LANES = 640
REST = FF // 2 - LANES

NORM_EPS = 1e-05
ROPE_BASE = 100000.0
BETA_ONE = 0.9
BETA_TWO = 0.95
ADAM_EPS = 1e-08
DECAY = 0.1
GAIN_RATE = 0.5
MASKED = -1e30
FLOPS_PER_US = 1153.5e6
VMEM_BYTES = 56 * 1024 * 1024

f32 = jnp.float32
bf16 = jnp.bfloat16


def dot_nt(a, b):
    return lax.dot_general(a, b, (((1,), (1,)), ((), ())), preferred_element_type=f32)


def dot_nn(a, b):
    return lax.dot_general(a, b, (((1,), (0,)), ((), ())), preferred_element_type=f32)


def lanes_of(shape):
    return lax.broadcasted_iota(jnp.int32, shape, len(shape) - 1)


def turned(v, first):
    lane = lanes_of(v.shape) % HEAD_DIM
    ahead = pltpu.roll(v, PACK - HEAD_DIM // 2, 1)
    behind = pltpu.roll(v, HEAD_DIM // 2, 1)
    if first:
        return jnp.where(lane < HEAD_DIM // 2, -ahead, behind)
    return jnp.where(lane < HEAD_DIM // 2, ahead, -behind)


def project_kernel(x_ref, gain_ref, weight_ref, cos_ref, sin_ref, normed_ref, query_ref, kv_ref):
    rows = x_ref.shape[1]
    blk = query_ref.shape[3] // GROUP
    x = x_ref[0].astype(f32)
    inv = lax.rsqrt(jnp.mean(x * x, axis=-1, keepdims=True) + NORM_EPS)
    normed = (x * inv * gain_ref[...]).astype(bf16)
    normed_ref[0] = normed
    raw = dot_nt(normed, weight_ref[...])
    cosine, sine = cos_ref[0], sin_ref[0]
    low_half = lanes_of((rows, PACK)) < HEAD_DIM
    for j in range(KV_HEADS):
        part = raw[:, j * PACK : (j + 1) * PACK]
        spun = part * cosine + turned(part, True) * sine
        kv_ref[0, :, j * PACK : (j + 1) * PACK] = jnp.where(low_half, spun, part).astype(bf16)
    for i in range((HEADS + 1) // 2):
        begin = KV_PACKED + i * PACK
        if 2 * i + 1 < HEADS:
            part = raw[:, begin : begin + PACK]
        else:
            tail = raw[:, begin : begin + HEAD_DIM]
            part = jnp.concatenate([tail, tail], axis=1)
        spun = part * cosine + turned(part, True) * sine
        spun = spun.astype(bf16).astype(f32) * (HEAD_DIM**-0.5)
        pair = [jnp.where(low_half, spun, 0.0)]
        if 2 * i + 1 < HEADS:
            pair.append(jnp.where(low_half, pltpu.roll(spun, HEAD_DIM, 1), 0.0))
        for offset, value in enumerate(pair):
            head = 2 * i + offset
            j, member = head // GROUP, head % GROUP
            value = value.astype(bf16)
            for b in range(rows // blk):
                query_ref[0, b, j, member * blk : (member + 1) * blk, :] = value[
                    b * blk : (b + 1) * blk
                ]


def sort_blocks(blocks_ref, kv_refs, sorted_ref, blk):
    per = kv_refs[0].shape[0] // blk
    for g, kv_ref in enumerate(kv_refs):
        for b in range(per):
            place = pl.multiple_of(blocks_ref[g * per + b] * blk, blk)
            sorted_ref[pl.ds(place, blk), :] = kv_ref[b * blk : (b + 1) * blk, :]


def allowed_mask(place, tile_begin, blk, rows):
    row = lax.broadcasted_iota(jnp.int32, (rows, TILE), 0) % blk
    col = lax.broadcasted_iota(jnp.int32, (rows, TILE), 1)
    return col <= row + (place * blk - tile_begin)


def attend_kernel(chunks, blocks_ref, query_ref, *refs):
    kv_refs = refs[:chunks]
    out_ref, log_ref, sorted_ref, score_ref, top_ref, acc_ref = refs[chunks:]
    per, rows = query_ref.shape[1], query_ref.shape[3]
    blk = rows // GROUP
    sort_blocks(blocks_ref, kv_refs, sorted_ref, blk)
    lane = lanes_of((TILE, PACK))
    for b in range(per):
        place = blocks_ref[b]
        full = (place * blk) // TILE

        def score_tile(t, masked):
            begin = pl.multiple_of(t * TILE, TILE)
            for j in range(KV_HEADS):
                kv = sorted_ref[pl.ds(begin, TILE), j * PACK : (j + 1) * PACK]
                score = dot_nt(query_ref[0, b, j], kv)
                if masked:
                    score = jnp.where(allowed_mask(place, begin, blk, rows), score, MASKED)
                score_ref[j, t] = score
                best = jnp.maximum(score[:, :PACK], score[:, PACK:])
                top_ref[j] = jnp.maximum(top_ref[j], best)

        top_ref[...] = jnp.full(top_ref.shape, MASKED, f32)
        acc_ref[...] = jnp.zeros(acc_ref.shape, f32)

        @pl.loop(0, full)
        def _(t):
            score_tile(t, False)

        score_tile(full, True)
        for j in range(KV_HEADS):
            top = jnp.max(top_ref[j], axis=-1, keepdims=True)
            top_ref[j] = jnp.broadcast_to(top, (rows, PACK))

        @pl.loop(0, full + 1)
        def _(t):
            begin = pl.multiple_of(t * TILE, TILE)
            for j in range(KV_HEADS):
                kv = sorted_ref[pl.ds(begin, TILE), j * PACK : (j + 1) * PACK]
                ones_v = jnp.where(lane < HEAD_DIM, jnp.ones((), bf16), kv)
                top = top_ref[j]
                score = score_ref[j, t]
                prob = jnp.concatenate(
                    [jnp.exp(score[:, :PACK] - top), jnp.exp(score[:, PACK:] - top)], axis=1
                )
                acc_ref[j] += dot_nn(prob.astype(bf16), ones_v)

        for j in range(KV_HEADS):
            acc = acc_ref[j]
            low_half = lanes_of(acc.shape) < HEAD_DIM
            total = jnp.where(low_half, acc, pltpu.roll(acc, HEAD_DIM, 1))
            log_ref[0, b, j] = top_ref[j] + jnp.log(total)
            attended = (acc / total).astype(bf16)
            for member in range(GROUP):
                head = j * GROUP + member
                out_ref[0, b * blk : (b + 1) * blk, head * HEAD_DIM : (head + 1) * HEAD_DIM] = (
                    attended[member * blk : (member + 1) * blk, HEAD_DIM:]
                )


def unpack_second(place_ref, part_refs, pack_ref, sems, out_w_ref, gate_w_ref, up_w_ref, down_w_ref):
    ctx = pack_ref.shape[1]
    f_cols, o_cols, half = FF // ctx, MODEL_WIDTH // ctx, MODEL_WIDTH // 2
    copies = []
    for part, part_ref in enumerate(part_refs):
        core = jnp.abs(place_ref[0] - part // 2)
        plane = jnp.abs(place_ref[1] - part % 2)
        for k in range(part_ref.shape[0]):
            index = 2 * place_ref[2 + k] + core
            copies.append(
                pltpu.make_async_copy(
                    part_ref.at[k], pack_ref.at[plane, index], sems.at[part, k]
                )
            )
    for copy in copies:
        copy.start()
    for copy in copies:
        copy.wait()
    for c in range(ctx):
        here = slice(c * f_cols, (c + 1) * f_cols)
        low, high = pack_ref[0, c, :f_cols, :], pack_ref[1, c, :f_cols, :]
        gate_w_ref[here, :] = jnp.concatenate([low[:, :half], high[:, :half]], axis=1)
        up_w_ref[here, :] = jnp.concatenate(
            [low[:, half:MODEL_WIDTH], high[:, half:MODEL_WIDTH]], axis=1
        )

    def natural(plane, base, lanes):
        pieces = [
            pack_ref[plane, c, base : base + o_cols, lanes].astype(f32) for c in range(ctx)
        ]
        return jnp.concatenate(pieces, axis=0).astype(bf16)

    base = f_cols + o_cols
    for plane in range(2):
        begin = plane * (FF // 2)
        down_w_ref[:, begin : begin + LANES] = natural(plane, f_cols, slice(0, LANES))
        down_w_ref[:, begin + LANES : begin + FF // 2] = natural(plane, base, slice(0, REST))
    out_w_ref[...] = jnp.concatenate(
        [natural(plane, base, slice(REST, REST + half)) for plane in range(2)], axis=1
    )


def middle_kernel(
    place_ref,
    x_ref,
    attn_ref,
    cot_ref,
    gain_ref,
    part_a_ref,
    part_b_ref,
    part_c_ref,
    part_d_ref,
    block_ref,
    normed_ref,
    hidden_ref,
    dgate_ref,
    dup_ref,
    dattn_ref,
    dout_ref,
    dresid_ref,
    gain_grad_ref,
    out_w_ref,
    gate_w_ref,
    up_w_ref,
    down_w_ref,
    pack_ref,
    sems,
):
    @pl.when(pl.program_id(0) == 0)
    def _():
        parts = (part_a_ref, part_b_ref, part_c_ref, part_d_ref)
        unpack_second(
            place_ref, parts, pack_ref, sems, out_w_ref, gate_w_ref, up_w_ref, down_w_ref
        )

    attn = attn_ref[0]
    cot = cot_ref[0]
    resid = x_ref[0].astype(f32) + dot_nt(attn, out_w_ref[...])
    inv = lax.rsqrt(jnp.mean(resid * resid, axis=-1, keepdims=True) + NORM_EPS)
    hat = resid * inv
    gain = gain_ref[...]
    normed = (hat * gain).astype(bf16)
    normed_ref[0] = normed
    block = resid
    dnormed = jnp.zeros(resid.shape, f32)
    for begin in range(0, FF, FF_CHUNK):
        span = slice(begin, min(begin + FF_CHUNK, FF))
        gate = dot_nt(normed, gate_w_ref[span, :])
        up = dot_nt(normed, up_w_ref[span, :])
        sig = 1.0 / (1.0 + jnp.exp(-gate))
        act = gate * sig
        hidden = (act * up).astype(bf16)
        hidden_ref[0, :, span] = hidden
        block = block + dot_nt(hidden, down_w_ref[:, span])
        dhidden = dot_nn(cot, down_w_ref[:, span])
        dgate = (dhidden * up * (sig * (1.0 + gate * (1.0 - sig)))).astype(bf16)
        dup = (dhidden * act).astype(bf16)
        dgate_ref[0, :, span] = dgate
        dup_ref[0, :, span] = dup
        dnormed = dnormed + dot_nn(dgate, gate_w_ref[span, :]) + dot_nn(dup, up_w_ref[span, :])
    block_ref[0] = block
    gain_grad_ref[0] = jnp.sum(dnormed * hat, axis=0, keepdims=True)
    scaled = dnormed * gain
    dresid = cot.astype(f32) + inv * (scaled - hat * jnp.mean(scaled * hat, axis=-1, keepdims=True))
    dresid_ref[0] = dresid
    dattn = dresid.astype(bf16)
    dattn_ref[0] = dattn
    dout_ref[0] = dot_nn(dattn, out_w_ref[...]).astype(bf16)


def attend_back_kernel(chunks, blocks_ref, query_ref, *refs):
    kv_refs = refs[:chunks]
    out_ref, dout_ref, log_ref, cos_ref, sin_ref, dquery_ref = refs[chunks : chunks + 6]
    dkv_refs = refs[chunks + 6 : 2 * chunks + 6]
    sorted_ref, both_ref, flip_ref, delta_ref, dq_ref, dkv_t_ref, dkv_s_ref = refs[2 * chunks + 6 :]
    per, rows = query_ref.shape[1], query_ref.shape[3]
    blk = rows // GROUP
    length = sorted_ref.shape[0]
    sort_blocks(blocks_ref, kv_refs, sorted_ref, blk)
    dkv_t_ref[...] = jnp.zeros(dkv_t_ref.shape, f32)
    for b in range(per):
        place = blocks_ref[b]
        full = (place * blk) // TILE
        span = slice(b * blk, (b + 1) * blk)
        for j in range(KV_HEADS):
            both_ref[j, :rows] = query_ref[0, b, j]
            for member in range(GROUP):
                head = j * GROUP + member
                lanes = slice(head * HEAD_DIM, (head + 1) * HEAD_DIM)
                dout = dout_ref[0, span, lanes]
                delta = jnp.sum(
                    dout.astype(f32) * out_ref[0, span, lanes].astype(f32), axis=-1, keepdims=True
                )
                here = slice(member * blk, (member + 1) * blk)
                delta_ref[j, here] = jnp.broadcast_to(delta, (blk, PACK))
                both_ref[j, rows + member * blk : rows + (member + 1) * blk] = jnp.concatenate(
                    [jnp.zeros_like(dout), dout], axis=1
                )
            flip_ref[j] = both_ref[j].T
        dq_ref[...] = jnp.zeros(dq_ref.shape, f32)

        def tile_step(t, masked):
            begin = pl.multiple_of(t * TILE, TILE)
            kvs = [
                sorted_ref[pl.ds(begin, TILE), j * PACK : (j + 1) * PACK] for j in range(KV_HEADS)
            ]
            joined = [dot_nt(both_ref[j], kvs[j]) for j in range(KV_HEADS)]
            dscores, joints = [], []
            for j in range(KV_HEADS):
                score, dprob = joined[j][:rows], joined[j][rows:]
                log_total = log_ref[0, b, j]
                delta = delta_ref[j]
                prob = jnp.concatenate(
                    [jnp.exp(score[:, :PACK] - log_total), jnp.exp(score[:, PACK:] - log_total)],
                    axis=1,
                )
                if masked:
                    prob = jnp.where(allowed_mask(place, begin, blk, rows), prob, 0.0)
                dscore = prob * jnp.concatenate(
                    [dprob[:, :PACK] - delta, dprob[:, PACK:] - delta], axis=1
                )
                dscores.append(dscore.astype(bf16))
                joints.append(jnp.concatenate([dscores[j], prob.astype(bf16)], axis=0))
            dqs = [dot_nn(dscores[j], kvs[j]) for j in range(KV_HEADS)]
            dkvs = [dot_nn(flip_ref[j], joints[j]) for j in range(KV_HEADS)]
            for j in range(KV_HEADS):
                dq_ref[j] += dqs[j]
                dkv_t_ref[j * PACK : (j + 1) * PACK, pl.ds(begin, TILE)] += dkvs[j]

        @pl.loop(0, full)
        def _(t):
            tile_step(t, False)

        tile_step(full, True)
        cosine, sine = cos_ref[0, span, :], sin_ref[0, span, :]
        for j in range(KV_HEADS):
            for member in range(GROUP):
                head = j * GROUP + member
                grad = dq_ref[j, member * blk : (member + 1) * blk]
                back = (grad * cosine + turned(grad, False) * sine) * (HEAD_DIM**-0.5)
                dquery_ref[0, span, head * HEAD_DIM : (head + 1) * HEAD_DIM] = back[
                    :, :HEAD_DIM
                ].astype(bf16)
    for begin in range(0, length, TILE):
        dkv_s_ref[begin : begin + TILE, :] = dkv_t_ref[:, begin : begin + TILE].T.astype(bf16)
    for g, dkv_ref in enumerate(dkv_refs):
        for b in range(per):
            place = pl.multiple_of(blocks_ref[g * per + b] * blk, blk)
            dkv_ref[b * blk : (b + 1) * blk, :] = dkv_s_ref[pl.ds(place, blk), :]


def final_kernel(
    x_ref,
    gain_ref,
    dquery_ref,
    dkv_ref,
    dresid_ref,
    cos_ref,
    sin_ref,
    weight_ref,
    dinput_ref,
    dall_ref,
    gain_grad_ref,
):
    rows = x_ref.shape[1]
    cosine, sine = cos_ref[0], sin_ref[0]
    low_half = lanes_of((rows, PACK)) < HEAD_DIM
    for j in range(KV_HEADS):
        part = dkv_ref[0, :, j * PACK : (j + 1) * PACK].astype(f32)
        back = part * cosine + turned(part, False) * sine
        dall_ref[0, :, j * PACK : (j + 1) * PACK] = jnp.where(low_half, back, part).astype(bf16)
    dall_ref[0, :, KV_PACKED:] = dquery_ref[0]
    dnormed = dot_nn(dall_ref[0], weight_ref[...])
    x = x_ref[0].astype(f32)
    inv = lax.rsqrt(jnp.mean(x * x, axis=-1, keepdims=True) + NORM_EPS)
    hat = x * inv
    gain_grad_ref[0] = jnp.sum(dnormed * hat, axis=0, keepdims=True)
    scaled = dnormed * gain_ref[...]
    dinput_ref[0] = dresid_ref[0] + inv * (
        scaled - hat * jnp.mean(scaled * hat, axis=-1, keepdims=True)
    )


def natural_pieces(where_ref, own_ref, other_ref, begin, size):
    zero = where_ref[0] == 0
    pieces = []
    for g in range(own_ref.shape[0]):
        slot = where_ref[1 + g]
        mine = own_ref[slot, begin : begin + size, :].astype(f32)
        theirs = other_ref[slot, begin : begin + size, :].astype(f32)
        pieces.append(jnp.where(zero, mine, theirs))
        pieces.append(jnp.where(zero, theirs, mine))
    return jnp.concatenate(pieces, axis=0).astype(bf16)


def unpack_first_kernel(q_cols, kv_cols, where_ref, own_ref, other_ref, inward_ref):
    width = inward_ref.shape[1]
    query = natural_pieces(where_ref, own_ref, other_ref, 0, q_cols)
    inward_ref[KV_PACKED:, :] = query[:, :width]
    for offset in range(2):
        part = natural_pieces(where_ref, own_ref, other_ref, q_cols + offset * kv_cols, kv_cols)
        for j in range(KV_HEADS):
            begin = j * PACK + offset * HEAD_DIM
            inward_ref[begin : begin + HEAD_DIM, :] = part[
                j * HEAD_DIM : (j + 1) * HEAD_DIM, :width
            ]


def pack_rows(where_ref, own_ref, other_ref, source, begin, size):
    zero = where_ref[0] == 0
    lanes = source.shape[1]
    for g in range(own_ref.shape[0]):
        slot = where_ref[1 + g]
        even = source[2 * g * size : (2 * g + 1) * size]
        odd = source[(2 * g + 1) * size : (2 * g + 2) * size]
        own_ref[slot, begin : begin + size, :lanes] = jnp.where(zero, even, odd).astype(bf16)
        other_ref[slot, begin : begin + size, :lanes] = jnp.where(zero, odd, even).astype(bf16)


def pack_first_kernel(q_cols, kv_cols, where_ref, grad_ref, gains_ref, own_ref, other_ref):
    width = grad_ref.shape[1]
    pack_rows(where_ref, own_ref, other_ref, grad_ref[KV_PACKED:, :].astype(f32), 0, q_cols)
    for offset in range(2):
        part = jnp.concatenate(
            [
                grad_ref[j * PACK + offset * HEAD_DIM : j * PACK + (offset + 1) * HEAD_DIM, :]
                for j in range(KV_HEADS)
            ],
            axis=0,
        ).astype(f32)
        pack_rows(where_ref, own_ref, other_ref, part, q_cols + offset * kv_cols, kv_cols)
    begin = q_cols + 2 * kv_cols
    for g in range(own_ref.shape[0]):
        own_ref[g, begin : begin + 2, :width] = gains_ref[...].astype(bf16)
        other_ref[g, begin : begin + 2, :width] = gains_ref[...].astype(bf16)


def pack_second_kernel(
    place_ref, out_g_ref, gate_g_ref, up_g_ref, down_g_ref, a_ref, b_ref, c_ref, d_ref, pack_ref, sems
):
    ctx = pack_ref.shape[1]
    f_cols, o_cols, half = FF // ctx, MODEL_WIDTH // ctx, MODEL_WIDTH // 2
    base = f_cols + o_cols
    for plane in range(2):
        lanes = slice(plane * half, (plane + 1) * half)
        for c in range(ctx):
            here = slice(c * f_cols, (c + 1) * f_cols)
            pack_ref[plane, c, :f_cols, :MODEL_WIDTH] = jnp.concatenate(
                [gate_g_ref[here, lanes], up_g_ref[here, lanes]], axis=1
            )
        begin = plane * (FF // 2)
        first = down_g_ref[:, begin : begin + LANES].astype(f32)
        rest = down_g_ref[:, begin + LANES : begin + FF // 2]
        second = jnp.concatenate([rest, out_g_ref[:, lanes]], axis=1).astype(f32)
        for c in range(ctx):
            here = slice(c * o_cols, (c + 1) * o_cols)
            pack_ref[plane, c, f_cols:base, :] = first[here].astype(bf16)
            pack_ref[plane, c, base : base + o_cols, : REST + half] = second[here].astype(bf16)
    copies = []
    for part, part_ref in enumerate((a_ref, b_ref, c_ref, d_ref)):
        core = jnp.abs(place_ref[0] - part // 2)
        plane = jnp.abs(place_ref[1] - part % 2)
        for k in range(part_ref.shape[0]):
            index = 2 * place_ref[2 + k] + core
            copies.append(
                pltpu.make_async_copy(
                    pack_ref.at[plane, index], part_ref.at[k], sems.at[part, k]
                )
            )
    for copy in copies:
        copy.start()
    for copy in copies:
        copy.wait()


def one(shape):
    rest = tuple(shape[1:])
    return pl.BlockSpec((1,) + rest, lambda s, *_: (s,) + (0,) * len(rest))


def whole(shape):
    return pl.BlockSpec(tuple(shape), lambda s, *_: (0,) * len(shape))


def anywhere(shape):
    return pl.BlockSpec(memory_space=pl.ANY)


def fixed(block, *index):
    def make(shape):
        full = tuple(index) + (0,) * (len(shape) - len(index))
        sizes = tuple(block) + tuple(shape[len(block) :])
        return pl.BlockSpec(sizes, lambda s, *_: full)

    return make


def call(kernel, seqs, inputs, outputs, scalars=(), scratch=(), us=1.0, after=()):
    begin = len(scalars) + len(inputs)

    def body_of(*refs):
        kernel(*refs[:begin], *refs[begin + len(after) :])

    in_specs = [make(array.shape) for make, array in inputs]
    in_specs += [anywhere(array.shape) for array in after]
    out_specs = [make(shape) for make, shape, _ in outputs]
    moved = sum(array.size * array.dtype.itemsize for _, array in inputs)
    for _, shape, kind in outputs:
        count = 1
        for size in shape:
            count *= size
        moved += count * jnp.dtype(kind).itemsize
    return pl.pallas_call(
        body_of,
        grid_spec=pltpu.PrefetchScalarGridSpec(
            num_scalar_prefetch=len(scalars),
            grid=(seqs,),
            in_specs=in_specs,
            out_specs=out_specs,
            scratch_shapes=list(scratch),
        ),
        out_shape=[jax.ShapeDtypeStruct(shape, kind) for _, shape, kind in outputs],
        compiler_params=pltpu.CompilerParams(vmem_limit_bytes=VMEM_BYTES),
        cost_estimate=pl.CostEstimate(
            flops=int(us * FLOPS_PER_US), bytes_accessed=int(moved), transcendentals=0
        ),
    )(*scalars, *[array for _, array in inputs], *after)


def join_kernel(*refs):
    del refs


def join(arrays, *after):
    return pl.pallas_call(
        join_kernel,
        in_specs=[pl.BlockSpec(memory_space=pl.ANY)] * (len(arrays) + len(after)),
        out_specs=[pl.BlockSpec(memory_space=pl.ANY)] * len(arrays),
        out_shape=[jax.ShapeDtypeStruct(array.shape, array.dtype) for array in arrays],
        input_output_aliases={i: i for i in range(len(arrays))},
    )(*arrays, *after)


def adam_update(weight, first, second, grad, rate, decay):
    first_next = BETA_ONE * first + (1.0 - BETA_ONE) * grad
    second_next = BETA_TWO * second + (1.0 - BETA_TWO) * grad * grad
    first_fix = first_next / (1.0 - BETA_ONE**STEP)
    second_fix = second_next / (1.0 - BETA_TWO**STEP)
    update = first_fix / (jnp.sqrt(second_fix) + ADAM_EPS) + decay * weight
    return (weight - rate * update, first_next, second_next)


def ring_of(chips):
    if chips == 8:
        return [0, 2, 4, 6, 7, 5, 3, 1]
    return list(range(chips))


def ring_pairs(chips, step):
    ring = ring_of(chips)
    return [
        (2 * ring[p] + core, 2 * ring[(p + step) % chips] + core)
        for p in range(chips)
        for core in range(2)
    ]


def ring_gather(mine, flip, pins=None):
    chips = lax.axis_size("ctx") // 2
    steps = (chips // 2, (chips - 1) // 2)
    if flip:
        steps = steps[::-1]
    result = [mine] * chips
    ahead = behind = mine
    for t in range(1, max(steps) + 1):
        if t <= steps[0]:
            ahead = lax.ppermute(ahead, "ctx", ring_pairs(chips, 1))
            result[-t % chips] = ahead
        if t <= steps[1]:
            behind = lax.ppermute(behind, "ctx", ring_pairs(chips, -1))
            result[t] = behind
        if pins and t in pins and t < min(steps):
            ahead, behind = join([ahead, behind], *pins[t])
            result[-t % chips], result[t] = ahead, behind
    return result


def plus(*terms):
    total = terms[0].astype(f32)
    for term in terms[1:]:
        total = total + term.astype(f32)
    return total


def ring_scatter(terms, flip):
    chips = lax.axis_size("ctx") // 2
    steps = (chips // 2, (chips - 1) // 2)
    if flip:
        steps = steps[::-1]
    moving = [terms[steps[0]]().astype(bf16), terms[-steps[1] % chips]().astype(bf16)]
    trace = []
    for t in range(max(steps)):
        for way in range(2):
            left = steps[way] - 1 - t
            if left < 0:
                continue
            sign = 1 - 2 * way
            got = lax.ppermute(moving[way], "ctx", ring_pairs(chips, sign))
            if left:
                got = plus(got, terms[sign * left % chips]()).astype(bf16)
            moving[way] = got
        trace.append(list(moving))
    return plus(terms[0](), moving[0], moving[1]), trace


def rows_gather(part):
    if lax.axis_size("fsdp") != 2:
        return lax.all_gather(part, "fsdp", axis=1, tiled=True)
    first = lax.axis_index("fsdp") == 0
    got = lax.ppermute(part, "fsdp", [(0, 1), (1, 0)])
    return jnp.concatenate([jnp.where(first, part, got), jnp.where(first, got, part)], axis=1)


def rows_scatter(grads):
    fsdp = lax.axis_size("fsdp")
    if fsdp != 2:
        return lax.psum_scatter(
            grads.astype(bf16), "fsdp", scatter_dimension=1, tiled=True
        ).astype(f32)
    first = lax.axis_index("fsdp") == 0
    half = grads.shape[1] // 2
    low, high = grads[:, :half], grads[:, half:]
    got = lax.ppermute(jnp.where(first, high, low).astype(bf16), "fsdp", [(0, 1), (1, 0)])
    return jnp.where(first, low, high) + got.astype(f32)


def widen(array):
    return jnp.pad(array, ((0, 0), (0, LANES - array.shape[1])))


def weight_grad(left, right):
    return lax.dot_general(left, right, (((0, 1), (0, 1)), ((), ())), preferred_element_type=f32)


def body(
    tokens,
    cotangent,
    pair_order,
    query_weight,
    key_master_weight,
    value_master_weight,
    output_weight,
    gate_weight,
    up_weight,
    down_weight,
    norm_gains,
    query_first,
    key_first_moment,
    value_first_moment,
    output_first,
    gate_first,
    up_first,
    down_first,
    gains_first,
    query_second,
    key_second_moment,
    value_second_moment,
    output_second,
    gate_second,
    up_second,
    down_second,
    gains_second,
):
    masters = (
        query_weight,
        key_master_weight,
        value_master_weight,
        output_weight,
        gate_weight,
        up_weight,
        down_weight,
    )
    ctx = lax.axis_size("ctx")
    index = lax.axis_index("ctx")
    chunks = ctx // 2
    core = index % 2
    seqs = tokens.shape[0] // 2
    part_rows = tokens.shape[1]
    rows = 2 * part_rows
    blk = part_rows // 2
    per = rows // blk
    length = part_rows * ctx
    mine, other = core * seqs, (1 - core) * seqs
    partners = [(i, i ^ 1) for i in range(ctx)]

    def take(array):
        own = lax.dynamic_slice_in_dim(array, mine, seqs, 0)
        got = lax.ppermute(lax.dynamic_slice_in_dim(array, other, seqs, 0), "ctx", partners)
        return jnp.concatenate([own, got], axis=1)

    def give(array):
        got = lax.ppermute(array[:, part_rows:], "ctx", partners)
        result = jnp.zeros((2 * seqs, part_rows) + array.shape[2:], array.dtype)
        result = lax.dynamic_update_slice_in_dim(result, array[:, :part_rows], mine, 0)
        return lax.dynamic_update_slice_in_dim(result, got, other, 0)

    ring = ring_of(chunks)
    position_of = [ring.index(g) for g in range(chunks)]
    position = jnp.array(position_of, jnp.int32)[index // 2]
    slots = (jnp.array(position_of, jnp.int32) - position) % chunks
    where = jnp.concatenate([core[None].astype(jnp.int32), slots])
    reached = jnp.array(ring, jnp.int32)[(position + jnp.arange(chunks)) % chunks]
    two_planes = lax.axis_size("fsdp") == 2
    plane = lax.axis_index("fsdp") if two_planes else jnp.zeros((), jnp.int32)
    place = jnp.concatenate([core[None].astype(jnp.int32), plane[None].astype(jnp.int32), reached])
    planes = [(0, 1), (1, 0)]

    turned_low = [matrix.astype(bf16).T for matrix in masters]
    q_cols, kv_cols = QUERY_WIDTH // ctx, KEY_WIDTH // ctx
    o_cols, f_cols = MODEL_WIDTH // ctx, FF // ctx

    def both_packs(pack, flip):
        stack = jnp.stack(ring_gather(pack, flip), axis=0)
        return stack, lax.ppermute(stack, "ctx", partners)

    first_part = rows_gather(jnp.concatenate(turned_low[:3] + [norm_gains.astype(bf16).T], axis=0))
    gains = first_part[q_cols + 2 * kv_cols :].astype(f32)
    gain_one, gain_two = gains[0:1], gains[1:2]
    first_own, first_other = both_packs(widen(first_part), False)
    (inward,) = call(
        functools.partial(unpack_first_kernel, q_cols, kv_cols),
        1,
        [(whole, first_own), (whole, first_other)],
        [(whole, (KV_PACKED + QUERY_WIDTH, MODEL_WIDTH), bf16)],
        scalars=(where,),
        us=3.3,
    )
    half = MODEL_WIDTH // 2

    def second_part(gate, up, output, down):
        return jnp.concatenate(
            [
                widen(jnp.concatenate([gate, up], axis=1)),
                down[:, :LANES],
                widen(jnp.concatenate([down[:, LANES:], output], axis=1)),
            ],
            axis=0,
        )

    def later(part):
        return lax.optimization_barrier((part, first_other))[0]

    x = take(tokens)
    cot = take(cotangent)
    order = lax.dynamic_slice_in_dim(pair_order, mine, seqs, 0)
    ends = jnp.stack([order, 2 * ctx - 1 - order], axis=2).reshape(seqs, chunks, 2, 2)
    ends = jnp.where(core == 0, ends, ends[:, :, ::-1])
    ends = ends.reshape(seqs, chunks, per)
    blocks = jnp.take(ends, reached, axis=1).reshape(seqs, chunks * per)
    own = blocks[:, :per]
    places = (own[:, :, None] * blk + jnp.arange(blk, dtype=jnp.int32)).reshape(seqs, rows)
    half_dim = HEAD_DIM // 2
    inverse = ROPE_BASE ** (-jnp.arange(half_dim, dtype=f32) * 2.0 / HEAD_DIM)
    angle = places.astype(f32)[..., None] * inverse
    cosine = jnp.tile(jnp.cos(angle), (1, 1, PACK // half_dim))
    sine = jnp.tile(jnp.sin(angle), (1, 1, PACK // half_dim))

    wide = (seqs, rows, MODEL_WIDTH)
    heads = (seqs, per, KV_HEADS, GROUP * blk, PACK)
    normed_one, query, kv = call(
        project_kernel,
        seqs,
        [(one, x), (whole, gain_one), (whole, inward), (one, cosine), (one, sine)],
        [(one, wide, bf16), (one, heads, bf16), (one, (seqs, rows, KV_PACKED), bf16)],
        us=6.2,
    )
    outer = (turned_low[4], turned_low[5], turned_low[3], turned_low[6])
    if two_planes:
        same = jnp.stack(ring_gather(later(second_part(*outer)), True, {1: [inward], 2: [kv]}), axis=0)
        cross = lax.ppermute(same, "fsdp", planes)
    else:
        outer = [rows_gather(part) for part in outer]
        same, cross = [
            jnp.stack(
                ring_gather(
                    second_part(*[jnp.split(part, 2, axis=1)[side] for part in outer]), True
                ),
                axis=0,
            )
            for side in range(2)
        ]
    second_parts = [same, cross] + [lax.ppermute(part, "ctx", partners) for part in (same, cross)]

    load = length / 2048
    tile_rows = (KV_HEADS, GROUP * blk, PACK)
    kv_alls, attns, logs = [], [], []
    for s in range(seqs):
        kv_all = ring_gather(kv[s], s % 2 == 0)
        attn_one, log_one = call(
            functools.partial(attend_kernel, chunks),
            1,
            [(fixed((1,), s), query)] + [(whole, chunk) for chunk in kv_all],
            [(whole, (1,) + wide[1:], bf16), (whole, (1,) + heads[1:], f32)],
            scalars=(blocks[s],),
            scratch=[
                pltpu.VMEM((length, KV_PACKED), bf16),
                pltpu.VMEM((KV_HEADS, length // TILE, GROUP * blk, TILE), f32),
                pltpu.VMEM(tile_rows, f32),
                pltpu.VMEM(tile_rows, f32),
            ],
            us=13.5 * load,
        )
        attns.append(attn_one)
        kv_alls.append(kv_all)
        logs.append(log_one)
    attn = jnp.concatenate(attns, axis=0)
    ff_wide = (seqs, rows, FF)
    (
        block_local,
        normed_two,
        hidden,
        dgate,
        dup,
        dattn,
        dout,
        dresid,
        gain_two_grad,
    ) = call(
        middle_kernel,
        seqs,
        [
            (one, x),
            (one, attn),
            (one, cot),
            (whole, gain_two),
        ]
        + [(anywhere, part) for part in second_parts],
        [
            (one, wide, f32),
            (one, wide, bf16),
            (one, ff_wide, bf16),
            (one, ff_wide, bf16),
            (one, ff_wide, bf16),
            (one, wide, bf16),
            (one, wide, bf16),
            (one, wide, f32),
            (one, (seqs, 1, MODEL_WIDTH), f32),
        ],
        scratch=[
            pltpu.VMEM((MODEL_WIDTH, QUERY_WIDTH), bf16),
            pltpu.VMEM((FF, MODEL_WIDTH), bf16),
            pltpu.VMEM((FF, MODEL_WIDTH), bf16),
            pltpu.VMEM((MODEL_WIDTH, FF), bf16),
            pltpu.VMEM((2, ctx) + same.shape[1:], bf16),
            pltpu.SemaphoreType.DMA((4, chunks)),
        ],
        scalars=(place,),
        us=26.0,
    )
    block_output = give(block_local)
    def reduced_packs(own_packs, other_packs, flip):
        got = lax.ppermute(other_packs, "ctx", partners)
        terms = [lambda k=k: plus(own_packs[k], got[k]) for k in range(chunks)]
        return ring_scatter(terms, flip)

    def outer_sums(earlier):
        behind, latest = traces[-2], traces[-1]
        dattn_, dgate_ = join([dattn, dgate], earlier, *behind[0])
        dup_, hidden_ = join([dup, hidden], *behind[1], *latest[0])
        packs = call(
            pack_second_kernel,
            1,
            [
                (whole, weight_grad(dattn_, attn).astype(bf16)),
                (whole, weight_grad(dgate_, normed_two).astype(bf16)),
                (whole, weight_grad(dup_, normed_two).astype(bf16)),
                (whole, weight_grad(cot, hidden_).astype(bf16)),
            ],
            [(anywhere, same.shape, bf16)] * 4,
            scalars=(place,),
            scratch=[
                pltpu.VMEM((2, ctx) + same.shape[1:], bf16),
                pltpu.SemaphoreType.DMA((4, chunks)),
            ],
            us=7.7,
            after=behind[2] + latest[1],
        )
        got = [lax.ppermute(part, "ctx", partners) for part in packs[2:]]
        if two_planes:
            sent = lax.ppermute(plus(packs[1], got[1]).astype(bf16), "fsdp", planes)
            terms = [lambda k=k: plus(packs[0][k], got[0][k], sent[k]) for k in range(chunks)]
            sums, trace = ring_scatter(terms, True)
            sums, before_last, before_final = [sums], got, [sent]
        else:
            sums = [
                ring_scatter(
                    [lambda k=k, i=i: plus(packs[i][k], got[i][k]) for k in range(chunks)], True
                )[0]
                for i in range(2)
            ]
            before_last, before_final, trace = got, [], [[], []]
        base = f_cols + o_cols
        result = []
        for pick in (
            lambda part: part[base:, REST : REST + half],
            lambda part: part[:f_cols, :half],
            lambda part: part[:f_cols, half:MODEL_WIDTH],
            lambda part: jnp.concatenate([part[f_cols:base], part[base:, :REST]], axis=1),
        ):
            if two_planes:
                result.append(pick(sums[0]))
            else:
                result.append(rows_scatter(jnp.concatenate([pick(part) for part in sums], axis=1)))
        return result, before_last, before_final, trace[1]

    inner = KV_PACKED + QUERY_WIDTH
    dinputs, dalls, gain_one_grads = [], [], []
    traces = []
    for s in range(seqs):
        this = fixed((1,), s)
        waits = [dquery] if s else []
        if s == seqs - 1:
            outer_reduced, before_last, before_final, before_pack = outer_sums(dquery)
            waits = waits + before_last + traces[0][-1] + traces[-1][-2]
        dquery, *dkv = call(
            functools.partial(attend_back_kernel, chunks),
            1,
            [(this, query)]
            + [(whole, chunk) for chunk in kv_alls[s]]
            + [(this, attn), (this, dout), (whole, logs[s])]
            + [(this, cosine), (this, sine)],
            [(whole, (1,) + wide[1:], bf16)] + [(whole, (rows, KV_PACKED), bf16)] * chunks,
            scalars=(blocks[s],),
            scratch=[
                pltpu.VMEM((length, KV_PACKED), bf16),
                pltpu.VMEM((KV_HEADS, 2 * GROUP * blk, PACK), bf16),
                pltpu.VMEM((KV_HEADS, PACK, 2 * GROUP * blk), bf16),
                pltpu.VMEM(tile_rows, f32),
                pltpu.VMEM(tile_rows, f32),
                pltpu.VMEM((KV_PACKED, length), f32),
                pltpu.VMEM((length, KV_PACKED), bf16),
            ],
            us=17.0 * load,
            after=waits,
        )
        dkv_own, trace = ring_scatter([lambda k=k: dkv[k] for k in range(chunks)], s % 2 == 0)
        traces.append(trace)
        dinput, dall, gain_one_grad = call(
            final_kernel,
            1,
            [
                (this, x),
                (whole, gain_one),
                (whole, dquery),
                (whole, dkv_own[None]),
                (this, dresid),
                (this, cosine),
                (this, sine),
                (whole, inward),
            ],
            [
                (whole, (1,) + wide[1:], f32),
                (whole, (1, rows, inner), bf16),
                (whole, (1, 1, MODEL_WIDTH), f32),
            ],
            us=3.7,
            after=before_final if s == seqs - 1 else (),
        )
        dinputs.append(dinput)
        dalls.append(dall)
        gain_one_grads.append(gain_one_grad)
    input_gradient = give(jnp.concatenate(dinputs, axis=0))
    inward_grad = weight_grad(jnp.concatenate(dalls, axis=0), normed_one).astype(bf16)
    gains_grad = jnp.concatenate(
        [sum(gain_one_grads)[0], jnp.sum(gain_two_grad, axis=0)], axis=0
    )
    packs = (chunks, first_part.shape[0], LANES)
    first_packs = call(
        functools.partial(pack_first_kernel, q_cols, kv_cols),
        1,
        [(whole, inward_grad), (whole, gains_grad)],
        [(whole, packs, bf16), (whole, packs, bf16)],
        scalars=(where,),
        us=3.5,
        after=before_pack,
    )
    first_sum = rows_scatter(reduced_packs(*first_packs, False)[0][:, :MODEL_WIDTH])
    reduced = (
        first_sum[:q_cols],
        first_sum[q_cols : q_cols + kv_cols],
        first_sum[q_cols + kv_cols : q_cols + 2 * kv_cols],
        *outer_reduced,
    )
    gains_total = first_sum[q_cols + 2 * kv_cols :].T
    rates = (
        (MODEL_WIDTH // 4) ** (-0.5),
        MODEL_WIDTH ** (-0.5),
        MODEL_WIDTH ** (-0.5),
        (MODEL_WIDTH // 32) ** (-0.5),
        MODEL_WIDTH ** (-0.5),
        MODEL_WIDTH ** (-0.5),
        (FF // 2) ** (-0.5),
    )
    firsts = (
        query_first,
        key_first_moment,
        value_first_moment,
        output_first,
        gate_first,
        up_first,
        down_first,
    )
    seconds = (
        query_second,
        key_second_moment,
        value_second_moment,
        output_second,
        gate_second,
        up_second,
        down_second,
    )
    results = [
        adam_update(
            masters[member], firsts[member], seconds[member], reduced[member].T, rates[member], DECAY
        )
        for member in range(7)
    ]
    results.append(adam_update(norm_gains, gains_first, gains_second, gains_total, GAIN_RATE, 0.0))
    new_weights = [result[0] for result in results]
    new_firsts = [result[1] for result in results]
    new_seconds = [result[2] for result in results]
    return tuple([block_output, input_gradient] + new_weights + new_firsts + new_seconds)


def solution(mesh):
    sequences = P("fsdp", "ctx", None)
    matrix = P("fsdp", "ctx")
    gains = P("fsdp", None)
    state = (matrix,) * 7 + (gains,)
    return jax.shard_map(
        body,
        mesh=mesh,
        in_specs=(sequences, sequences, P("fsdp", None)) + state * 3,
        out_specs=(sequences, sequences) + state * 3,
        check_vma=False,
    )
```

```python
import functools

import jax
import jax.numpy as jnp
from jax import lax
from jax.experimental import pallas as pl
from jax.experimental.pallas import tpu as pltpu
from jax.sharding import PartitionSpec as P

MODEL_WIDTH = 576
FF = 1536
HEADS = 9
KV_HEADS = 3
HEAD_DIM = 64
STEP = 10
GROUP = HEADS // KV_HEADS
KEY_WIDTH = KV_HEADS * HEAD_DIM
QUERY_WIDTH = HEADS * HEAD_DIM
PACK = 2 * HEAD_DIM
KV_PACKED = KV_HEADS * PACK
TILE = 256
FF_CHUNK = 640
LANES = 640
INNER = 1024
REST = FF // 2 - LANES

NORM_EPS = 1e-05
ROPE_BASE = 100000.0
BETA_ONE = 0.9
BETA_TWO = 0.95
ADAM_EPS = 1e-08
DECAY = 0.1
GAIN_RATE = 0.5
MASKED = -1e30
FLOPS_PER_US = 1153.5e6
VMEM_BYTES = 56 * 1024 * 1024

f32 = jnp.float32
bf16 = jnp.bfloat16


def dot_nt(a, b):
    return lax.dot_general(a, b, (((1,), (1,)), ((), ())), preferred_element_type=f32)


def dot_nn(a, b):
    return lax.dot_general(a, b, (((1,), (0,)), ((), ())), preferred_element_type=f32)


def lanes_of(shape):
    return lax.broadcasted_iota(jnp.int32, shape, len(shape) - 1)


def turned(v, first):
    lane = lanes_of(v.shape) % HEAD_DIM
    ahead = pltpu.roll(v, PACK - HEAD_DIM // 2, 1)
    behind = pltpu.roll(v, HEAD_DIM // 2, 1)
    if first:
        return jnp.where(lane < HEAD_DIM // 2, -ahead, behind)
    return jnp.where(lane < HEAD_DIM // 2, ahead, -behind)


def project_kernel(x_ref, gain_ref, weight_ref, cos_ref, sin_ref, normed_ref, query_ref, kv_ref):
    rows = x_ref.shape[1]
    blk = query_ref.shape[3] // GROUP
    x = x_ref[0].astype(f32)
    inv = lax.rsqrt(jnp.mean(x * x, axis=-1, keepdims=True) + NORM_EPS)
    normed = (x * inv * gain_ref[...]).astype(bf16)
    normed_ref[0] = normed
    raw = dot_nt(normed, weight_ref[...])
    cosine, sine = cos_ref[0], sin_ref[0]
    low_half = lanes_of((rows, PACK)) < HEAD_DIM
    for j in range(KV_HEADS):
        part = raw[:, j * PACK : (j + 1) * PACK]
        spun = part * cosine + turned(part, True) * sine
        kv_ref[0, :, j * PACK : (j + 1) * PACK] = jnp.where(low_half, spun, part).astype(bf16)
    for i in range((HEADS + 1) // 2):
        begin = KV_PACKED + i * PACK
        if 2 * i + 1 < HEADS:
            part = raw[:, begin : begin + PACK]
        else:
            tail = raw[:, begin : begin + HEAD_DIM]
            part = jnp.concatenate([tail, tail], axis=1)
        spun = part * cosine + turned(part, True) * sine
        spun = spun.astype(bf16).astype(f32) * (HEAD_DIM**-0.5)
        pair = [jnp.where(low_half, spun, 0.0)]
        if 2 * i + 1 < HEADS:
            pair.append(jnp.where(low_half, pltpu.roll(spun, HEAD_DIM, 1), 0.0))
        for offset, value in enumerate(pair):
            head = 2 * i + offset
            j, member = head // GROUP, head % GROUP
            value = value.astype(bf16)
            for b in range(rows // blk):
                query_ref[0, b, j, member * blk : (member + 1) * blk, :] = value[
                    b * blk : (b + 1) * blk
                ]


def sort_blocks(blocks_ref, s, kv_refs, sorted_ref, blk):
    per = kv_refs[0].shape[1] // blk
    for g, kv_ref in enumerate(kv_refs):
        for b in range(per):
            place = pl.multiple_of(blocks_ref[s, g * per + b] * blk, blk)
            sorted_ref[pl.ds(place, blk), :] = kv_ref[0, b * blk : (b + 1) * blk, :]


def allowed_mask(place, tile_begin, blk, rows):
    row = lax.broadcasted_iota(jnp.int32, (rows, TILE), 0) % blk
    col = lax.broadcasted_iota(jnp.int32, (rows, TILE), 1)
    return col <= row + (place * blk - tile_begin)


def attend_kernel(chunks, blocks_ref, query_ref, *refs):
    s = pl.program_id(0)
    kv_refs = refs[:chunks]
    out_ref, log_ref, sorted_ref, score_ref, top_ref, acc_ref = refs[chunks:]
    per, rows = query_ref.shape[1], query_ref.shape[3]
    blk = rows // GROUP
    sort_blocks(blocks_ref, s, kv_refs, sorted_ref, blk)
    lane = lanes_of((TILE, PACK))
    for b in range(per):
        place = blocks_ref[s, b]
        full = (place * blk) // TILE

        def score_tile(t, masked):
            begin = pl.multiple_of(t * TILE, TILE)
            for j in range(KV_HEADS):
                kv = sorted_ref[pl.ds(begin, TILE), j * PACK : (j + 1) * PACK]
                score = dot_nt(query_ref[0, b, j], kv)
                if masked:
                    score = jnp.where(allowed_mask(place, begin, blk, rows), score, MASKED)
                score_ref[j, t] = score
                best = jnp.maximum(score[:, :PACK], score[:, PACK:])
                top_ref[j] = jnp.maximum(top_ref[j], best)

        top_ref[...] = jnp.full(top_ref.shape, MASKED, f32)
        acc_ref[...] = jnp.zeros(acc_ref.shape, f32)

        @pl.loop(0, full)
        def _(t):
            score_tile(t, False)

        score_tile(full, True)
        for j in range(KV_HEADS):
            top = jnp.max(top_ref[j], axis=-1, keepdims=True)
            top_ref[j] = jnp.broadcast_to(top, (rows, PACK))

        @pl.loop(0, full + 1)
        def _(t):
            begin = pl.multiple_of(t * TILE, TILE)
            for j in range(KV_HEADS):
                kv = sorted_ref[pl.ds(begin, TILE), j * PACK : (j + 1) * PACK]
                ones_v = jnp.where(lane < HEAD_DIM, jnp.ones((), bf16), kv)
                top = top_ref[j]
                score = score_ref[j, t]
                prob = jnp.concatenate(
                    [jnp.exp(score[:, :PACK] - top), jnp.exp(score[:, PACK:] - top)], axis=1
                )
                acc_ref[j] += dot_nn(prob.astype(bf16), ones_v)

        for j in range(KV_HEADS):
            acc = acc_ref[j]
            low_half = lanes_of(acc.shape) < HEAD_DIM
            total = jnp.where(low_half, acc, pltpu.roll(acc, HEAD_DIM, 1))
            log_ref[0, b, j] = top_ref[j] + jnp.log(total)
            attended = (acc / total).astype(bf16)
            for member in range(GROUP):
                head = j * GROUP + member
                out_ref[0, b * blk : (b + 1) * blk, head * HEAD_DIM : (head + 1) * HEAD_DIM] = (
                    attended[member * blk : (member + 1) * blk, HEAD_DIM:]
                )


def unpack_second(place_ref, part_refs, pack_ref, sems, out_w_ref, gate_w_ref, up_w_ref, down_w_ref):
    ctx = pack_ref.shape[1]
    f_cols, o_cols, half = FF // ctx, MODEL_WIDTH // ctx, MODEL_WIDTH // 2
    copies = []
    for part, part_ref in enumerate(part_refs):
        core = jnp.abs(place_ref[0] - part // 2)
        plane = jnp.abs(place_ref[1] - part % 2)
        for k in range(part_ref.shape[0]):
            index = 2 * place_ref[2 + k] + core
            copies.append(
                pltpu.make_async_copy(
                    part_ref.at[k], pack_ref.at[plane, index], sems.at[part, k]
                )
            )
    for copy in copies:
        copy.start()
    for copy in copies:
        copy.wait()
    for c in range(ctx):
        here = slice(c * f_cols, (c + 1) * f_cols)
        low, high = pack_ref[0, c, :f_cols, :], pack_ref[1, c, :f_cols, :]
        gate_w_ref[here, :] = jnp.concatenate([low[:, :half], high[:, :half]], axis=1)
        up_w_ref[here, :] = jnp.concatenate(
            [low[:, half:MODEL_WIDTH], high[:, half:MODEL_WIDTH]], axis=1
        )

    def natural(plane, base, lanes):
        pieces = [
            pack_ref[plane, c, base : base + o_cols, lanes].astype(f32) for c in range(ctx)
        ]
        return jnp.concatenate(pieces, axis=0).astype(bf16)

    base = f_cols + o_cols
    for plane in range(2):
        begin = plane * (FF // 2)
        down_w_ref[:, begin : begin + LANES] = natural(plane, f_cols, slice(0, LANES))
        down_w_ref[:, begin + LANES : begin + FF // 2] = natural(plane, base, slice(0, REST))
    out_w_ref[...] = jnp.concatenate(
        [natural(plane, base, slice(REST, REST + half)) for plane in range(2)], axis=1
    )


def middle_kernel(
    place_ref,
    x_ref,
    attn_ref,
    cot_ref,
    gain_ref,
    part_a_ref,
    part_b_ref,
    part_c_ref,
    part_d_ref,
    block_ref,
    normed_ref,
    hidden_ref,
    dgate_ref,
    dup_ref,
    dattn_ref,
    dout_ref,
    dresid_ref,
    gain_grad_ref,
    out_w_ref,
    gate_w_ref,
    up_w_ref,
    down_w_ref,
    pack_ref,
    sems,
):
    @pl.when(pl.program_id(0) == 0)
    def _():
        parts = (part_a_ref, part_b_ref, part_c_ref, part_d_ref)
        unpack_second(
            place_ref, parts, pack_ref, sems, out_w_ref, gate_w_ref, up_w_ref, down_w_ref
        )

    attn = attn_ref[0]
    cot = cot_ref[0]
    resid = x_ref[0].astype(f32) + dot_nt(attn, out_w_ref[...])
    inv = lax.rsqrt(jnp.mean(resid * resid, axis=-1, keepdims=True) + NORM_EPS)
    hat = resid * inv
    gain = gain_ref[...]
    normed = (hat * gain).astype(bf16)
    normed_ref[0] = normed
    block = resid
    dnormed = jnp.zeros(resid.shape, f32)
    for begin in range(0, FF, FF_CHUNK):
        span = slice(begin, min(begin + FF_CHUNK, FF))
        gate = dot_nt(normed, gate_w_ref[span, :])
        up = dot_nt(normed, up_w_ref[span, :])
        sig = 1.0 / (1.0 + jnp.exp(-gate))
        act = gate * sig
        hidden = (act * up).astype(bf16)
        hidden_ref[0, :, span] = hidden
        block = block + dot_nt(hidden, down_w_ref[:, span])
        dhidden = dot_nn(cot, down_w_ref[:, span])
        dgate = (dhidden * up * (sig * (1.0 + gate * (1.0 - sig)))).astype(bf16)
        dup = (dhidden * act).astype(bf16)
        dgate_ref[0, :, span] = dgate
        dup_ref[0, :, span] = dup
        dnormed = dnormed + dot_nn(dgate, gate_w_ref[span, :]) + dot_nn(dup, up_w_ref[span, :])
    block_ref[0] = block
    gain_grad_ref[0] = jnp.sum(dnormed * hat, axis=0, keepdims=True)
    scaled = dnormed * gain
    dresid = cot.astype(f32) + inv * (scaled - hat * jnp.mean(scaled * hat, axis=-1, keepdims=True))
    dresid_ref[0] = dresid
    dattn = dresid.astype(bf16)
    dattn_ref[0] = dattn
    dout_ref[0] = dot_nn(dattn, out_w_ref[...]).astype(bf16)


def attend_back_kernel(chunks, first, blocks_ref, query_ref, *refs):
    s = first + pl.program_id(0)
    kv_refs = refs[:chunks]
    out_ref, dout_ref, log_ref, cos_ref, sin_ref, dquery_ref = refs[chunks : chunks + 6]
    dkv_refs = refs[chunks + 6 : 2 * chunks + 6]
    sorted_ref, both_ref, flip_ref, delta_ref, dq_ref, dkv_t_ref, dkv_s_ref = refs[2 * chunks + 6 :]
    per, rows = query_ref.shape[1], query_ref.shape[3]
    blk = rows // GROUP
    length = sorted_ref.shape[0]
    sort_blocks(blocks_ref, s, kv_refs, sorted_ref, blk)
    dkv_t_ref[...] = jnp.zeros(dkv_t_ref.shape, f32)
    for b in range(per):
        place = blocks_ref[s, b]
        full = (place * blk) // TILE
        span = slice(b * blk, (b + 1) * blk)
        for j in range(KV_HEADS):
            both_ref[j, :rows] = query_ref[0, b, j]
            for member in range(GROUP):
                head = j * GROUP + member
                lanes = slice(head * HEAD_DIM, (head + 1) * HEAD_DIM)
                dout = dout_ref[0, span, lanes]
                delta = jnp.sum(
                    dout.astype(f32) * out_ref[0, span, lanes].astype(f32), axis=-1, keepdims=True
                )
                here = slice(member * blk, (member + 1) * blk)
                delta_ref[j, here] = jnp.broadcast_to(delta, (blk, PACK))
                both_ref[j, rows + member * blk : rows + (member + 1) * blk] = jnp.concatenate(
                    [jnp.zeros_like(dout), dout], axis=1
                )
            flip_ref[j] = both_ref[j].T
        dq_ref[...] = jnp.zeros(dq_ref.shape, f32)

        def tile_step(t, masked):
            begin = pl.multiple_of(t * TILE, TILE)
            kvs = [
                sorted_ref[pl.ds(begin, TILE), j * PACK : (j + 1) * PACK] for j in range(KV_HEADS)
            ]
            joined = [dot_nt(both_ref[j], kvs[j]) for j in range(KV_HEADS)]
            dscores, joints = [], []
            for j in range(KV_HEADS):
                score, dprob = joined[j][:rows], joined[j][rows:]
                log_total = log_ref[0, b, j]
                delta = delta_ref[j]
                prob = jnp.concatenate(
                    [jnp.exp(score[:, :PACK] - log_total), jnp.exp(score[:, PACK:] - log_total)],
                    axis=1,
                )
                if masked:
                    prob = jnp.where(allowed_mask(place, begin, blk, rows), prob, 0.0)
                dscore = prob * jnp.concatenate(
                    [dprob[:, :PACK] - delta, dprob[:, PACK:] - delta], axis=1
                )
                dscores.append(dscore.astype(bf16))
                joints.append(jnp.concatenate([dscores[j], prob.astype(bf16)], axis=0))
            dqs = [dot_nn(dscores[j], kvs[j]) for j in range(KV_HEADS)]
            dkvs = [dot_nn(flip_ref[j], joints[j]) for j in range(KV_HEADS)]
            for j in range(KV_HEADS):
                dq_ref[j] += dqs[j]
                dkv_t_ref[j * PACK : (j + 1) * PACK, pl.ds(begin, TILE)] += dkvs[j]

        @pl.loop(0, full)
        def _(t):
            tile_step(t, False)

        tile_step(full, True)
        cosine, sine = cos_ref[0, span, :], sin_ref[0, span, :]
        for j in range(KV_HEADS):
            for member in range(GROUP):
                head = j * GROUP + member
                grad = dq_ref[j, member * blk : (member + 1) * blk]
                back = (grad * cosine + turned(grad, False) * sine) * (HEAD_DIM**-0.5)
                dquery_ref[0, span, head * HEAD_DIM : (head + 1) * HEAD_DIM] = back[
                    :, :HEAD_DIM
                ].astype(bf16)
    for begin in range(0, length, TILE):
        dkv_s_ref[begin : begin + TILE, :] = dkv_t_ref[:, begin : begin + TILE].T.astype(bf16)
    for g, dkv_ref in enumerate(dkv_refs):
        for b in range(per):
            place = pl.multiple_of(blocks_ref[s, g * per + b] * blk, blk)
            dkv_ref[0, b * blk : (b + 1) * blk, :] = dkv_s_ref[pl.ds(place, blk), :]


def final_kernel(
    x_ref,
    gain_ref,
    dquery_ref,
    dkv_ref,
    dresid_ref,
    cos_ref,
    sin_ref,
    weight_ref,
    dinput_ref,
    dall_ref,
    gain_grad_ref,
):
    rows = x_ref.shape[1]
    cosine, sine = cos_ref[0], sin_ref[0]
    low_half = lanes_of((rows, PACK)) < HEAD_DIM
    for j in range(KV_HEADS):
        part = dkv_ref[0, :, j * PACK : (j + 1) * PACK].astype(f32)
        back = part * cosine + turned(part, False) * sine
        dall_ref[0, :, j * PACK : (j + 1) * PACK] = jnp.where(low_half, back, part).astype(bf16)
    used = KV_PACKED + QUERY_WIDTH
    dall_ref[0, :, KV_PACKED:used] = dquery_ref[0]
    dall_ref[0, :, used:] = jnp.zeros((rows, INNER - used), bf16)
    dnormed = dot_nn(dall_ref[0, :, :used], weight_ref[...])
    x = x_ref[0].astype(f32)
    inv = lax.rsqrt(jnp.mean(x * x, axis=-1, keepdims=True) + NORM_EPS)
    hat = x * inv
    gain_grad_ref[0] = jnp.sum(dnormed * hat, axis=0, keepdims=True)
    scaled = dnormed * gain_ref[...]
    dinput_ref[0] = dresid_ref[0] + inv * (
        scaled - hat * jnp.mean(scaled * hat, axis=-1, keepdims=True)
    )


def natural_pieces(where_ref, own_ref, other_ref, begin, size):
    zero = where_ref[0] == 0
    pieces = []
    for g in range(own_ref.shape[0]):
        slot = where_ref[1 + g]
        mine = own_ref[slot, begin : begin + size, :].astype(f32)
        theirs = other_ref[slot, begin : begin + size, :].astype(f32)
        pieces.append(jnp.where(zero, mine, theirs))
        pieces.append(jnp.where(zero, theirs, mine))
    return jnp.concatenate(pieces, axis=0).astype(bf16)


def unpack_first_kernel(q_cols, kv_cols, where_ref, own_ref, other_ref, inward_ref):
    width = inward_ref.shape[1]
    query = natural_pieces(where_ref, own_ref, other_ref, 0, q_cols)
    inward_ref[KV_PACKED:, :] = query[:, :width]
    for offset in range(2):
        part = natural_pieces(where_ref, own_ref, other_ref, q_cols + offset * kv_cols, kv_cols)
        for j in range(KV_HEADS):
            begin = j * PACK + offset * HEAD_DIM
            inward_ref[begin : begin + HEAD_DIM, :] = part[
                j * HEAD_DIM : (j + 1) * HEAD_DIM, :width
            ]


def pack_rows(where_ref, own_ref, other_ref, source, begin, size):
    zero = where_ref[0] == 0
    lanes = source.shape[1]
    for g in range(own_ref.shape[0]):
        slot = where_ref[1 + g]
        even = source[2 * g * size : (2 * g + 1) * size]
        odd = source[(2 * g + 1) * size : (2 * g + 2) * size]
        own_ref[slot, begin : begin + size, :lanes] = jnp.where(zero, even, odd).astype(bf16)
        other_ref[slot, begin : begin + size, :lanes] = jnp.where(zero, odd, even).astype(bf16)


def pack_first_kernel(q_cols, kv_cols, parts, where_ref, normed_ref, *refs):
    dall_refs, (gains_ref, own_ref, other_ref, grad_ref) = refs[:parts], refs[parts:]
    width = grad_ref.shape[1]
    seq = 0
    for dall_ref in dall_refs:
        for s in range(dall_ref.shape[0]):
            term = dot_nn(dall_ref[s].T, normed_ref[seq])
            grad_ref[...] = term if seq == 0 else grad_ref[...] + term
            seq += 1
    query = grad_ref[KV_PACKED : KV_PACKED + QUERY_WIDTH, :]
    pack_rows(where_ref, own_ref, other_ref, query, 0, q_cols)
    for offset in range(2):
        part = jnp.concatenate(
            [
                grad_ref[j * PACK + offset * HEAD_DIM : j * PACK + (offset + 1) * HEAD_DIM, :]
                for j in range(KV_HEADS)
            ],
            axis=0,
        )
        pack_rows(where_ref, own_ref, other_ref, part, q_cols + offset * kv_cols, kv_cols)
    begin = q_cols + 2 * kv_cols
    for g in range(own_ref.shape[0]):
        own_ref[g, begin : begin + 2, :width] = gains_ref[...].astype(bf16)
        other_ref[g, begin : begin + 2, :width] = gains_ref[...].astype(bf16)


def pack_second_kernel(
    place_ref, out_g_ref, gate_g_ref, up_g_ref, down_g_ref, a_ref, b_ref, c_ref, d_ref, pack_ref, sems
):
    ctx = pack_ref.shape[1]
    f_cols, o_cols, half = FF // ctx, MODEL_WIDTH // ctx, MODEL_WIDTH // 2
    base = f_cols + o_cols
    for plane in range(2):
        lanes = slice(plane * half, (plane + 1) * half)
        for c in range(ctx):
            here = slice(c * f_cols, (c + 1) * f_cols)
            pack_ref[plane, c, :f_cols, :MODEL_WIDTH] = jnp.concatenate(
                [gate_g_ref[here, lanes], up_g_ref[here, lanes]], axis=1
            )
        begin = plane * (FF // 2)
        first = down_g_ref[:, begin : begin + LANES].astype(f32)
        rest = down_g_ref[:, begin + LANES : begin + FF // 2]
        second = jnp.concatenate([rest, out_g_ref[:, lanes]], axis=1).astype(f32)
        for c in range(ctx):
            here = slice(c * o_cols, (c + 1) * o_cols)
            pack_ref[plane, c, f_cols:base, :] = first[here].astype(bf16)
            pack_ref[plane, c, base : base + o_cols, : REST + half] = second[here].astype(bf16)
    copies = []
    for part, part_ref in enumerate((a_ref, b_ref, c_ref, d_ref)):
        core = jnp.abs(place_ref[0] - part // 2)
        plane = jnp.abs(place_ref[1] - part % 2)
        for k in range(part_ref.shape[0]):
            index = 2 * place_ref[2 + k] + core
            copies.append(
                pltpu.make_async_copy(
                    pack_ref.at[plane, index], part_ref.at[k], sems.at[part, k]
                )
            )
    for copy in copies:
        copy.start()
    for copy in copies:
        copy.wait()


def one(shape):
    rest = tuple(shape[1:])
    return pl.BlockSpec((1,) + rest, lambda s, *_: (s,) + (0,) * len(rest))


def whole(shape):
    return pl.BlockSpec(tuple(shape), lambda s, *_: (0,) * len(shape))


def anywhere(shape):
    return pl.BlockSpec(memory_space=pl.ANY)


def since(first):
    def make(shape):
        rest = tuple(shape[1:])
        return pl.BlockSpec((1,) + rest, lambda s, *_: (first + s,) + (0,) * len(rest))

    return make


def call(kernel, seqs, inputs, outputs, scalars=(), scratch=(), us=1.0, after=()):
    begin = len(scalars) + len(inputs)

    def body_of(*refs):
        kernel(*refs[:begin], *refs[begin + len(after) :])

    in_specs = [make(array.shape) for make, array in inputs]
    in_specs += [anywhere(array.shape) for array in after]
    out_specs = [make(shape) for make, shape, _ in outputs]
    moved = sum(array.size * array.dtype.itemsize for _, array in inputs)
    for _, shape, kind in outputs:
        count = 1
        for size in shape:
            count *= size
        moved += count * jnp.dtype(kind).itemsize
    return pl.pallas_call(
        body_of,
        grid_spec=pltpu.PrefetchScalarGridSpec(
            num_scalar_prefetch=len(scalars),
            grid=(seqs,),
            in_specs=in_specs,
            out_specs=out_specs,
            scratch_shapes=list(scratch),
        ),
        out_shape=[jax.ShapeDtypeStruct(shape, kind) for _, shape, kind in outputs],
        compiler_params=pltpu.CompilerParams(vmem_limit_bytes=VMEM_BYTES),
        cost_estimate=pl.CostEstimate(
            flops=int(us * FLOPS_PER_US), bytes_accessed=int(moved), transcendentals=0
        ),
    )(*scalars, *[array for _, array in inputs], *after)


def join_kernel(*refs):
    del refs


def join(arrays, *after):
    return pl.pallas_call(
        join_kernel,
        in_specs=[pl.BlockSpec(memory_space=pl.ANY)] * (len(arrays) + len(after)),
        out_specs=[pl.BlockSpec(memory_space=pl.ANY)] * len(arrays),
        out_shape=[jax.ShapeDtypeStruct(array.shape, array.dtype) for array in arrays],
        input_output_aliases={i: i for i in range(len(arrays))},
    )(*arrays, *after)


def adam_update(weight, first, second, grad, rate, decay):
    first_next = BETA_ONE * first + (1.0 - BETA_ONE) * grad
    second_next = BETA_TWO * second + (1.0 - BETA_TWO) * grad * grad
    first_fix = first_next / (1.0 - BETA_ONE**STEP)
    second_fix = second_next / (1.0 - BETA_TWO**STEP)
    update = first_fix / (jnp.sqrt(second_fix) + ADAM_EPS) + decay * weight
    return (weight - rate * update, first_next, second_next)


def ring_of(chips):
    if chips == 8:
        return [0, 2, 4, 6, 7, 5, 3, 1]
    return list(range(chips))


def ring_pairs(chips, step):
    ring = ring_of(chips)
    return [
        (2 * ring[p] + core, 2 * ring[(p + step) % chips] + core)
        for p in range(chips)
        for core in range(2)
    ]


def ring_gather(mine, flip, pins=None, trace=None):
    chips = lax.axis_size("ctx") // 2
    steps = (chips // 2, (chips - 1) // 2)
    if flip:
        steps = steps[::-1]
    result = [mine] * chips
    ahead = behind = mine
    for t in range(1, max(steps) + 1):
        if t <= steps[0]:
            ahead = lax.ppermute(ahead, "ctx", ring_pairs(chips, 1))
            result[-t % chips] = ahead
        if t <= steps[1]:
            behind = lax.ppermute(behind, "ctx", ring_pairs(chips, -1))
            result[t] = behind
        if pins and t in pins and t <= min(steps):
            ahead, behind = join([ahead, behind], *pins[t])
            result[-t % chips], result[t] = ahead, behind
        if trace is not None:
            trace.append([ahead, behind])
    return result


def plus(*terms):
    total = terms[0].astype(f32)
    for term in terms[1:]:
        total = total + term.astype(f32)
    return total


def ring_scatter(terms, flip):
    chips = lax.axis_size("ctx") // 2
    steps = (chips // 2, (chips - 1) // 2)
    if flip:
        steps = steps[::-1]
    moving = [terms[steps[0]]().astype(bf16), terms[-steps[1] % chips]().astype(bf16)]
    trace = []
    for t in range(max(steps)):
        for way in range(2):
            left = steps[way] - 1 - t
            if left < 0:
                continue
            sign = 1 - 2 * way
            got = lax.ppermute(moving[way], "ctx", ring_pairs(chips, sign))
            if left:
                got = plus(got, terms[sign * left % chips]()).astype(bf16)
            moving[way] = got
        trace.append(list(moving))
    return plus(terms[0](), moving[0], moving[1]), trace


def rows_gather(part):
    if lax.axis_size("fsdp") != 2:
        return lax.all_gather(part, "fsdp", axis=1, tiled=True)
    first = lax.axis_index("fsdp") == 0
    got = lax.ppermute(part, "fsdp", [(0, 1), (1, 0)])
    return jnp.concatenate([jnp.where(first, part, got), jnp.where(first, got, part)], axis=1)


def rows_scatter(grads):
    fsdp = lax.axis_size("fsdp")
    if fsdp != 2:
        return lax.psum_scatter(
            grads.astype(bf16), "fsdp", scatter_dimension=1, tiled=True
        ).astype(f32)
    first = lax.axis_index("fsdp") == 0
    half = grads.shape[1] // 2
    low, high = grads[:, :half], grads[:, half:]
    got = lax.ppermute(jnp.where(first, high, low).astype(bf16), "fsdp", [(0, 1), (1, 0)])
    return jnp.where(first, low, high) + got.astype(f32)


def widen(array):
    return jnp.pad(array, ((0, 0), (0, LANES - array.shape[1])))


def weight_grad(left, right):
    return lax.dot_general(left, right, (((0, 1), (0, 1)), ((), ())), preferred_element_type=f32)


def body(
    tokens,
    cotangent,
    pair_order,
    query_weight,
    key_master_weight,
    value_master_weight,
    output_weight,
    gate_weight,
    up_weight,
    down_weight,
    norm_gains,
    query_first,
    key_first_moment,
    value_first_moment,
    output_first,
    gate_first,
    up_first,
    down_first,
    gains_first,
    query_second,
    key_second_moment,
    value_second_moment,
    output_second,
    gate_second,
    up_second,
    down_second,
    gains_second,
):
    masters = (
        query_weight,
        key_master_weight,
        value_master_weight,
        output_weight,
        gate_weight,
        up_weight,
        down_weight,
    )
    ctx = lax.axis_size("ctx")
    index = lax.axis_index("ctx")
    chunks = ctx // 2
    core = index % 2
    seqs = tokens.shape[0] // 2
    part_rows = tokens.shape[1]
    rows = 2 * part_rows
    blk = part_rows // 2
    per = rows // blk
    length = part_rows * ctx
    mine, other = core * seqs, (1 - core) * seqs
    partners = [(i, i ^ 1) for i in range(ctx)]

    def take(array):
        own = lax.dynamic_slice_in_dim(array, mine, seqs, 0)
        got = lax.ppermute(lax.dynamic_slice_in_dim(array, other, seqs, 0), "ctx", partners)
        return jnp.concatenate([own, got], axis=1)

    def give(array):
        got = lax.ppermute(array[:, part_rows:], "ctx", partners)
        result = jnp.zeros((2 * seqs, part_rows) + array.shape[2:], array.dtype)
        result = lax.dynamic_update_slice_in_dim(result, array[:, :part_rows], mine, 0)
        return lax.dynamic_update_slice_in_dim(result, got, other, 0)

    ring = ring_of(chunks)
    position_of = [ring.index(g) for g in range(chunks)]
    position = jnp.array(position_of, jnp.int32)[index // 2]
    slots = (jnp.array(position_of, jnp.int32) - position) % chunks
    where = jnp.concatenate([core[None].astype(jnp.int32), slots])
    reached = jnp.array(ring, jnp.int32)[(position + jnp.arange(chunks)) % chunks]
    two_planes = lax.axis_size("fsdp") == 2
    plane = lax.axis_index("fsdp") if two_planes else jnp.zeros((), jnp.int32)
    place = jnp.concatenate([core[None].astype(jnp.int32), plane[None].astype(jnp.int32), reached])
    planes = [(0, 1), (1, 0)]

    turned_low = [matrix.astype(bf16).T for matrix in masters]
    q_cols, kv_cols = QUERY_WIDTH // ctx, KEY_WIDTH // ctx
    o_cols, f_cols = MODEL_WIDTH // ctx, FF // ctx

    def both_packs(pack, flip):
        stack = jnp.stack(ring_gather(pack, flip), axis=0)
        return stack, lax.ppermute(stack, "ctx", partners)

    first_part = rows_gather(jnp.concatenate(turned_low[:3] + [norm_gains.astype(bf16).T], axis=0))
    first_used = first_part.shape[0]
    first_part = jnp.pad(first_part, ((0, -first_used % 16), (0, 0)))
    gains = first_part[q_cols + 2 * kv_cols : first_used].astype(f32)
    gain_one, gain_two = gains[0:1], gains[1:2]
    first_own, first_other = both_packs(widen(first_part), False)
    (inward,) = call(
        functools.partial(unpack_first_kernel, q_cols, kv_cols),
        1,
        [(whole, first_own), (whole, first_other)],
        [(whole, (KV_PACKED + QUERY_WIDTH, MODEL_WIDTH), bf16)],
        scalars=(where,),
        us=3.3,
    )
    half = MODEL_WIDTH // 2

    def second_part(gate, up, output, down):
        return jnp.concatenate(
            [
                widen(jnp.concatenate([gate, up], axis=1)),
                down[:, :LANES],
                widen(jnp.concatenate([down[:, LANES:], output], axis=1)),
            ],
            axis=0,
        )

    def later(part):
        return lax.optimization_barrier((part, first_other))[0]

    x = take(tokens)
    cot = take(cotangent)
    order = lax.dynamic_slice_in_dim(pair_order, mine, seqs, 0)
    ends = jnp.stack([order, 2 * ctx - 1 - order], axis=2).reshape(seqs, chunks, 2, 2)
    ends = jnp.where(core == 0, ends, ends[:, :, ::-1])
    ends = ends.reshape(seqs, chunks, per)
    blocks = jnp.take(ends, reached, axis=1).reshape(seqs, chunks * per)
    own = blocks[:, :per]
    places = (own[:, :, None] * blk + jnp.arange(blk, dtype=jnp.int32)).reshape(seqs, rows)
    half_dim = HEAD_DIM // 2
    inverse = ROPE_BASE ** (-jnp.arange(half_dim, dtype=f32) * 2.0 / HEAD_DIM)
    angle = places.astype(f32)[..., None] * inverse
    cosine = jnp.tile(jnp.cos(angle), (1, 1, PACK // half_dim))
    sine = jnp.tile(jnp.sin(angle), (1, 1, PACK // half_dim))

    wide = (seqs, rows, MODEL_WIDTH)
    heads = (seqs, per, KV_HEADS, GROUP * blk, PACK)
    normed_one, query, kv = call(
        project_kernel,
        seqs,
        [(one, x), (whole, gain_one), (whole, inward), (one, cosine), (one, sine)],
        [(one, wide, bf16), (one, heads, bf16), (one, (seqs, rows, KV_PACKED), bf16)],
        us=6.2,
    )
    load = length / 2048
    tile_rows = (KV_HEADS, GROUP * blk, PACK)
    kv_trace = []
    kv_all = ring_gather(kv, False, trace=kv_trace)
    outer = (turned_low[4], turned_low[5], turned_low[3], turned_low[6])
    if two_planes:
        same = jnp.stack(ring_gather(later(second_part(*outer)), True, {1: [inward], 2: kv_trace[0], 3: kv_trace[1]}), axis=0)
        cross = lax.ppermute(same, "fsdp", planes)
    else:
        outer = [rows_gather(part) for part in outer]
        same, cross = [
            jnp.stack(
                ring_gather(
                    second_part(*[jnp.split(part, 2, axis=1)[side] for part in outer]), True
                ),
                axis=0,
            )
            for side in range(2)
        ]
    second_parts = [same, cross] + [lax.ppermute(part, "ctx", partners) for part in (same, cross)]

    attn, logs = call(
        functools.partial(attend_kernel, chunks),
        seqs,
        [(one, query)] + [(one, chunk) for chunk in kv_all],
        [(one, wide, bf16), (one, heads, f32)],
        scalars=(blocks,),
        scratch=[
            pltpu.VMEM((length, KV_PACKED), bf16),
            pltpu.VMEM((KV_HEADS, length // TILE, GROUP * blk, TILE), f32),
            pltpu.VMEM(tile_rows, f32),
            pltpu.VMEM(tile_rows, f32),
        ],
        us=11.0 * seqs * load,
    )
    ff_wide = (seqs, rows, FF)
    (
        block_local,
        normed_two,
        hidden,
        dgate,
        dup,
        dattn,
        dout,
        dresid,
        gain_two_grad,
    ) = call(
        middle_kernel,
        seqs,
        [
            (one, x),
            (one, attn),
            (one, cot),
            (whole, gain_two),
        ]
        + [(anywhere, part) for part in second_parts],
        [
            (one, wide, f32),
            (one, wide, bf16),
            (one, ff_wide, bf16),
            (one, ff_wide, bf16),
            (one, ff_wide, bf16),
            (one, wide, bf16),
            (one, wide, bf16),
            (one, wide, f32),
            (one, (seqs, 1, MODEL_WIDTH), f32),
        ],
        scratch=[
            pltpu.VMEM((MODEL_WIDTH, QUERY_WIDTH), bf16),
            pltpu.VMEM((FF, MODEL_WIDTH), bf16),
            pltpu.VMEM((FF, MODEL_WIDTH), bf16),
            pltpu.VMEM((MODEL_WIDTH, FF), bf16),
            pltpu.VMEM((2, ctx) + same.shape[1:], bf16),
            pltpu.SemaphoreType.DMA((4, chunks)),
        ],
        scalars=(place,),
        us=26.0,
    )
    block_output = give(block_local)
    def reduced_packs(own_packs, other_packs, flip):
        got = lax.ppermute(other_packs, "ctx", partners)
        terms = [lambda k=k: plus(own_packs[k], got[k]) for k in range(chunks)]
        return ring_scatter(terms, flip)

    def outer_sums(earlier):
        behind = traces[-1]
        dattn_, dgate_ = join([dattn, dgate], earlier)
        (dup_,) = join([dup], *behind[0])
        (hidden_,) = join([hidden], *behind[1])
        packs = call(
            pack_second_kernel,
            1,
            [
                (whole, weight_grad(dattn_, attn).astype(bf16)),
                (whole, weight_grad(dgate_, normed_two).astype(bf16)),
                (whole, weight_grad(dup_, normed_two).astype(bf16)),
                (whole, weight_grad(cot, hidden_).astype(bf16)),
            ],
            [(anywhere, same.shape, bf16)] * 4,
            scalars=(place,),
            scratch=[
                pltpu.VMEM((2, ctx) + same.shape[1:], bf16),
                pltpu.SemaphoreType.DMA((4, chunks)),
            ],
            us=7.7,
            after=behind[2],
        )
        got = [lax.ppermute(part, "ctx", partners) for part in packs[2:]]
        if two_planes:
            sent = lax.ppermute(plus(packs[1], got[1]).astype(bf16), "fsdp", planes)
            terms = [lambda k=k: plus(packs[0][k], got[0][k], sent[k]) for k in range(chunks)]
            sums, trace = ring_scatter(terms, True)
            sums, before_last, before_final = [sums], got, [sent]
        else:
            sums = [
                ring_scatter(
                    [lambda k=k, i=i: plus(packs[i][k], got[i][k]) for k in range(chunks)], True
                )[0]
                for i in range(2)
            ]
            before_last, before_final, trace = got, [], [[], []]
        base = f_cols + o_cols
        result = []
        for pick in (
            lambda part: part[base:, REST : REST + half],
            lambda part: part[:f_cols, :half],
            lambda part: part[:f_cols, half:MODEL_WIDTH],
            lambda part: jnp.concatenate([part[f_cols:base], part[base:, :REST]], axis=1),
        ):
            if two_planes:
                result.append(pick(sums[0]))
            else:
                result.append(rows_scatter(jnp.concatenate([pick(part) for part in sums], axis=1)))
        return result, before_last, before_final, trace[1]

    dinputs, dalls, gain_one_grads, traces = [], [], [], []
    last = seqs - 1
    for first, count in ((0, last), (last, 1)):
        these = since(first)
        waits = []
        if first == last:
            outer_reduced, before_last, before_final, before_pack = outer_sums(dquery)
            waits = before_last
        dquery, *dkv = call(
            functools.partial(attend_back_kernel, chunks, first),
            count,
            [(these, query)]
            + [(these, chunk) for chunk in kv_all]
            + [(these, array) for array in (attn, dout, logs, cosine, sine)],
            [(one, (count,) + wide[1:], bf16)] + [(one, (count, rows, KV_PACKED), bf16)] * chunks,
            scalars=(blocks,),
            scratch=[
                pltpu.VMEM((length, KV_PACKED), bf16),
                pltpu.VMEM((KV_HEADS, 2 * GROUP * blk, PACK), bf16),
                pltpu.VMEM((KV_HEADS, PACK, 2 * GROUP * blk), bf16),
                pltpu.VMEM(tile_rows, f32),
                pltpu.VMEM(tile_rows, f32),
                pltpu.VMEM((KV_PACKED, length), f32),
                pltpu.VMEM((length, KV_PACKED), bf16),
            ],
            us=17.0 * count * load,
            after=waits,
        )
        dkv_own, trace = ring_scatter(
            [lambda k=k, dkv=dkv: dkv[k] for k in range(chunks)], first > 0
        )
        traces.append(trace)
        dinput, dall, gain_one_grad = call(
            final_kernel,
            count,
            [
                (these, x),
                (whole, gain_one),
                (one, dquery),
                (one, dkv_own),
                (these, dresid),
                (these, cosine),
                (these, sine),
                (whole, inward),
            ],
            [
                (one, (count,) + wide[1:], f32),
                (one, (count, rows, INNER), bf16),
                (one, (count, 1, MODEL_WIDTH), f32),
            ],
            us=2.0 * count,
            after=before_final if first == last else (),
        )
        dinputs.append(dinput)
        dalls.append(dall)
        gain_one_grads.append(jnp.sum(gain_one_grad, axis=0))
    input_gradient = give(jnp.concatenate(dinputs, axis=0))
    gains_grad = jnp.concatenate([sum(gain_one_grads), jnp.sum(gain_two_grad, axis=0)], axis=0)
    packs = (chunks, first_part.shape[0], LANES)
    first_packs = call(
        functools.partial(pack_first_kernel, q_cols, kv_cols, len(dalls)),
        1,
        [(whole, normed_one)] + [(whole, dall) for dall in dalls] + [(whole, gains_grad)],
        [(whole, packs, bf16), (whole, packs, bf16)],
        scalars=(where,),
        scratch=[pltpu.VMEM((INNER, MODEL_WIDTH), f32)],
        us=3.5,
        after=before_pack,
    )
    first_sum = rows_scatter(reduced_packs(*first_packs, False)[0][:, :MODEL_WIDTH])
    reduced = (
        first_sum[:q_cols],
        first_sum[q_cols : q_cols + kv_cols],
        first_sum[q_cols + kv_cols : q_cols + 2 * kv_cols],
        *outer_reduced,
    )
    gains_total = first_sum[q_cols + 2 * kv_cols : first_used].T
    rates = (
        (MODEL_WIDTH // 4) ** (-0.5),
        MODEL_WIDTH ** (-0.5),
        MODEL_WIDTH ** (-0.5),
        (MODEL_WIDTH // 32) ** (-0.5),
        MODEL_WIDTH ** (-0.5),
        MODEL_WIDTH ** (-0.5),
        (FF // 2) ** (-0.5),
    )
    firsts = (
        query_first,
        key_first_moment,
        value_first_moment,
        output_first,
        gate_first,
        up_first,
        down_first,
    )
    seconds = (
        query_second,
        key_second_moment,
        value_second_moment,
        output_second,
        gate_second,
        up_second,
        down_second,
    )
    results = [
        adam_update(
            masters[member], firsts[member], seconds[member], reduced[member].T, rates[member], DECAY
        )
        for member in range(7)
    ]
    results.append(adam_update(norm_gains, gains_first, gains_second, gains_total, GAIN_RATE, 0.0))
    new_weights = [result[0] for result in results]
    new_firsts = [result[1] for result in results]
    new_seconds = [result[2] for result in results]
    return tuple([block_output, input_gradient] + new_weights + new_firsts + new_seconds)


def solution(mesh):
    sequences = P("fsdp", "ctx", None)
    matrix = P("fsdp", "ctx")
    gains = P("fsdp", None)
    state = (matrix,) * 7 + (gains,)
    return jax.shard_map(
        body,
        mesh=mesh,
        in_specs=(sequences, sequences, P("fsdp", None)) + state * 3,
        out_specs=(sequences, sequences) + state * 3,
        check_vma=False,
    )
```

```python
import functools

import jax
import jax.numpy as jnp
from jax import lax
from jax.experimental import pallas as pl
from jax.experimental.pallas import tpu as pltpu
from jax.sharding import PartitionSpec as P

MODEL_WIDTH = 576
FF = 1536
HEADS = 9
KV_HEADS = 3
HEAD_DIM = 64
STEP = 10
GROUP = HEADS // KV_HEADS
KEY_WIDTH = KV_HEADS * HEAD_DIM
QUERY_WIDTH = HEADS * HEAD_DIM
PACK = 2 * HEAD_DIM
KV_PACKED = KV_HEADS * PACK
TILE = 256
FF_CHUNK = 640
LANES = 640
INNER = 1024
REST = FF // 2 - LANES

NORM_EPS = 1e-05
ROPE_BASE = 100000.0
BETA_ONE = 0.9
BETA_TWO = 0.95
ADAM_EPS = 1e-08
DECAY = 0.1
GAIN_RATE = 0.5
MASKED = -1e30
FLOPS_PER_US = 1153.5e6
VMEM_BYTES = 56 * 1024 * 1024

f32 = jnp.float32
bf16 = jnp.bfloat16


def dot_nt(a, b):
    return lax.dot_general(a, b, (((1,), (1,)), ((), ())), preferred_element_type=f32)


def dot_nn(a, b):
    return lax.dot_general(a, b, (((1,), (0,)), ((), ())), preferred_element_type=f32)


def lanes_of(shape):
    return lax.broadcasted_iota(jnp.int32, shape, len(shape) - 1)


def turned(v, first):
    lane = lanes_of(v.shape) % HEAD_DIM
    ahead = pltpu.roll(v, PACK - HEAD_DIM // 2, 1)
    behind = pltpu.roll(v, HEAD_DIM // 2, 1)
    if first:
        return jnp.where(lane < HEAD_DIM // 2, -ahead, behind)
    return jnp.where(lane < HEAD_DIM // 2, ahead, -behind)


def project_kernel(x_ref, gain_ref, weight_ref, cos_ref, sin_ref, normed_ref, query_ref, kv_ref):
    rows = x_ref.shape[1]
    blk = query_ref.shape[3] // GROUP
    x = x_ref[0].astype(f32)
    inv = lax.rsqrt(jnp.mean(x * x, axis=-1, keepdims=True) + NORM_EPS)
    normed = (x * inv * gain_ref[...]).astype(bf16)
    normed_ref[0] = normed
    raw = dot_nt(normed, weight_ref[...])
    cosine, sine = cos_ref[0], sin_ref[0]
    low_half = lanes_of((rows, PACK)) < HEAD_DIM
    for j in range(KV_HEADS):
        part = raw[:, j * PACK : (j + 1) * PACK]
        spun = part * cosine + turned(part, True) * sine
        kv_ref[0, :, j * PACK : (j + 1) * PACK] = jnp.where(low_half, spun, part).astype(bf16)
    for i in range((HEADS + 1) // 2):
        begin = KV_PACKED + i * PACK
        if 2 * i + 1 < HEADS:
            part = raw[:, begin : begin + PACK]
        else:
            tail = raw[:, begin : begin + HEAD_DIM]
            part = jnp.concatenate([tail, tail], axis=1)
        spun = part * cosine + turned(part, True) * sine
        spun = spun.astype(bf16).astype(f32) * (HEAD_DIM**-0.5)
        pair = [jnp.where(low_half, spun, 0.0)]
        if 2 * i + 1 < HEADS:
            pair.append(jnp.where(low_half, pltpu.roll(spun, HEAD_DIM, 1), 0.0))
        for offset, value in enumerate(pair):
            head = 2 * i + offset
            j, member = head // GROUP, head % GROUP
            value = value.astype(bf16)
            for b in range(rows // blk):
                query_ref[0, b, j, member * blk : (member + 1) * blk, :] = value[
                    b * blk : (b + 1) * blk
                ]


def sort_blocks(blocks_ref, s, kv_refs, sorted_ref, blk):
    per = kv_refs[0].shape[1] // blk
    for g, kv_ref in enumerate(kv_refs):
        for b in range(per):
            place = pl.multiple_of(blocks_ref[s, g * per + b] * blk, blk)
            sorted_ref[pl.ds(place, blk), :] = kv_ref[0, b * blk : (b + 1) * blk, :]


def allowed_mask(place, tile_begin, blk, rows):
    row = lax.broadcasted_iota(jnp.int32, (rows, TILE), 0) % blk
    col = lax.broadcasted_iota(jnp.int32, (rows, TILE), 1)
    return col <= row + (place * blk - tile_begin)


def attend_kernel(chunks, blocks_ref, query_ref, *refs):
    s = pl.program_id(0)
    kv_refs = refs[:chunks]
    out_ref, log_ref, sorted_ref, score_ref, top_ref, acc_ref = refs[chunks:]
    per, rows = query_ref.shape[1], query_ref.shape[3]
    blk = rows // GROUP
    sort_blocks(blocks_ref, s, kv_refs, sorted_ref, blk)
    lane = lanes_of((TILE, PACK))
    for b in range(per):
        place = blocks_ref[s, b]
        full = (place * blk) // TILE

        def score_tile(t, masked):
            begin = pl.multiple_of(t * TILE, TILE)
            for j in range(KV_HEADS):
                kv = sorted_ref[pl.ds(begin, TILE), j * PACK : (j + 1) * PACK]
                score = dot_nt(query_ref[0, b, j], kv)
                if masked:
                    score = jnp.where(allowed_mask(place, begin, blk, rows), score, MASKED)
                score_ref[j, t] = score
                best = jnp.maximum(score[:, :PACK], score[:, PACK:])
                top_ref[j] = jnp.maximum(top_ref[j], best)

        top_ref[...] = jnp.full(top_ref.shape, MASKED, f32)
        acc_ref[...] = jnp.zeros(acc_ref.shape, f32)

        @pl.loop(0, full)
        def _(t):
            score_tile(t, False)

        score_tile(full, True)
        for j in range(KV_HEADS):
            top = jnp.max(top_ref[j], axis=-1, keepdims=True)
            top_ref[j] = jnp.broadcast_to(top, (rows, PACK))

        @pl.loop(0, full + 1)
        def _(t):
            begin = pl.multiple_of(t * TILE, TILE)
            for j in range(KV_HEADS):
                kv = sorted_ref[pl.ds(begin, TILE), j * PACK : (j + 1) * PACK]
                ones_v = jnp.where(lane < HEAD_DIM, jnp.ones((), bf16), kv)
                top = top_ref[j]
                score = score_ref[j, t]
                prob = jnp.concatenate(
                    [jnp.exp(score[:, :PACK] - top), jnp.exp(score[:, PACK:] - top)], axis=1
                )
                acc_ref[j] += dot_nn(prob.astype(bf16), ones_v)

        for j in range(KV_HEADS):
            acc = acc_ref[j]
            low_half = lanes_of(acc.shape) < HEAD_DIM
            total = jnp.where(low_half, acc, pltpu.roll(acc, HEAD_DIM, 1))
            log_ref[0, b, j] = top_ref[j] + jnp.log(total)
            attended = (acc / total).astype(bf16)
            for member in range(GROUP):
                head = j * GROUP + member
                out_ref[0, b * blk : (b + 1) * blk, head * HEAD_DIM : (head + 1) * HEAD_DIM] = (
                    attended[member * blk : (member + 1) * blk, HEAD_DIM:]
                )


def unpack_second(pack_ref, out_w_ref, gate_w_ref, up_w_ref, down_w_ref):
    ctx = pack_ref.shape[0]
    f_cols, o_cols = FF // ctx, MODEL_WIDTH // ctx
    for c in range(ctx):
        here = slice(c * f_cols, (c + 1) * f_cols)
        gate_w_ref[here, :] = pack_ref[c, :f_cols, :MODEL_WIDTH]
        up_w_ref[here, :] = pack_ref[c, f_cols : 2 * f_cols, :MODEL_WIDTH]

    def natural(base, size):
        pieces = [pack_ref[c, base : base + o_cols, :size].astype(f32) for c in range(ctx)]
        return jnp.concatenate(pieces, axis=0).astype(bf16)

    base = 2 * f_cols
    out_w_ref[...] = natural(base, MODEL_WIDTH)
    for begin in range(0, FF, LANES):
        base += o_cols
        size = min(LANES, FF - begin)
        down_w_ref[:, begin : begin + size] = natural(base, size)


def middle_kernel(
    x_ref,
    attn_ref,
    cot_ref,
    gain_ref,
    pack_ref,
    block_ref,
    normed_ref,
    hidden_ref,
    dgate_ref,
    dup_ref,
    dattn_ref,
    dout_ref,
    dresid_ref,
    gain_grad_ref,
    out_w_ref,
    gate_w_ref,
    up_w_ref,
    down_w_ref,
):
    @pl.when(pl.program_id(0) == 0)
    def _():
        unpack_second(pack_ref, out_w_ref, gate_w_ref, up_w_ref, down_w_ref)

    attn = attn_ref[0]
    cot = cot_ref[0]
    resid = x_ref[0].astype(f32) + dot_nt(attn, out_w_ref[...])
    inv = lax.rsqrt(jnp.mean(resid * resid, axis=-1, keepdims=True) + NORM_EPS)
    hat = resid * inv
    gain = gain_ref[...]
    normed = (hat * gain).astype(bf16)
    normed_ref[0] = normed
    block = resid
    dnormed = jnp.zeros(resid.shape, f32)
    for begin in range(0, FF, FF_CHUNK):
        span = slice(begin, min(begin + FF_CHUNK, FF))
        gate = dot_nt(normed, gate_w_ref[span, :])
        up = dot_nt(normed, up_w_ref[span, :])
        sig = 1.0 / (1.0 + jnp.exp(-gate))
        act = gate * sig
        hidden = (act * up).astype(bf16)
        hidden_ref[0, :, span] = hidden
        block = block + dot_nt(hidden, down_w_ref[:, span])
        dhidden = dot_nn(cot, down_w_ref[:, span])
        dgate = (dhidden * up * (sig * (1.0 + gate * (1.0 - sig)))).astype(bf16)
        dup = (dhidden * act).astype(bf16)
        dgate_ref[0, :, span] = dgate
        dup_ref[0, :, span] = dup
        dnormed = dnormed + dot_nn(dgate, gate_w_ref[span, :]) + dot_nn(dup, up_w_ref[span, :])
    block_ref[0] = block
    gain_grad_ref[0] = jnp.sum(dnormed * hat, axis=0, keepdims=True)
    scaled = dnormed * gain
    dresid = cot.astype(f32) + inv * (scaled - hat * jnp.mean(scaled * hat, axis=-1, keepdims=True))
    dresid_ref[0] = dresid
    dattn = dresid.astype(bf16)
    dattn_ref[0] = dattn
    dout_ref[0] = dot_nn(dattn, out_w_ref[...]).astype(bf16)


def attend_back_kernel(chunks, first, blocks_ref, query_ref, *refs):
    s = first + pl.program_id(0)
    kv_refs = refs[:chunks]
    out_ref, dout_ref, log_ref, cos_ref, sin_ref, dquery_ref = refs[chunks : chunks + 6]
    dkv_refs = refs[chunks + 6 : 2 * chunks + 6]
    sorted_ref, both_ref, flip_ref, delta_ref, dq_ref, dkv_t_ref, dkv_s_ref = refs[2 * chunks + 6 :]
    per, rows = query_ref.shape[1], query_ref.shape[3]
    blk = rows // GROUP
    length = sorted_ref.shape[0]
    sort_blocks(blocks_ref, s, kv_refs, sorted_ref, blk)
    dkv_t_ref[...] = jnp.zeros(dkv_t_ref.shape, f32)
    for b in range(per):
        place = blocks_ref[s, b]
        full = (place * blk) // TILE
        span = slice(b * blk, (b + 1) * blk)
        for j in range(KV_HEADS):
            both_ref[j, :rows] = query_ref[0, b, j]
            for member in range(GROUP):
                head = j * GROUP + member
                lanes = slice(head * HEAD_DIM, (head + 1) * HEAD_DIM)
                dout = dout_ref[0, span, lanes]
                delta = jnp.sum(
                    dout.astype(f32) * out_ref[0, span, lanes].astype(f32), axis=-1, keepdims=True
                )
                here = slice(member * blk, (member + 1) * blk)
                delta_ref[j, here] = jnp.broadcast_to(delta, (blk, PACK))
                both_ref[j, rows + member * blk : rows + (member + 1) * blk] = jnp.concatenate(
                    [jnp.zeros_like(dout), dout], axis=1
                )
            flip_ref[j] = both_ref[j].T
        dq_ref[...] = jnp.zeros(dq_ref.shape, f32)

        def tile_step(t, masked):
            begin = pl.multiple_of(t * TILE, TILE)
            kvs = [
                sorted_ref[pl.ds(begin, TILE), j * PACK : (j + 1) * PACK] for j in range(KV_HEADS)
            ]
            joined = [dot_nt(both_ref[j], kvs[j]) for j in range(KV_HEADS)]
            dscores, joints = [], []
            for j in range(KV_HEADS):
                score, dprob = joined[j][:rows], joined[j][rows:]
                log_total = log_ref[0, b, j]
                delta = delta_ref[j]
                prob = jnp.concatenate(
                    [jnp.exp(score[:, :PACK] - log_total), jnp.exp(score[:, PACK:] - log_total)],
                    axis=1,
                )
                if masked:
                    prob = jnp.where(allowed_mask(place, begin, blk, rows), prob, 0.0)
                dscore = prob * jnp.concatenate(
                    [dprob[:, :PACK] - delta, dprob[:, PACK:] - delta], axis=1
                )
                dscores.append(dscore.astype(bf16))
                joints.append(jnp.concatenate([dscores[j], prob.astype(bf16)], axis=0))
            dqs = [dot_nn(dscores[j], kvs[j]) for j in range(KV_HEADS)]
            dkvs = [dot_nn(flip_ref[j], joints[j]) for j in range(KV_HEADS)]
            for j in range(KV_HEADS):
                dq_ref[j] += dqs[j]
                dkv_t_ref[j * PACK : (j + 1) * PACK, pl.ds(begin, TILE)] += dkvs[j]

        @pl.loop(0, full)
        def _(t):
            tile_step(t, False)

        tile_step(full, True)
        cosine, sine = cos_ref[0, span, :], sin_ref[0, span, :]
        for j in range(KV_HEADS):
            for member in range(GROUP):
                head = j * GROUP + member
                grad = dq_ref[j, member * blk : (member + 1) * blk]
                back = (grad * cosine + turned(grad, False) * sine) * (HEAD_DIM**-0.5)
                dquery_ref[0, span, head * HEAD_DIM : (head + 1) * HEAD_DIM] = back[
                    :, :HEAD_DIM
                ].astype(bf16)
    for begin in range(0, length, TILE):
        dkv_s_ref[begin : begin + TILE, :] = dkv_t_ref[:, begin : begin + TILE].T.astype(bf16)
    for g, dkv_ref in enumerate(dkv_refs):
        for b in range(per):
            place = pl.multiple_of(blocks_ref[s, g * per + b] * blk, blk)
            dkv_ref[0, b * blk : (b + 1) * blk, :] = dkv_s_ref[pl.ds(place, blk), :]


def final_kernel(
    x_ref,
    gain_ref,
    dquery_ref,
    dkv_ref,
    dresid_ref,
    cos_ref,
    sin_ref,
    weight_ref,
    dinput_ref,
    dall_ref,
    gain_grad_ref,
):
    rows = x_ref.shape[1]
    cosine, sine = cos_ref[0], sin_ref[0]
    low_half = lanes_of((rows, PACK)) < HEAD_DIM
    for j in range(KV_HEADS):
        part = dkv_ref[0, :, j * PACK : (j + 1) * PACK].astype(f32)
        back = part * cosine + turned(part, False) * sine
        dall_ref[0, :, j * PACK : (j + 1) * PACK] = jnp.where(low_half, back, part).astype(bf16)
    used = KV_PACKED + QUERY_WIDTH
    dall_ref[0, :, KV_PACKED:used] = dquery_ref[0]
    dall_ref[0, :, used:] = jnp.zeros((rows, INNER - used), bf16)
    dnormed = dot_nn(dall_ref[0, :, :used], weight_ref[...])
    x = x_ref[0].astype(f32)
    inv = lax.rsqrt(jnp.mean(x * x, axis=-1, keepdims=True) + NORM_EPS)
    hat = x * inv
    gain_grad_ref[0] = jnp.sum(dnormed * hat, axis=0, keepdims=True)
    scaled = dnormed * gain_ref[...]
    dinput_ref[0] = dresid_ref[0] + inv * (
        scaled - hat * jnp.mean(scaled * hat, axis=-1, keepdims=True)
    )


def natural_pieces(where_ref, own_ref, other_ref, begin, size):
    zero = where_ref[0] == 0
    pieces = []
    for g in range(own_ref.shape[0]):
        slot = where_ref[1 + g]
        mine = own_ref[slot, begin : begin + size, :].astype(f32)
        theirs = other_ref[slot, begin : begin + size, :].astype(f32)
        pieces.append(jnp.where(zero, mine, theirs))
        pieces.append(jnp.where(zero, theirs, mine))
    return jnp.concatenate(pieces, axis=0).astype(bf16)


def unpack_first_kernel(q_cols, kv_cols, where_ref, own_ref, other_ref, inward_ref):
    width = inward_ref.shape[1]
    query = natural_pieces(where_ref, own_ref, other_ref, 0, q_cols)
    inward_ref[KV_PACKED:, :] = query[:, :width]
    for offset in range(2):
        part = natural_pieces(where_ref, own_ref, other_ref, q_cols + offset * kv_cols, kv_cols)
        for j in range(KV_HEADS):
            begin = j * PACK + offset * HEAD_DIM
            inward_ref[begin : begin + HEAD_DIM, :] = part[
                j * HEAD_DIM : (j + 1) * HEAD_DIM, :width
            ]


def pack_rows(where_ref, own_ref, other_ref, source, begin, size):
    zero = where_ref[0] == 0
    lanes = source.shape[1]
    for g in range(own_ref.shape[0]):
        slot = where_ref[1 + g]
        even = source[2 * g * size : (2 * g + 1) * size]
        odd = source[(2 * g + 1) * size : (2 * g + 2) * size]
        own_ref[slot, begin : begin + size, :lanes] = jnp.where(zero, even, odd).astype(bf16)
        other_ref[slot, begin : begin + size, :lanes] = jnp.where(zero, odd, even).astype(bf16)


def pack_first_kernel(q_cols, kv_cols, parts, where_ref, normed_ref, *refs):
    dall_refs, (gains_ref, own_ref, other_ref, grad_ref) = refs[:parts], refs[parts:]
    width = grad_ref.shape[1]
    seq = 0
    for dall_ref in dall_refs:
        for s in range(dall_ref.shape[0]):
            term = dot_nn(dall_ref[s].T, normed_ref[seq])
            grad_ref[...] = term if seq == 0 else grad_ref[...] + term
            seq += 1
    query = grad_ref[KV_PACKED : KV_PACKED + QUERY_WIDTH, :]
    pack_rows(where_ref, own_ref, other_ref, query, 0, q_cols)
    for offset in range(2):
        part = jnp.concatenate(
            [
                grad_ref[j * PACK + offset * HEAD_DIM : j * PACK + (offset + 1) * HEAD_DIM, :]
                for j in range(KV_HEADS)
            ],
            axis=0,
        )
        pack_rows(where_ref, own_ref, other_ref, part, q_cols + offset * kv_cols, kv_cols)
    begin = q_cols + 2 * kv_cols
    for g in range(own_ref.shape[0]):
        own_ref[g, begin : begin + 2, :width] = gains_ref[...].astype(bf16)
        other_ref[g, begin : begin + 2, :width] = gains_ref[...].astype(bf16)


def pack_second_kernel(out_g_ref, gate_g_ref, up_g_ref, down_g_ref, pack_ref):
    ctx = pack_ref.shape[0]
    f_cols, o_cols = FF // ctx, MODEL_WIDTH // ctx
    for c in range(ctx):
        here = slice(c * f_cols, (c + 1) * f_cols)
        pack_ref[c, :f_cols, :MODEL_WIDTH] = gate_g_ref[here, :]
        pack_ref[c, f_cols : 2 * f_cols, :MODEL_WIDTH] = up_g_ref[here, :]
    base = 2 * f_cols
    parts = [out_g_ref[...]]
    parts += [down_g_ref[:, begin : min(begin + LANES, FF)] for begin in range(0, FF, LANES)]
    for part in parts:
        wide = part.astype(f32)
        for c in range(ctx):
            piece = wide[c * o_cols : (c + 1) * o_cols].astype(bf16)
            pack_ref[c, base : base + o_cols, : part.shape[1]] = piece
        base += o_cols


def one(shape):
    rest = tuple(shape[1:])
    return pl.BlockSpec((1,) + rest, lambda s, *_: (s,) + (0,) * len(rest))


def whole(shape):
    return pl.BlockSpec(tuple(shape), lambda s, *_: (0,) * len(shape))


def anywhere(shape):
    return pl.BlockSpec(memory_space=pl.ANY)


def since(first):
    def make(shape):
        rest = tuple(shape[1:])
        return pl.BlockSpec((1,) + rest, lambda s, *_: (first + s,) + (0,) * len(rest))

    return make


def call(kernel, seqs, inputs, outputs, scalars=(), scratch=(), us=1.0, after=()):
    begin = len(scalars) + len(inputs)

    def body_of(*refs):
        kernel(*refs[:begin], *refs[begin + len(after) :])

    in_specs = [make(array.shape) for make, array in inputs]
    in_specs += [anywhere(array.shape) for array in after]
    out_specs = [make(shape) for make, shape, _ in outputs]
    moved = sum(array.size * array.dtype.itemsize for _, array in inputs)
    for _, shape, kind in outputs:
        count = 1
        for size in shape:
            count *= size
        moved += count * jnp.dtype(kind).itemsize
    return pl.pallas_call(
        body_of,
        grid_spec=pltpu.PrefetchScalarGridSpec(
            num_scalar_prefetch=len(scalars),
            grid=(seqs,),
            in_specs=in_specs,
            out_specs=out_specs,
            scratch_shapes=list(scratch),
        ),
        out_shape=[jax.ShapeDtypeStruct(shape, kind) for _, shape, kind in outputs],
        compiler_params=pltpu.CompilerParams(vmem_limit_bytes=VMEM_BYTES),
        cost_estimate=pl.CostEstimate(
            flops=int(us * FLOPS_PER_US), bytes_accessed=int(moved), transcendentals=0
        ),
    )(*scalars, *[array for _, array in inputs], *after)


def join_kernel(*refs):
    del refs


def join(arrays, *after):
    return pl.pallas_call(
        join_kernel,
        in_specs=[pl.BlockSpec(memory_space=pl.ANY)] * (len(arrays) + len(after)),
        out_specs=[pl.BlockSpec(memory_space=pl.ANY)] * len(arrays),
        out_shape=[jax.ShapeDtypeStruct(array.shape, array.dtype) for array in arrays],
        input_output_aliases={i: i for i in range(len(arrays))},
    )(*arrays, *after)


def adam_update(weight, first, second, grad, rate, decay):
    first_next = BETA_ONE * first + (1.0 - BETA_ONE) * grad
    second_next = BETA_TWO * second + (1.0 - BETA_TWO) * grad * grad
    first_fix = first_next / (1.0 - BETA_ONE**STEP)
    second_fix = second_next / (1.0 - BETA_TWO**STEP)
    update = first_fix / (jnp.sqrt(second_fix) + ADAM_EPS) + decay * weight
    return (weight - rate * update, first_next, second_next)


def ring_of(chips):
    if chips == 8:
        return [0, 2, 4, 6, 7, 5, 3, 1]
    return list(range(chips))


def ring_pairs(chips, step):
    ring = ring_of(chips)
    return [
        (2 * ring[p] + core, 2 * ring[(p + step) % chips] + core)
        for p in range(chips)
        for core in range(2)
    ]


def ring_gather(mine, flip, pins=None, trace=None):
    chips = lax.axis_size("ctx") // 2
    steps = (chips // 2, (chips - 1) // 2)
    if flip:
        steps = steps[::-1]
    result = [mine] * chips
    ahead = behind = mine
    for t in range(1, max(steps) + 1):
        if t <= steps[0]:
            ahead = lax.ppermute(ahead, "ctx", ring_pairs(chips, 1))
            result[-t % chips] = ahead
        if t <= steps[1]:
            behind = lax.ppermute(behind, "ctx", ring_pairs(chips, -1))
            result[t] = behind
        if pins and t in pins and t <= min(steps):
            ahead, behind = join([ahead, behind], *pins[t])
            result[-t % chips], result[t] = ahead, behind
        if trace is not None:
            trace.append([ahead, behind])
    return result


def plus(*terms):
    total = terms[0].astype(f32)
    for term in terms[1:]:
        total = total + term.astype(f32)
    return total


def ring_scatter(terms, flip, pin=()):
    chips = lax.axis_size("ctx") // 2
    steps = (chips // 2, (chips - 1) // 2)
    if flip:
        steps = steps[::-1]
    moving = [terms[steps[0]]().astype(bf16), terms[-steps[1] % chips]().astype(bf16)]
    if pin:
        moving = list(join(moving, *pin))
    trace = []
    for t in range(max(steps)):
        for way in range(2):
            left = steps[way] - 1 - t
            if left < 0:
                continue
            sign = 1 - 2 * way
            got = lax.ppermute(moving[way], "ctx", ring_pairs(chips, sign))
            if left:
                got = plus(got, terms[sign * left % chips]()).astype(bf16)
            moving[way] = got
        trace.append(list(moving))
    return plus(terms[0](), moving[0], moving[1]), trace


def rows_gather(part):
    if lax.axis_size("fsdp") != 2:
        return lax.all_gather(part, "fsdp", axis=1, tiled=True)
    first = lax.axis_index("fsdp") == 0
    got = lax.ppermute(part, "fsdp", [(0, 1), (1, 0)])
    return jnp.concatenate([jnp.where(first, part, got), jnp.where(first, got, part)], axis=1)


def rows_scatter(grads):
    fsdp = lax.axis_size("fsdp")
    if fsdp != 2:
        return lax.psum_scatter(
            grads.astype(bf16), "fsdp", scatter_dimension=1, tiled=True
        ).astype(f32)
    first = lax.axis_index("fsdp") == 0
    half = grads.shape[1] // 2
    low, high = grads[:, :half], grads[:, half:]
    got = lax.ppermute(jnp.where(first, high, low).astype(bf16), "fsdp", [(0, 1), (1, 0)])
    return jnp.where(first, low, high) + got.astype(f32)


def widen(array):
    return jnp.pad(array, ((0, 0), (0, LANES - array.shape[1])))


def weight_grad(left, right):
    return lax.dot_general(left, right, (((0, 1), (0, 1)), ((), ())), preferred_element_type=f32)


def body(
    tokens,
    cotangent,
    pair_order,
    query_weight,
    key_master_weight,
    value_master_weight,
    output_weight,
    gate_weight,
    up_weight,
    down_weight,
    norm_gains,
    query_first,
    key_first_moment,
    value_first_moment,
    output_first,
    gate_first,
    up_first,
    down_first,
    gains_first,
    query_second,
    key_second_moment,
    value_second_moment,
    output_second,
    gate_second,
    up_second,
    down_second,
    gains_second,
):
    masters = (
        query_weight,
        key_master_weight,
        value_master_weight,
        output_weight,
        gate_weight,
        up_weight,
        down_weight,
    )
    ctx = lax.axis_size("ctx")
    index = lax.axis_index("ctx")
    chunks = ctx // 2
    core = index % 2
    seqs = tokens.shape[0] // 2
    part_rows = tokens.shape[1]
    rows = 2 * part_rows
    blk = part_rows // 2
    per = rows // blk
    length = part_rows * ctx
    mine, other = core * seqs, (1 - core) * seqs
    partners = [(i, i ^ 1) for i in range(ctx)]

    def take(array):
        own = lax.dynamic_slice_in_dim(array, mine, seqs, 0)
        got = lax.ppermute(lax.dynamic_slice_in_dim(array, other, seqs, 0), "ctx", partners)
        return jnp.concatenate([own, got], axis=1)

    def give(array):
        got = lax.ppermute(array[:, part_rows:], "ctx", partners)
        result = jnp.zeros((2 * seqs, part_rows) + array.shape[2:], array.dtype)
        result = lax.dynamic_update_slice_in_dim(result, array[:, :part_rows], mine, 0)
        return lax.dynamic_update_slice_in_dim(result, got, other, 0)

    ring = ring_of(chunks)
    position_of = [ring.index(g) for g in range(chunks)]
    position = jnp.array(position_of, jnp.int32)[index // 2]
    slots = (jnp.array(position_of, jnp.int32) - position) % chunks
    where = jnp.concatenate([core[None].astype(jnp.int32), slots])
    reached = jnp.array(ring, jnp.int32)[(position + jnp.arange(chunks)) % chunks]

    turned_low = [matrix.astype(bf16).T for matrix in masters]
    q_cols, kv_cols = QUERY_WIDTH // ctx, KEY_WIDTH // ctx
    o_cols, f_cols = MODEL_WIDTH // ctx, FF // ctx

    def both_packs(pack, flip):
        stack = jnp.stack(ring_gather(pack, flip), axis=0)
        return stack, lax.ppermute(stack, "ctx", partners)

    first_part = rows_gather(jnp.concatenate(turned_low[:3] + [norm_gains.astype(bf16).T], axis=0))
    first_used = first_part.shape[0]
    first_part = jnp.pad(first_part, ((0, -first_used % 16), (0, 0)))
    gains = first_part[q_cols + 2 * kv_cols : first_used].astype(f32)
    gain_one, gain_two = gains[0:1], gains[1:2]
    first_own, first_other = both_packs(widen(first_part), False)
    (inward,) = call(
        functools.partial(unpack_first_kernel, q_cols, kv_cols),
        1,
        [(whole, first_own), (whole, first_other)],
        [(whole, (KV_PACKED + QUERY_WIDTH, MODEL_WIDTH), bf16)],
        scalars=(where,),
        us=3.3,
    )
    down_part = rows_gather(turned_low[6])
    second_part = jnp.concatenate(
        [widen(rows_gather(jnp.concatenate(turned_low[4:6] + turned_low[3:4], axis=0)))]
        + [widen(down_part[:, begin : begin + LANES]) for begin in range(0, FF, LANES)],
        axis=0,
    )
    (second_part,) = join([second_part], first_other)
    second_all = lax.all_gather(second_part, "ctx", axis=0, tiled=False)

    x = take(tokens)
    cot = take(cotangent)
    order = lax.dynamic_slice_in_dim(pair_order, mine, seqs, 0)
    ends = jnp.stack([order, 2 * ctx - 1 - order], axis=2).reshape(seqs, chunks, 2, 2)
    ends = jnp.where(core == 0, ends, ends[:, :, ::-1])
    ends = ends.reshape(seqs, chunks, per)
    blocks = jnp.take(ends, reached, axis=1).reshape(seqs, chunks * per)
    own = blocks[:, :per]
    places = (own[:, :, None] * blk + jnp.arange(blk, dtype=jnp.int32)).reshape(seqs, rows)
    half_dim = HEAD_DIM // 2
    inverse = ROPE_BASE ** (-jnp.arange(half_dim, dtype=f32) * 2.0 / HEAD_DIM)
    angle = places.astype(f32)[..., None] * inverse
    cosine = jnp.tile(jnp.cos(angle), (1, 1, PACK // half_dim))
    sine = jnp.tile(jnp.sin(angle), (1, 1, PACK // half_dim))

    wide = (seqs, rows, MODEL_WIDTH)
    heads = (seqs, per, KV_HEADS, GROUP * blk, PACK)
    normed_one, query, kv = call(
        project_kernel,
        seqs,
        [(one, x), (whole, gain_one), (whole, inward), (one, cosine), (one, sine)],
        [(one, wide, bf16), (one, heads, bf16), (one, (seqs, rows, KV_PACKED), bf16)],
        us=6.2,
    )
    load = length / 2048
    tile_rows = (KV_HEADS, GROUP * blk, PACK)
    kv_trace = []
    kv_all = ring_gather(kv, False, trace=kv_trace)
    attn, logs = call(
        functools.partial(attend_kernel, chunks),
        seqs,
        [(one, query)] + [(one, chunk) for chunk in kv_all],
        [(one, wide, bf16), (one, heads, f32)],
        scalars=(blocks,),
        scratch=[
            pltpu.VMEM((length, KV_PACKED), bf16),
            pltpu.VMEM((KV_HEADS, length // TILE, GROUP * blk, TILE), f32),
            pltpu.VMEM(tile_rows, f32),
            pltpu.VMEM(tile_rows, f32),
        ],
        us=11.0 * seqs * load,
    )
    ff_wide = (seqs, rows, FF)
    (
        block_local,
        normed_two,
        hidden,
        dgate,
        dup,
        dattn,
        dout,
        dresid,
        gain_two_grad,
    ) = call(
        middle_kernel,
        seqs,
        [
            (one, x),
            (one, attn),
            (one, cot),
            (whole, gain_two),
            (whole, second_all),
        ],
        [
            (one, wide, f32),
            (one, wide, bf16),
            (one, ff_wide, bf16),
            (one, ff_wide, bf16),
            (one, ff_wide, bf16),
            (one, wide, bf16),
            (one, wide, bf16),
            (one, wide, f32),
            (one, (seqs, 1, MODEL_WIDTH), f32),
        ],
        scratch=[
            pltpu.VMEM((MODEL_WIDTH, QUERY_WIDTH), bf16),
            pltpu.VMEM((FF, MODEL_WIDTH), bf16),
            pltpu.VMEM((FF, MODEL_WIDTH), bf16),
            pltpu.VMEM((MODEL_WIDTH, FF), bf16),
        ],
        us=26.0,
    )
    block_output = give(block_local)
    def reduced_packs(own_packs, other_packs, flip):
        got = lax.ppermute(other_packs, "ctx", partners)
        terms = [lambda k=k: plus(own_packs[k], got[k]) for k in range(chunks)]
        return ring_scatter(terms, flip)

    def outer_sums(earlier):
        behind = traces[-1]
        dattn_, dgate_ = join([dattn, dgate], earlier)
        (dup_,) = join([dup], *behind[0])
        (hidden_,) = join([hidden], *behind[1])
        (second_pack,) = call(
            pack_second_kernel,
            1,
            [
                (whole, weight_grad(dattn_, attn).astype(bf16)),
                (whole, weight_grad(dgate_, normed_two).astype(bf16)),
                (whole, weight_grad(dup_, normed_two).astype(bf16)),
                (whole, weight_grad(cot, hidden_).astype(bf16)),
            ],
            [(whole, second_all.shape, bf16)],
            us=6.3,
            after=behind[2],
        )
        second_sum = lax.psum_scatter(second_pack, "ctx", scatter_dimension=0, tiled=False)
        base = 2 * f_cols + o_cols
        down_sum = rows_scatter(
            jnp.concatenate(
                [
                    second_sum[base + i * o_cols : base + (i + 1) * o_cols, : min(LANES, FF - begin)]
                    for i, begin in enumerate(range(0, FF, LANES))
                ],
                axis=1,
            ).astype(f32)
        )
        second_sum = rows_scatter(second_sum[:base, :MODEL_WIDTH].astype(f32))
        outer = (second_sum[2 * f_cols :], second_sum[:f_cols], second_sum[f_cols : 2 * f_cols])
        return second_pack, outer + (down_sum,)

    dinputs, dalls, gain_one_grads, traces = [], [], [], []
    last = seqs - 1
    for first, count in ((0, last), (last, 1)):
        these = since(first)
        waits = []
        if first == last:
            second_pack, outer_reduced = outer_sums(dquery)
            waits = [second_pack]
        dquery, *dkv = call(
            functools.partial(attend_back_kernel, chunks, first),
            count,
            [(these, query)]
            + [(these, chunk) for chunk in kv_all]
            + [(these, array) for array in (attn, dout, logs, cosine, sine)],
            [(one, (count,) + wide[1:], bf16)] + [(one, (count, rows, KV_PACKED), bf16)] * chunks,
            scalars=(blocks,),
            scratch=[
                pltpu.VMEM((length, KV_PACKED), bf16),
                pltpu.VMEM((KV_HEADS, 2 * GROUP * blk, PACK), bf16),
                pltpu.VMEM((KV_HEADS, PACK, 2 * GROUP * blk), bf16),
                pltpu.VMEM(tile_rows, f32),
                pltpu.VMEM(tile_rows, f32),
                pltpu.VMEM((KV_PACKED, length), f32),
                pltpu.VMEM((length, KV_PACKED), bf16),
            ],
            us=17.0 * count * load,
            after=waits,
        )
        dkv_own, trace = ring_scatter(
            [lambda k=k, dkv=dkv: dkv[k] for k in range(chunks)],
            first > 0,
            traces[-1][-1] if traces else (),
        )
        traces.append(trace)
        dinput, dall, gain_one_grad = call(
            final_kernel,
            count,
            [
                (these, x),
                (whole, gain_one),
                (one, dquery),
                (one, dkv_own),
                (these, dresid),
                (these, cosine),
                (these, sine),
                (whole, inward),
            ],
            [
                (one, (count,) + wide[1:], f32),
                (one, (count, rows, INNER), bf16),
                (one, (count, 1, MODEL_WIDTH), f32),
            ],
            us=2.0 * count,
        )
        dinputs.append(dinput)
        dalls.append(dall)
        gain_one_grads.append(jnp.sum(gain_one_grad, axis=0))
    input_gradient = give(jnp.concatenate(dinputs, axis=0))
    gains_grad = jnp.concatenate([sum(gain_one_grads), jnp.sum(gain_two_grad, axis=0)], axis=0)
    packs = (chunks, first_part.shape[0], LANES)
    first_packs = call(
        functools.partial(pack_first_kernel, q_cols, kv_cols, len(dalls)),
        1,
        [(whole, normed_one)] + [(whole, dall) for dall in dalls] + [(whole, gains_grad)],
        [(whole, packs, bf16), (whole, packs, bf16)],
        scalars=(where,),
        scratch=[pltpu.VMEM((INNER, MODEL_WIDTH), f32)],
        us=3.5,
    )
    first_sum = rows_scatter(reduced_packs(*first_packs, False)[0][:, :MODEL_WIDTH])
    reduced = (
        first_sum[:q_cols],
        first_sum[q_cols : q_cols + kv_cols],
        first_sum[q_cols + kv_cols : q_cols + 2 * kv_cols],
        *outer_reduced,
    )
    gains_total = first_sum[q_cols + 2 * kv_cols : first_used].T
    rates = (
        (MODEL_WIDTH // 4) ** (-0.5),
        MODEL_WIDTH ** (-0.5),
        MODEL_WIDTH ** (-0.5),
        (MODEL_WIDTH // 32) ** (-0.5),
        MODEL_WIDTH ** (-0.5),
        MODEL_WIDTH ** (-0.5),
        (FF // 2) ** (-0.5),
    )
    firsts = (
        query_first,
        key_first_moment,
        value_first_moment,
        output_first,
        gate_first,
        up_first,
        down_first,
    )
    seconds = (
        query_second,
        key_second_moment,
        value_second_moment,
        output_second,
        gate_second,
        up_second,
        down_second,
    )
    results = [
        adam_update(
            masters[member], firsts[member], seconds[member], reduced[member].T, rates[member], DECAY
        )
        for member in range(7)
    ]
    results.append(adam_update(norm_gains, gains_first, gains_second, gains_total, GAIN_RATE, 0.0))
    new_weights = [result[0] for result in results]
    new_firsts = [result[1] for result in results]
    new_seconds = [result[2] for result in results]
    return tuple([block_output, input_gradient] + new_weights + new_firsts + new_seconds)


def solution(mesh):
    sequences = P("fsdp", "ctx", None)
    matrix = P("fsdp", "ctx")
    gains = P("fsdp", None)
    state = (matrix,) * 7 + (gains,)
    return jax.shard_map(
        body,
        mesh=mesh,
        in_specs=(sequences, sequences, P("fsdp", None)) + state * 3,
        out_specs=(sequences, sequences) + state * 3,
        check_vma=False,
    )
```

```python
import functools

import jax
import jax.numpy as jnp
from jax import lax
from jax.experimental import pallas as pl
from jax.experimental.pallas import tpu as pltpu
from jax.sharding import PartitionSpec as P

MODEL_WIDTH = 576
FF = 1536
HEADS = 9
KV_HEADS = 3
HEAD_DIM = 64
STEP = 10
GROUP = HEADS // KV_HEADS
KEY_WIDTH = KV_HEADS * HEAD_DIM
QUERY_WIDTH = HEADS * HEAD_DIM
PACK = 2 * HEAD_DIM
KV_PACKED = KV_HEADS * PACK
TILE = 256
FF_CHUNK = 640
LANES = 640
INNER = 1024
REST = FF // 2 - LANES

NORM_EPS = 1e-05
ROPE_BASE = 100000.0
BETA_ONE = 0.9
BETA_TWO = 0.95
ADAM_EPS = 1e-08
DECAY = 0.1
GAIN_RATE = 0.5
MASKED = -1e30
FLOPS_PER_US = 1153.5e6
VMEM_BYTES = 56 * 1024 * 1024

f32 = jnp.float32
bf16 = jnp.bfloat16


def dot_nt(a, b):
    return lax.dot_general(a, b, (((1,), (1,)), ((), ())), preferred_element_type=f32)


def dot_nn(a, b):
    return lax.dot_general(a, b, (((1,), (0,)), ((), ())), preferred_element_type=f32)


def lanes_of(shape):
    return lax.broadcasted_iota(jnp.int32, shape, len(shape) - 1)


def turned(v, first):
    lane = lanes_of(v.shape) % HEAD_DIM
    ahead = pltpu.roll(v, PACK - HEAD_DIM // 2, 1)
    behind = pltpu.roll(v, HEAD_DIM // 2, 1)
    if first:
        return jnp.where(lane < HEAD_DIM // 2, -ahead, behind)
    return jnp.where(lane < HEAD_DIM // 2, ahead, -behind)


def project_kernel(x_ref, gain_ref, weight_ref, cos_ref, sin_ref, normed_ref, query_ref, kv_ref):
    rows = x_ref.shape[1]
    blk = query_ref.shape[3] // GROUP
    x = x_ref[0].astype(f32)
    inv = lax.rsqrt(jnp.mean(x * x, axis=-1, keepdims=True) + NORM_EPS)
    normed = (x * inv * gain_ref[...]).astype(bf16)
    normed_ref[0] = normed
    raw = dot_nt(normed, weight_ref[...])
    cosine, sine = cos_ref[0], sin_ref[0]
    low_half = lanes_of((rows, PACK)) < HEAD_DIM
    for j in range(KV_HEADS):
        part = raw[:, j * PACK : (j + 1) * PACK]
        spun = part * cosine + turned(part, True) * sine
        kv_ref[0, :, j * PACK : (j + 1) * PACK] = jnp.where(low_half, spun, part).astype(bf16)
    for i in range((HEADS + 1) // 2):
        begin = KV_PACKED + i * PACK
        if 2 * i + 1 < HEADS:
            part = raw[:, begin : begin + PACK]
        else:
            tail = raw[:, begin : begin + HEAD_DIM]
            part = jnp.concatenate([tail, tail], axis=1)
        spun = part * cosine + turned(part, True) * sine
        spun = spun.astype(bf16).astype(f32) * (HEAD_DIM**-0.5)
        pair = [jnp.where(low_half, spun, 0.0)]
        if 2 * i + 1 < HEADS:
            pair.append(jnp.where(low_half, pltpu.roll(spun, HEAD_DIM, 1), 0.0))
        for offset, value in enumerate(pair):
            head = 2 * i + offset
            j, member = head // GROUP, head % GROUP
            value = value.astype(bf16)
            for b in range(rows // blk):
                query_ref[0, b, j, member * blk : (member + 1) * blk, :] = value[
                    b * blk : (b + 1) * blk
                ]


def sort_blocks(blocks_ref, s, kv_refs, sorted_ref, blk):
    per = kv_refs[0].shape[1] // blk
    for g, kv_ref in enumerate(kv_refs):
        for b in range(per):
            place = pl.multiple_of(blocks_ref[s, g * per + b] * blk, blk)
            sorted_ref[pl.ds(place, blk), :] = kv_ref[0, b * blk : (b + 1) * blk, :]


def allowed_mask(place, tile_begin, blk, rows):
    row = lax.broadcasted_iota(jnp.int32, (rows, TILE), 0) % blk
    col = lax.broadcasted_iota(jnp.int32, (rows, TILE), 1)
    return col <= row + (place * blk - tile_begin)


def attend_kernel(chunks, blocks_ref, query_ref, *refs):
    s = pl.program_id(0)
    kv_refs = refs[:chunks]
    out_ref, log_ref, sorted_ref, score_ref, top_ref, acc_ref = refs[chunks:]
    per, rows = query_ref.shape[1], query_ref.shape[3]
    blk = rows // GROUP
    sort_blocks(blocks_ref, s, kv_refs, sorted_ref, blk)
    lane = lanes_of((TILE, PACK))
    for b in range(per):
        place = blocks_ref[s, b]
        full = (place * blk) // TILE

        def score_tile(t, masked):
            begin = pl.multiple_of(t * TILE, TILE)
            for j in range(KV_HEADS):
                kv = sorted_ref[pl.ds(begin, TILE), j * PACK : (j + 1) * PACK]
                score = dot_nt(query_ref[0, b, j], kv)
                if masked:
                    score = jnp.where(allowed_mask(place, begin, blk, rows), score, MASKED)
                score_ref[j, t] = score
                best = jnp.maximum(score[:, :PACK], score[:, PACK:])
                top_ref[j] = jnp.maximum(top_ref[j], best)

        top_ref[...] = jnp.full(top_ref.shape, MASKED, f32)
        acc_ref[...] = jnp.zeros(acc_ref.shape, f32)

        @pl.loop(0, full)
        def _(t):
            score_tile(t, False)

        score_tile(full, True)
        for j in range(KV_HEADS):
            top = jnp.max(top_ref[j], axis=-1, keepdims=True)
            top_ref[j] = jnp.broadcast_to(top, (rows, PACK))

        @pl.loop(0, full + 1)
        def _(t):
            begin = pl.multiple_of(t * TILE, TILE)
            for j in range(KV_HEADS):
                kv = sorted_ref[pl.ds(begin, TILE), j * PACK : (j + 1) * PACK]
                ones_v = jnp.where(lane < HEAD_DIM, jnp.ones((), bf16), kv)
                top = top_ref[j]
                score = score_ref[j, t]
                prob = jnp.concatenate(
                    [jnp.exp(score[:, :PACK] - top), jnp.exp(score[:, PACK:] - top)], axis=1
                )
                acc_ref[j] += dot_nn(prob.astype(bf16), ones_v)

        for j in range(KV_HEADS):
            acc = acc_ref[j]
            low_half = lanes_of(acc.shape) < HEAD_DIM
            total = jnp.where(low_half, acc, pltpu.roll(acc, HEAD_DIM, 1))
            log_ref[0, b, j] = top_ref[j] + jnp.log(total)
            attended = (acc / total).astype(bf16)
            for member in range(GROUP):
                head = j * GROUP + member
                out_ref[0, b * blk : (b + 1) * blk, head * HEAD_DIM : (head + 1) * HEAD_DIM] = (
                    attended[member * blk : (member + 1) * blk, HEAD_DIM:]
                )


def unpack_second(place_ref, part_refs, pack_ref, sems, out_w_ref, gate_w_ref, up_w_ref, down_w_ref):
    ctx = pack_ref.shape[1]
    f_cols, o_cols, half = FF // ctx, MODEL_WIDTH // ctx, MODEL_WIDTH // 2
    copies = []
    for part, part_ref in enumerate(part_refs):
        core = jnp.abs(place_ref[0] - part // 2)
        plane = jnp.abs(place_ref[1] - part % 2)
        for k in range(part_ref.shape[0]):
            index = 2 * place_ref[2 + k] + core
            copies.append(
                pltpu.make_async_copy(
                    part_ref.at[k], pack_ref.at[plane, index], sems.at[part, k]
                )
            )
    for copy in copies:
        copy.start()
    for copy in copies:
        copy.wait()
    for c in range(ctx):
        here = slice(c * f_cols, (c + 1) * f_cols)
        low, high = pack_ref[0, c, :f_cols, :], pack_ref[1, c, :f_cols, :]
        gate_w_ref[here, :] = jnp.concatenate([low[:, :half], high[:, :half]], axis=1)
        up_w_ref[here, :] = jnp.concatenate(
            [low[:, half:MODEL_WIDTH], high[:, half:MODEL_WIDTH]], axis=1
        )

    def natural(plane, base, lanes):
        pieces = [
            pack_ref[plane, c, base : base + o_cols, lanes].astype(f32) for c in range(ctx)
        ]
        return jnp.concatenate(pieces, axis=0).astype(bf16)

    base = f_cols + o_cols
    for plane in range(2):
        begin = plane * (FF // 2)
        down_w_ref[:, begin : begin + LANES] = natural(plane, f_cols, slice(0, LANES))
        down_w_ref[:, begin + LANES : begin + FF // 2] = natural(plane, base, slice(0, REST))
    out_w_ref[...] = jnp.concatenate(
        [natural(plane, base, slice(REST, REST + half)) for plane in range(2)], axis=1
    )


def middle_kernel(
    place_ref,
    x_ref,
    attn_ref,
    cot_ref,
    gain_ref,
    part_a_ref,
    part_b_ref,
    part_c_ref,
    part_d_ref,
    block_ref,
    normed_ref,
    hidden_ref,
    dgate_ref,
    dup_ref,
    dattn_ref,
    dout_ref,
    dresid_ref,
    gain_grad_ref,
    out_w_ref,
    gate_w_ref,
    up_w_ref,
    down_w_ref,
    pack_ref,
    sems,
):
    @pl.when(pl.program_id(0) == 0)
    def _():
        parts = (part_a_ref, part_b_ref, part_c_ref, part_d_ref)
        unpack_second(
            place_ref, parts, pack_ref, sems, out_w_ref, gate_w_ref, up_w_ref, down_w_ref
        )

    attn = attn_ref[0]
    cot = cot_ref[0]
    resid = x_ref[0].astype(f32) + dot_nt(attn, out_w_ref[...])
    inv = lax.rsqrt(jnp.mean(resid * resid, axis=-1, keepdims=True) + NORM_EPS)
    hat = resid * inv
    gain = gain_ref[...]
    normed = (hat * gain).astype(bf16)
    normed_ref[0] = normed
    block = resid
    dnormed = jnp.zeros(resid.shape, f32)
    for begin in range(0, FF, FF_CHUNK):
        span = slice(begin, min(begin + FF_CHUNK, FF))
        gate = dot_nt(normed, gate_w_ref[span, :])
        up = dot_nt(normed, up_w_ref[span, :])
        sig = 1.0 / (1.0 + jnp.exp(-gate))
        act = gate * sig
        hidden = (act * up).astype(bf16)
        hidden_ref[0, :, span] = hidden
        block = block + dot_nt(hidden, down_w_ref[:, span])
        dhidden = dot_nn(cot, down_w_ref[:, span])
        dgate = (dhidden * up * (sig * (1.0 + gate * (1.0 - sig)))).astype(bf16)
        dup = (dhidden * act).astype(bf16)
        dgate_ref[0, :, span] = dgate
        dup_ref[0, :, span] = dup
        dnormed = dnormed + dot_nn(dgate, gate_w_ref[span, :]) + dot_nn(dup, up_w_ref[span, :])
    block_ref[0] = block
    gain_grad_ref[0] = jnp.sum(dnormed * hat, axis=0, keepdims=True)
    scaled = dnormed * gain
    dresid = cot.astype(f32) + inv * (scaled - hat * jnp.mean(scaled * hat, axis=-1, keepdims=True))
    dresid_ref[0] = dresid
    dattn = dresid.astype(bf16)
    dattn_ref[0] = dattn
    dout_ref[0] = dot_nn(dattn, out_w_ref[...]).astype(bf16)


def attend_back_kernel(chunks, first, blocks_ref, query_ref, *refs):
    s = first + pl.program_id(0)
    kv_refs = refs[:chunks]
    out_ref, dout_ref, log_ref, cos_ref, sin_ref, dquery_ref = refs[chunks : chunks + 6]
    dkv_refs = refs[chunks + 6 : 2 * chunks + 6]
    sorted_ref, both_ref, flip_ref, delta_ref, dq_ref, dkv_t_ref, dkv_s_ref = refs[2 * chunks + 6 :]
    per, rows = query_ref.shape[1], query_ref.shape[3]
    blk = rows // GROUP
    length = sorted_ref.shape[0]
    sort_blocks(blocks_ref, s, kv_refs, sorted_ref, blk)
    dkv_t_ref[...] = jnp.zeros(dkv_t_ref.shape, f32)
    for b in range(per):
        place = blocks_ref[s, b]
        full = (place * blk) // TILE
        span = slice(b * blk, (b + 1) * blk)
        for j in range(KV_HEADS):
            both_ref[j, :rows] = query_ref[0, b, j]
            for member in range(GROUP):
                head = j * GROUP + member
                lanes = slice(head * HEAD_DIM, (head + 1) * HEAD_DIM)
                dout = dout_ref[0, span, lanes]
                delta = jnp.sum(
                    dout.astype(f32) * out_ref[0, span, lanes].astype(f32), axis=-1, keepdims=True
                )
                here = slice(member * blk, (member + 1) * blk)
                delta_ref[j, here] = jnp.broadcast_to(delta, (blk, PACK))
                both_ref[j, rows + member * blk : rows + (member + 1) * blk] = jnp.concatenate(
                    [jnp.zeros_like(dout), dout], axis=1
                )
            flip_ref[j] = both_ref[j].T
        dq_ref[...] = jnp.zeros(dq_ref.shape, f32)

        def tile_step(t, masked):
            begin = pl.multiple_of(t * TILE, TILE)
            kvs = [
                sorted_ref[pl.ds(begin, TILE), j * PACK : (j + 1) * PACK] for j in range(KV_HEADS)
            ]
            joined = [dot_nt(both_ref[j], kvs[j]) for j in range(KV_HEADS)]
            dscores, joints = [], []
            for j in range(KV_HEADS):
                score, dprob = joined[j][:rows], joined[j][rows:]
                log_total = log_ref[0, b, j]
                delta = delta_ref[j]
                prob = jnp.concatenate(
                    [jnp.exp(score[:, :PACK] - log_total), jnp.exp(score[:, PACK:] - log_total)],
                    axis=1,
                )
                if masked:
                    prob = jnp.where(allowed_mask(place, begin, blk, rows), prob, 0.0)
                dscore = prob * jnp.concatenate(
                    [dprob[:, :PACK] - delta, dprob[:, PACK:] - delta], axis=1
                )
                dscores.append(dscore.astype(bf16))
                joints.append(jnp.concatenate([dscores[j], prob.astype(bf16)], axis=0))
            dqs = [dot_nn(dscores[j], kvs[j]) for j in range(KV_HEADS)]
            dkvs = [dot_nn(flip_ref[j], joints[j]) for j in range(KV_HEADS)]
            for j in range(KV_HEADS):
                dq_ref[j] += dqs[j]
                dkv_t_ref[j * PACK : (j + 1) * PACK, pl.ds(begin, TILE)] += dkvs[j]

        @pl.loop(0, full)
        def _(t):
            tile_step(t, False)

        tile_step(full, True)
        cosine, sine = cos_ref[0, span, :], sin_ref[0, span, :]
        for j in range(KV_HEADS):
            for member in range(GROUP):
                head = j * GROUP + member
                grad = dq_ref[j, member * blk : (member + 1) * blk]
                back = (grad * cosine + turned(grad, False) * sine) * (HEAD_DIM**-0.5)
                dquery_ref[0, span, head * HEAD_DIM : (head + 1) * HEAD_DIM] = back[
                    :, :HEAD_DIM
                ].astype(bf16)
    for begin in range(0, length, TILE):
        dkv_s_ref[begin : begin + TILE, :] = dkv_t_ref[:, begin : begin + TILE].T.astype(bf16)
    for g, dkv_ref in enumerate(dkv_refs):
        for b in range(per):
            place = pl.multiple_of(blocks_ref[s, g * per + b] * blk, blk)
            dkv_ref[0, b * blk : (b + 1) * blk, :] = dkv_s_ref[pl.ds(place, blk), :]


def final_kernel(
    x_ref,
    gain_ref,
    dquery_ref,
    dkv_ref,
    dresid_ref,
    cos_ref,
    sin_ref,
    weight_ref,
    dinput_ref,
    dall_ref,
    gain_grad_ref,
):
    rows = x_ref.shape[1]
    cosine, sine = cos_ref[0], sin_ref[0]
    low_half = lanes_of((rows, PACK)) < HEAD_DIM
    for j in range(KV_HEADS):
        part = dkv_ref[0, :, j * PACK : (j + 1) * PACK].astype(f32)
        back = part * cosine + turned(part, False) * sine
        dall_ref[0, :, j * PACK : (j + 1) * PACK] = jnp.where(low_half, back, part).astype(bf16)
    used = KV_PACKED + QUERY_WIDTH
    dall_ref[0, :, KV_PACKED:used] = dquery_ref[0]
    dall_ref[0, :, used:] = jnp.zeros((rows, INNER - used), bf16)
    dnormed = dot_nn(dall_ref[0, :, :used], weight_ref[...])
    x = x_ref[0].astype(f32)
    inv = lax.rsqrt(jnp.mean(x * x, axis=-1, keepdims=True) + NORM_EPS)
    hat = x * inv
    gain_grad_ref[0] = jnp.sum(dnormed * hat, axis=0, keepdims=True)
    scaled = dnormed * gain_ref[...]
    dinput_ref[0] = dresid_ref[0] + inv * (
        scaled - hat * jnp.mean(scaled * hat, axis=-1, keepdims=True)
    )


def natural_pieces(where_ref, own_ref, other_ref, begin, size):
    zero = where_ref[0] == 0
    pieces = []
    for g in range(own_ref.shape[0]):
        slot = where_ref[1 + g]
        mine = own_ref[slot, begin : begin + size, :].astype(f32)
        theirs = other_ref[slot, begin : begin + size, :].astype(f32)
        pieces.append(jnp.where(zero, mine, theirs))
        pieces.append(jnp.where(zero, theirs, mine))
    return jnp.concatenate(pieces, axis=0).astype(bf16)


def unpack_first_kernel(q_cols, kv_cols, where_ref, own_ref, other_ref, inward_ref):
    width = inward_ref.shape[1]
    query = natural_pieces(where_ref, own_ref, other_ref, 0, q_cols)
    inward_ref[KV_PACKED:, :] = query[:, :width]
    for offset in range(2):
        part = natural_pieces(where_ref, own_ref, other_ref, q_cols + offset * kv_cols, kv_cols)
        for j in range(KV_HEADS):
            begin = j * PACK + offset * HEAD_DIM
            inward_ref[begin : begin + HEAD_DIM, :] = part[
                j * HEAD_DIM : (j + 1) * HEAD_DIM, :width
            ]


def pack_rows(where_ref, own_ref, other_ref, source, begin, size):
    zero = where_ref[0] == 0
    lanes = source.shape[1]
    for g in range(own_ref.shape[0]):
        slot = where_ref[1 + g]
        even = source[2 * g * size : (2 * g + 1) * size]
        odd = source[(2 * g + 1) * size : (2 * g + 2) * size]
        own_ref[slot, begin : begin + size, :lanes] = jnp.where(zero, even, odd).astype(bf16)
        other_ref[slot, begin : begin + size, :lanes] = jnp.where(zero, odd, even).astype(bf16)


def pack_first_kernel(q_cols, kv_cols, parts, where_ref, normed_ref, *refs):
    dall_refs, (gains_ref, own_ref, other_ref, grad_ref) = refs[:parts], refs[parts:]
    width = grad_ref.shape[1]
    seq = 0
    for dall_ref in dall_refs:
        for s in range(dall_ref.shape[0]):
            term = dot_nn(dall_ref[s].T, normed_ref[seq])
            grad_ref[...] = term if seq == 0 else grad_ref[...] + term
            seq += 1
    query = grad_ref[KV_PACKED : KV_PACKED + QUERY_WIDTH, :]
    pack_rows(where_ref, own_ref, other_ref, query, 0, q_cols)
    for offset in range(2):
        part = jnp.concatenate(
            [
                grad_ref[j * PACK + offset * HEAD_DIM : j * PACK + (offset + 1) * HEAD_DIM, :]
                for j in range(KV_HEADS)
            ],
            axis=0,
        )
        pack_rows(where_ref, own_ref, other_ref, part, q_cols + offset * kv_cols, kv_cols)
    begin = q_cols + 2 * kv_cols
    for g in range(own_ref.shape[0]):
        own_ref[g, begin : begin + 2, :width] = gains_ref[...].astype(bf16)
        other_ref[g, begin : begin + 2, :width] = gains_ref[...].astype(bf16)


def pack_second_kernel(
    place_ref, out_g_ref, gate_g_ref, up_g_ref, down_g_ref, a_ref, b_ref, c_ref, d_ref, pack_ref, sems
):
    ctx = pack_ref.shape[1]
    f_cols, o_cols, half = FF // ctx, MODEL_WIDTH // ctx, MODEL_WIDTH // 2
    base = f_cols + o_cols
    for plane in range(2):
        lanes = slice(plane * half, (plane + 1) * half)
        for c in range(ctx):
            here = slice(c * f_cols, (c + 1) * f_cols)
            pack_ref[plane, c, :f_cols, :MODEL_WIDTH] = jnp.concatenate(
                [gate_g_ref[here, lanes], up_g_ref[here, lanes]], axis=1
            )
        begin = plane * (FF // 2)
        first = down_g_ref[:, begin : begin + LANES].astype(f32)
        rest = down_g_ref[:, begin + LANES : begin + FF // 2]
        second = jnp.concatenate([rest, out_g_ref[:, lanes]], axis=1).astype(f32)
        for c in range(ctx):
            here = slice(c * o_cols, (c + 1) * o_cols)
            pack_ref[plane, c, f_cols:base, :] = first[here].astype(bf16)
            pack_ref[plane, c, base : base + o_cols, : REST + half] = second[here].astype(bf16)
    copies = []
    for part, part_ref in enumerate((a_ref, b_ref, c_ref, d_ref)):
        core = jnp.abs(place_ref[0] - part // 2)
        plane = jnp.abs(place_ref[1] - part % 2)
        for k in range(part_ref.shape[0]):
            index = 2 * place_ref[2 + k] + core
            copies.append(
                pltpu.make_async_copy(
                    pack_ref.at[plane, index], part_ref.at[k], sems.at[part, k]
                )
            )
    for copy in copies:
        copy.start()
    for copy in copies:
        copy.wait()


def one(shape):
    rest = tuple(shape[1:])
    return pl.BlockSpec((1,) + rest, lambda s, *_: (s,) + (0,) * len(rest))


def whole(shape):
    return pl.BlockSpec(tuple(shape), lambda s, *_: (0,) * len(shape))


def anywhere(shape):
    return pl.BlockSpec(memory_space=pl.ANY)


def since(first):
    def make(shape):
        rest = tuple(shape[1:])
        return pl.BlockSpec((1,) + rest, lambda s, *_: (first + s,) + (0,) * len(rest))

    return make


def call(kernel, seqs, inputs, outputs, scalars=(), scratch=(), us=1.0, after=()):
    begin = len(scalars) + len(inputs)

    def body_of(*refs):
        kernel(*refs[:begin], *refs[begin + len(after) :])

    in_specs = [make(array.shape) for make, array in inputs]
    in_specs += [anywhere(array.shape) for array in after]
    out_specs = [make(shape) for make, shape, _ in outputs]
    moved = sum(array.size * array.dtype.itemsize for _, array in inputs)
    for _, shape, kind in outputs:
        count = 1
        for size in shape:
            count *= size
        moved += count * jnp.dtype(kind).itemsize
    return pl.pallas_call(
        body_of,
        grid_spec=pltpu.PrefetchScalarGridSpec(
            num_scalar_prefetch=len(scalars),
            grid=(seqs,),
            in_specs=in_specs,
            out_specs=out_specs,
            scratch_shapes=list(scratch),
        ),
        out_shape=[jax.ShapeDtypeStruct(shape, kind) for _, shape, kind in outputs],
        compiler_params=pltpu.CompilerParams(vmem_limit_bytes=VMEM_BYTES),
        cost_estimate=pl.CostEstimate(
            flops=int(us * FLOPS_PER_US), bytes_accessed=int(moved), transcendentals=0
        ),
    )(*scalars, *[array for _, array in inputs], *after)


def join_kernel(*refs):
    del refs


def join(arrays, *after):
    return pl.pallas_call(
        join_kernel,
        in_specs=[pl.BlockSpec(memory_space=pl.ANY)] * (len(arrays) + len(after)),
        out_specs=[pl.BlockSpec(memory_space=pl.ANY)] * len(arrays),
        out_shape=[jax.ShapeDtypeStruct(array.shape, array.dtype) for array in arrays],
        input_output_aliases={i: i for i in range(len(arrays))},
    )(*arrays, *after)


def adam_update(weight, first, second, grad, rate, decay):
    first_next = BETA_ONE * first + (1.0 - BETA_ONE) * grad
    second_next = BETA_TWO * second + (1.0 - BETA_TWO) * grad * grad
    first_fix = first_next / (1.0 - BETA_ONE**STEP)
    second_fix = second_next / (1.0 - BETA_TWO**STEP)
    update = first_fix / (jnp.sqrt(second_fix) + ADAM_EPS) + decay * weight
    return (weight - rate * update, first_next, second_next)


def ring_of(chips):
    if chips == 8:
        return [0, 2, 4, 6, 7, 5, 3, 1]
    return list(range(chips))


def ring_pairs(chips, step):
    ring = ring_of(chips)
    return [
        (2 * ring[p] + core, 2 * ring[(p + step) % chips] + core)
        for p in range(chips)
        for core in range(2)
    ]


def ring_gather(mine, flip, pins=None, trace=None):
    chips = lax.axis_size("ctx") // 2
    steps = (chips // 2, (chips - 1) // 2)
    if flip:
        steps = steps[::-1]
    result = [mine] * chips
    ahead = behind = mine
    for t in range(1, max(steps) + 1):
        if t <= steps[0]:
            ahead = lax.ppermute(ahead, "ctx", ring_pairs(chips, 1))
            result[-t % chips] = ahead
        if t <= steps[1]:
            behind = lax.ppermute(behind, "ctx", ring_pairs(chips, -1))
            result[t] = behind
        if pins and t in pins and t <= min(steps):
            ahead, behind = join([ahead, behind], *pins[t])
            result[-t % chips], result[t] = ahead, behind
        if trace is not None:
            trace.append([ahead, behind])
    return result


def plus(*terms):
    total = terms[0].astype(f32)
    for term in terms[1:]:
        total = total + term.astype(f32)
    return total


def ring_scatter(terms, flip, pin=()):
    chips = lax.axis_size("ctx") // 2
    steps = (chips // 2, (chips - 1) // 2)
    if flip:
        steps = steps[::-1]
    moving = [terms[steps[0]]().astype(bf16), terms[-steps[1] % chips]().astype(bf16)]
    if pin:
        moving = list(join(moving, *pin))
    trace = []
    for t in range(max(steps)):
        for way in range(2):
            left = steps[way] - 1 - t
            if left < 0:
                continue
            sign = 1 - 2 * way
            got = lax.ppermute(moving[way], "ctx", ring_pairs(chips, sign))
            if left:
                got = plus(got, terms[sign * left % chips]()).astype(bf16)
            moving[way] = got
        trace.append(list(moving))
    return plus(terms[0](), moving[0], moving[1]), trace


def rows_gather(part):
    if lax.axis_size("fsdp") != 2:
        return lax.all_gather(part, "fsdp", axis=1, tiled=True)
    first = lax.axis_index("fsdp") == 0
    got = lax.ppermute(part, "fsdp", [(0, 1), (1, 0)])
    return jnp.concatenate([jnp.where(first, part, got), jnp.where(first, got, part)], axis=1)


def rows_scatter(grads):
    fsdp = lax.axis_size("fsdp")
    if fsdp != 2:
        return lax.psum_scatter(
            grads.astype(bf16), "fsdp", scatter_dimension=1, tiled=True
        ).astype(f32)
    first = lax.axis_index("fsdp") == 0
    half = grads.shape[1] // 2
    low, high = grads[:, :half], grads[:, half:]
    got = lax.ppermute(jnp.where(first, high, low).astype(bf16), "fsdp", [(0, 1), (1, 0)])
    return jnp.where(first, low, high) + got.astype(f32)


def widen(array):
    return jnp.pad(array, ((0, 0), (0, LANES - array.shape[1])))


def weight_grad(left, right):
    return lax.dot_general(left, right, (((0, 1), (0, 1)), ((), ())), preferred_element_type=f32)


def body(
    tokens,
    cotangent,
    pair_order,
    query_weight,
    key_master_weight,
    value_master_weight,
    output_weight,
    gate_weight,
    up_weight,
    down_weight,
    norm_gains,
    query_first,
    key_first_moment,
    value_first_moment,
    output_first,
    gate_first,
    up_first,
    down_first,
    gains_first,
    query_second,
    key_second_moment,
    value_second_moment,
    output_second,
    gate_second,
    up_second,
    down_second,
    gains_second,
):
    masters = (
        query_weight,
        key_master_weight,
        value_master_weight,
        output_weight,
        gate_weight,
        up_weight,
        down_weight,
    )
    ctx = lax.axis_size("ctx")
    index = lax.axis_index("ctx")
    chunks = ctx // 2
    core = index % 2
    seqs = tokens.shape[0] // 2
    part_rows = tokens.shape[1]
    rows = 2 * part_rows
    blk = part_rows // 2
    per = rows // blk
    length = part_rows * ctx
    mine, other = core * seqs, (1 - core) * seqs
    partners = [(i, i ^ 1) for i in range(ctx)]

    def take(array):
        own = lax.dynamic_slice_in_dim(array, mine, seqs, 0)
        got = lax.ppermute(lax.dynamic_slice_in_dim(array, other, seqs, 0), "ctx", partners)
        return jnp.concatenate([own, got], axis=1)

    def give(array):
        got = lax.ppermute(array[:, part_rows:], "ctx", partners)
        result = jnp.zeros((2 * seqs, part_rows) + array.shape[2:], array.dtype)
        result = lax.dynamic_update_slice_in_dim(result, array[:, :part_rows], mine, 0)
        return lax.dynamic_update_slice_in_dim(result, got, other, 0)

    ring = ring_of(chunks)
    position_of = [ring.index(g) for g in range(chunks)]
    position = jnp.array(position_of, jnp.int32)[index // 2]
    slots = (jnp.array(position_of, jnp.int32) - position) % chunks
    where = jnp.concatenate([core[None].astype(jnp.int32), slots])
    reached = jnp.array(ring, jnp.int32)[(position + jnp.arange(chunks)) % chunks]
    two_planes = lax.axis_size("fsdp") == 2
    plane = lax.axis_index("fsdp") if two_planes else jnp.zeros((), jnp.int32)
    place = jnp.concatenate([core[None].astype(jnp.int32), plane[None].astype(jnp.int32), reached])
    planes = [(0, 1), (1, 0)]

    turned_low = [matrix.astype(bf16).T for matrix in masters]
    q_cols, kv_cols = QUERY_WIDTH // ctx, KEY_WIDTH // ctx
    o_cols, f_cols = MODEL_WIDTH // ctx, FF // ctx

    def both_packs(pack, flip):
        stack = jnp.stack(ring_gather(pack, flip), axis=0)
        return stack, lax.ppermute(stack, "ctx", partners)

    first_part = rows_gather(jnp.concatenate(turned_low[:3] + [norm_gains.astype(bf16).T], axis=0))
    first_used = first_part.shape[0]
    first_part = jnp.pad(first_part, ((0, -first_used % 16), (0, 0)))
    gains = first_part[q_cols + 2 * kv_cols : first_used].astype(f32)
    gain_one, gain_two = gains[0:1], gains[1:2]
    first_own, first_other = both_packs(widen(first_part), False)
    (inward,) = call(
        functools.partial(unpack_first_kernel, q_cols, kv_cols),
        1,
        [(whole, first_own), (whole, first_other)],
        [(whole, (KV_PACKED + QUERY_WIDTH, MODEL_WIDTH), bf16)],
        scalars=(where,),
        us=3.3,
    )
    half = MODEL_WIDTH // 2

    def second_part(gate, up, output, down):
        return jnp.concatenate(
            [
                widen(jnp.concatenate([gate, up], axis=1)),
                down[:, :LANES],
                widen(jnp.concatenate([down[:, LANES:], output], axis=1)),
            ],
            axis=0,
        )

    x = take(tokens)
    cot = take(cotangent)
    order = lax.dynamic_slice_in_dim(pair_order, mine, seqs, 0)
    ends = jnp.stack([order, 2 * ctx - 1 - order], axis=2).reshape(seqs, chunks, 2, 2)
    ends = jnp.where(core == 0, ends, ends[:, :, ::-1])
    ends = ends.reshape(seqs, chunks, per)
    blocks = jnp.take(ends, reached, axis=1).reshape(seqs, chunks * per)
    own = blocks[:, :per]
    places = (own[:, :, None] * blk + jnp.arange(blk, dtype=jnp.int32)).reshape(seqs, rows)
    half_dim = HEAD_DIM // 2
    inverse = ROPE_BASE ** (-jnp.arange(half_dim, dtype=f32) * 2.0 / HEAD_DIM)
    angle = places.astype(f32)[..., None] * inverse
    cosine = jnp.tile(jnp.cos(angle), (1, 1, PACK // half_dim))
    sine = jnp.tile(jnp.sin(angle), (1, 1, PACK // half_dim))

    wide = (seqs, rows, MODEL_WIDTH)
    heads = (seqs, per, KV_HEADS, GROUP * blk, PACK)
    normed_one, query, kv = call(
        project_kernel,
        seqs,
        [(one, x), (whole, gain_one), (whole, inward), (one, cosine), (one, sine)],
        [(one, wide, bf16), (one, heads, bf16), (one, (seqs, rows, KV_PACKED), bf16)],
        us=6.2,
    )
    load = length / 2048
    tile_rows = (KV_HEADS, GROUP * blk, PACK)
    kv_trace = []
    kv_all = ring_gather(kv, False, trace=kv_trace)
    outer = (turned_low[4], turned_low[5], turned_low[3], turned_low[6])
    if two_planes:
        same = jnp.stack(ring_gather(second_part(*outer), True, {2: [inward]}), axis=0)
        cross = lax.ppermute(same, "fsdp", planes)
    else:
        outer = [rows_gather(part) for part in outer]
        same, cross = [
            jnp.stack(
                ring_gather(
                    second_part(*[jnp.split(part, 2, axis=1)[side] for part in outer]), True
                ),
                axis=0,
            )
            for side in range(2)
        ]
    second_parts = [same, cross] + [lax.ppermute(part, "ctx", partners) for part in (same, cross)]

    attn, logs = call(
        functools.partial(attend_kernel, chunks),
        seqs,
        [(one, query)] + [(one, chunk) for chunk in kv_all],
        [(one, wide, bf16), (one, heads, f32)],
        scalars=(blocks,),
        scratch=[
            pltpu.VMEM((length, KV_PACKED), bf16),
            pltpu.VMEM((KV_HEADS, length // TILE, GROUP * blk, TILE), f32),
            pltpu.VMEM(tile_rows, f32),
            pltpu.VMEM(tile_rows, f32),
        ],
        us=11.0 * seqs * load,
    )
    ff_wide = (seqs, rows, FF)
    (
        block_local,
        normed_two,
        hidden,
        dgate,
        dup,
        dattn,
        dout,
        dresid,
        gain_two_grad,
    ) = call(
        middle_kernel,
        seqs,
        [
            (one, x),
            (one, attn),
            (one, cot),
            (whole, gain_two),
        ]
        + [(anywhere, part) for part in second_parts],
        [
            (one, wide, f32),
            (one, wide, bf16),
            (one, ff_wide, bf16),
            (one, ff_wide, bf16),
            (one, ff_wide, bf16),
            (one, wide, bf16),
            (one, wide, bf16),
            (one, wide, f32),
            (one, (seqs, 1, MODEL_WIDTH), f32),
        ],
        scratch=[
            pltpu.VMEM((MODEL_WIDTH, QUERY_WIDTH), bf16),
            pltpu.VMEM((FF, MODEL_WIDTH), bf16),
            pltpu.VMEM((FF, MODEL_WIDTH), bf16),
            pltpu.VMEM((MODEL_WIDTH, FF), bf16),
            pltpu.VMEM((2, ctx) + same.shape[1:], bf16),
            pltpu.SemaphoreType.DMA((4, chunks)),
        ],
        scalars=(place,),
        us=26.0,
    )
    block_output = give(block_local)
    def reduced_packs(own_packs, other_packs, flip):
        got = lax.ppermute(other_packs, "ctx", partners)
        terms = [lambda k=k: plus(own_packs[k], got[k]) for k in range(chunks)]
        return ring_scatter(terms, flip)

    def outer_sums(earlier):
        behind = traces[-1]
        dattn_, dgate_ = join([dattn, dgate], earlier)
        (dup_,) = join([dup], *behind[0])
        (hidden_,) = join([hidden], *behind[1])
        packs = call(
            pack_second_kernel,
            1,
            [
                (whole, weight_grad(dattn_, attn).astype(bf16)),
                (whole, weight_grad(dgate_, normed_two).astype(bf16)),
                (whole, weight_grad(dup_, normed_two).astype(bf16)),
                (whole, weight_grad(cot, hidden_).astype(bf16)),
            ],
            [(anywhere, same.shape, bf16)] * 4,
            scalars=(place,),
            scratch=[
                pltpu.VMEM((2, ctx) + same.shape[1:], bf16),
                pltpu.SemaphoreType.DMA((4, chunks)),
            ],
            us=7.7,
            after=behind[2],
        )
        got = [lax.ppermute(part, "ctx", partners) for part in packs[2:]]
        if two_planes:
            sent = lax.ppermute(plus(packs[1], got[1]).astype(bf16), "fsdp", planes)
            terms = [lambda k=k: plus(packs[0][k], got[0][k], sent[k]) for k in range(chunks)]
            sums, trace = ring_scatter(terms, True)
            sums, before_last, before_final = [sums], got, [sent]
        else:
            sums = [
                ring_scatter(
                    [lambda k=k, i=i: plus(packs[i][k], got[i][k]) for k in range(chunks)], True
                )[0]
                for i in range(2)
            ]
            before_last, before_final, trace = got, [], [[], []]
        base = f_cols + o_cols
        result = []
        for pick in (
            lambda part: part[base:, REST : REST + half],
            lambda part: part[:f_cols, :half],
            lambda part: part[:f_cols, half:MODEL_WIDTH],
            lambda part: jnp.concatenate([part[f_cols:base], part[base:, :REST]], axis=1),
        ):
            if two_planes:
                result.append(pick(sums[0]))
            else:
                result.append(rows_scatter(jnp.concatenate([pick(part) for part in sums], axis=1)))
        return result, before_last, before_final, trace[1]

    dinputs, dalls, gain_one_grads, traces = [], [], [], []
    last = seqs - 1
    for first, count in ((0, last), (last, 1)):
        these = since(first)
        waits = []
        if first == last:
            outer_reduced, before_last, before_final, before_pack = outer_sums(dquery)
            waits = before_last
        dquery, *dkv = call(
            functools.partial(attend_back_kernel, chunks, first),
            count,
            [(these, query)]
            + [(these, chunk) for chunk in kv_all]
            + [(these, array) for array in (attn, dout, logs, cosine, sine)],
            [(one, (count,) + wide[1:], bf16)] + [(one, (count, rows, KV_PACKED), bf16)] * chunks,
            scalars=(blocks,),
            scratch=[
                pltpu.VMEM((length, KV_PACKED), bf16),
                pltpu.VMEM((KV_HEADS, 2 * GROUP * blk, PACK), bf16),
                pltpu.VMEM((KV_HEADS, PACK, 2 * GROUP * blk), bf16),
                pltpu.VMEM(tile_rows, f32),
                pltpu.VMEM(tile_rows, f32),
                pltpu.VMEM((KV_PACKED, length), f32),
                pltpu.VMEM((length, KV_PACKED), bf16),
            ],
            us=17.0 * count * load,
            after=waits,
        )
        dkv_own, trace = ring_scatter(
            [lambda k=k, dkv=dkv: dkv[k] for k in range(chunks)],
            first > 0,
            traces[-1][-1] if traces else (),
        )
        traces.append(trace)
        dinput, dall, gain_one_grad = call(
            final_kernel,
            count,
            [
                (these, x),
                (whole, gain_one),
                (one, dquery),
                (one, dkv_own),
                (these, dresid),
                (these, cosine),
                (these, sine),
                (whole, inward),
            ],
            [
                (one, (count,) + wide[1:], f32),
                (one, (count, rows, INNER), bf16),
                (one, (count, 1, MODEL_WIDTH), f32),
            ],
            us=2.0 * count,
            after=before_final if first == last else (),
        )
        dinputs.append(dinput)
        dalls.append(dall)
        gain_one_grads.append(jnp.sum(gain_one_grad, axis=0))
    input_gradient = give(jnp.concatenate(dinputs, axis=0))
    gains_grad = jnp.concatenate([sum(gain_one_grads), jnp.sum(gain_two_grad, axis=0)], axis=0)
    packs = (chunks, first_part.shape[0], LANES)
    first_packs = call(
        functools.partial(pack_first_kernel, q_cols, kv_cols, len(dalls)),
        1,
        [(whole, normed_one)] + [(whole, dall) for dall in dalls] + [(whole, gains_grad)],
        [(whole, packs, bf16), (whole, packs, bf16)],
        scalars=(where,),
        scratch=[pltpu.VMEM((INNER, MODEL_WIDTH), f32)],
        us=3.5,
        after=before_pack,
    )
    first_sum = rows_scatter(reduced_packs(*first_packs, False)[0][:, :MODEL_WIDTH])
    reduced = (
        first_sum[:q_cols],
        first_sum[q_cols : q_cols + kv_cols],
        first_sum[q_cols + kv_cols : q_cols + 2 * kv_cols],
        *outer_reduced,
    )
    gains_total = first_sum[q_cols + 2 * kv_cols : first_used].T
    rates = (
        (MODEL_WIDTH // 4) ** (-0.5),
        MODEL_WIDTH ** (-0.5),
        MODEL_WIDTH ** (-0.5),
        (MODEL_WIDTH // 32) ** (-0.5),
        MODEL_WIDTH ** (-0.5),
        MODEL_WIDTH ** (-0.5),
        (FF // 2) ** (-0.5),
    )
    firsts = (
        query_first,
        key_first_moment,
        value_first_moment,
        output_first,
        gate_first,
        up_first,
        down_first,
    )
    seconds = (
        query_second,
        key_second_moment,
        value_second_moment,
        output_second,
        gate_second,
        up_second,
        down_second,
    )
    results = [
        adam_update(
            masters[member], firsts[member], seconds[member], reduced[member].T, rates[member], DECAY
        )
        for member in range(7)
    ]
    results.append(adam_update(norm_gains, gains_first, gains_second, gains_total, GAIN_RATE, 0.0))
    new_weights = [result[0] for result in results]
    new_firsts = [result[1] for result in results]
    new_seconds = [result[2] for result in results]
    return tuple([block_output, input_gradient] + new_weights + new_firsts + new_seconds)


def solution(mesh):
    sequences = P("fsdp", "ctx", None)
    matrix = P("fsdp", "ctx")
    gains = P("fsdp", None)
    state = (matrix,) * 7 + (gains,)
    return jax.shard_map(
        body,
        mesh=mesh,
        in_specs=(sequences, sequences, P("fsdp", None)) + state * 3,
        out_specs=(sequences, sequences) + state * 3,
        check_vma=False,
    )
```

```python
import functools

import jax
import jax.numpy as jnp
from jax import lax
from jax.experimental import pallas as pl
from jax.experimental.pallas import tpu as pltpu
from jax.sharding import PartitionSpec as P

MODEL_WIDTH = 576
FF = 1536
HEADS = 9
KV_HEADS = 3
HEAD_DIM = 64
STEP = 10
GROUP = HEADS // KV_HEADS
KEY_WIDTH = KV_HEADS * HEAD_DIM
QUERY_WIDTH = HEADS * HEAD_DIM
PACK = 2 * HEAD_DIM
KV_PACKED = KV_HEADS * PACK
TILE = 256
FF_CHUNK = 640
LANES = 640
INNER = 1024
REST = FF // 2 - LANES

NORM_EPS = 1e-05
ROPE_BASE = 100000.0
BETA_ONE = 0.9
BETA_TWO = 0.95
ADAM_EPS = 1e-08
DECAY = 0.1
GAIN_RATE = 0.5
MASKED = -1e30
FLOPS_PER_US = 1153.5e6
VMEM_BYTES = 56 * 1024 * 1024

f32 = jnp.float32
bf16 = jnp.bfloat16


def dot_nt(a, b):
    return lax.dot_general(a, b, (((1,), (1,)), ((), ())), preferred_element_type=f32)


def dot_nn(a, b):
    return lax.dot_general(a, b, (((1,), (0,)), ((), ())), preferred_element_type=f32)


def lanes_of(shape):
    return lax.broadcasted_iota(jnp.int32, shape, len(shape) - 1)


def turned(v, first):
    lane = lanes_of(v.shape) % HEAD_DIM
    ahead = pltpu.roll(v, PACK - HEAD_DIM // 2, 1)
    behind = pltpu.roll(v, HEAD_DIM // 2, 1)
    if first:
        return jnp.where(lane < HEAD_DIM // 2, -ahead, behind)
    return jnp.where(lane < HEAD_DIM // 2, ahead, -behind)


def project_kernel(x_ref, gain_ref, weight_ref, cos_ref, sin_ref, normed_ref, query_ref, kv_ref):
    rows = x_ref.shape[1]
    blk = query_ref.shape[3] // GROUP
    x = x_ref[0].astype(f32)
    inv = lax.rsqrt(jnp.mean(x * x, axis=-1, keepdims=True) + NORM_EPS)
    normed = (x * inv * gain_ref[...]).astype(bf16)
    normed_ref[0] = normed
    raw = dot_nt(normed, weight_ref[...])
    cosine, sine = cos_ref[0], sin_ref[0]
    low_half = lanes_of((rows, PACK)) < HEAD_DIM
    for j in range(KV_HEADS):
        part = raw[:, j * PACK : (j + 1) * PACK]
        spun = part * cosine + turned(part, True) * sine
        kv_ref[0, :, j * PACK : (j + 1) * PACK] = jnp.where(low_half, spun, part).astype(bf16)
    for i in range((HEADS + 1) // 2):
        begin = KV_PACKED + i * PACK
        if 2 * i + 1 < HEADS:
            part = raw[:, begin : begin + PACK]
        else:
            tail = raw[:, begin : begin + HEAD_DIM]
            part = jnp.concatenate([tail, tail], axis=1)
        spun = part * cosine + turned(part, True) * sine
        spun = spun.astype(bf16).astype(f32) * (HEAD_DIM**-0.5)
        pair = [jnp.where(low_half, spun, 0.0)]
        if 2 * i + 1 < HEADS:
            pair.append(jnp.where(low_half, pltpu.roll(spun, HEAD_DIM, 1), 0.0))
        for offset, value in enumerate(pair):
            head = 2 * i + offset
            j, member = head // GROUP, head % GROUP
            value = value.astype(bf16)
            for b in range(rows // blk):
                query_ref[0, b, j, member * blk : (member + 1) * blk, :] = value[
                    b * blk : (b + 1) * blk
                ]


def sort_blocks(blocks_ref, s, kv_refs, sorted_ref, blk):
    per = kv_refs[0].shape[1] // blk
    for g, kv_ref in enumerate(kv_refs):
        for b in range(per):
            place = pl.multiple_of(blocks_ref[s, g * per + b] * blk, blk)
            sorted_ref[pl.ds(place, blk), :] = kv_ref[0, b * blk : (b + 1) * blk, :]


def allowed_mask(place, tile_begin, blk, rows):
    row = lax.broadcasted_iota(jnp.int32, (rows, TILE), 0) % blk
    col = lax.broadcasted_iota(jnp.int32, (rows, TILE), 1)
    return col <= row + (place * blk - tile_begin)


def attend_kernel(chunks, blocks_ref, query_ref, *refs):
    s = pl.program_id(0)
    kv_refs = refs[:chunks]
    out_ref, log_ref, sorted_ref, score_ref, top_ref, acc_ref = refs[chunks:]
    per, rows = query_ref.shape[1], query_ref.shape[3]
    blk = rows // GROUP
    sort_blocks(blocks_ref, s, kv_refs, sorted_ref, blk)
    lane = lanes_of((TILE, PACK))
    for b in range(per):
        place = blocks_ref[s, b]
        full = (place * blk) // TILE

        def score_tile(t, masked):
            begin = pl.multiple_of(t * TILE, TILE)
            for j in range(KV_HEADS):
                kv = sorted_ref[pl.ds(begin, TILE), j * PACK : (j + 1) * PACK]
                score = dot_nt(query_ref[0, b, j], kv)
                if masked:
                    score = jnp.where(allowed_mask(place, begin, blk, rows), score, MASKED)
                score_ref[j, t] = score
                best = jnp.maximum(score[:, :PACK], score[:, PACK:])
                top_ref[j] = jnp.maximum(top_ref[j], best)

        top_ref[...] = jnp.full(top_ref.shape, MASKED, f32)
        acc_ref[...] = jnp.zeros(acc_ref.shape, f32)

        @pl.loop(0, full)
        def _(t):
            score_tile(t, False)

        score_tile(full, True)
        for j in range(KV_HEADS):
            top = jnp.max(top_ref[j], axis=-1, keepdims=True)
            top_ref[j] = jnp.broadcast_to(top, (rows, PACK))

        @pl.loop(0, full + 1)
        def _(t):
            begin = pl.multiple_of(t * TILE, TILE)
            for j in range(KV_HEADS):
                kv = sorted_ref[pl.ds(begin, TILE), j * PACK : (j + 1) * PACK]
                ones_v = jnp.where(lane < HEAD_DIM, jnp.ones((), bf16), kv)
                top = top_ref[j]
                score = score_ref[j, t]
                prob = jnp.concatenate(
                    [jnp.exp(score[:, :PACK] - top), jnp.exp(score[:, PACK:] - top)], axis=1
                )
                acc_ref[j] += dot_nn(prob.astype(bf16), ones_v)

        for j in range(KV_HEADS):
            acc = acc_ref[j]
            low_half = lanes_of(acc.shape) < HEAD_DIM
            total = jnp.where(low_half, acc, pltpu.roll(acc, HEAD_DIM, 1))
            log_ref[0, b, j] = top_ref[j] + jnp.log(total)
            attended = (acc / total).astype(bf16)
            for member in range(GROUP):
                head = j * GROUP + member
                out_ref[0, b * blk : (b + 1) * blk, head * HEAD_DIM : (head + 1) * HEAD_DIM] = (
                    attended[member * blk : (member + 1) * blk, HEAD_DIM:]
                )


def unpack_second(place_ref, part_refs, pack_ref, sems, out_w_ref, gate_w_ref, up_w_ref, down_w_ref):
    ctx = pack_ref.shape[1]
    f_cols, o_cols, half = FF // ctx, MODEL_WIDTH // ctx, MODEL_WIDTH // 2
    copies = []
    for part, part_ref in enumerate(part_refs):
        core = jnp.abs(place_ref[0] - part // 2)
        plane = jnp.abs(place_ref[1] - part % 2)
        for k in range(part_ref.shape[0]):
            index = 2 * place_ref[2 + k] + core
            copies.append(
                pltpu.make_async_copy(
                    part_ref.at[k], pack_ref.at[plane, index], sems.at[part, k]
                )
            )
    for copy in copies:
        copy.start()
    for copy in copies:
        copy.wait()
    for c in range(ctx):
        here = slice(c * f_cols, (c + 1) * f_cols)
        low, high = pack_ref[0, c, :f_cols, :], pack_ref[1, c, :f_cols, :]
        gate_w_ref[here, :] = jnp.concatenate([low[:, :half], high[:, :half]], axis=1)
        up_w_ref[here, :] = jnp.concatenate(
            [low[:, half:MODEL_WIDTH], high[:, half:MODEL_WIDTH]], axis=1
        )

    def natural(plane, base, lanes):
        pieces = [
            pack_ref[plane, c, base : base + o_cols, lanes].astype(f32) for c in range(ctx)
        ]
        return jnp.concatenate(pieces, axis=0).astype(bf16)

    base = f_cols + o_cols
    for plane in range(2):
        begin = plane * (FF // 2)
        down_w_ref[:, begin : begin + LANES] = natural(plane, f_cols, slice(0, LANES))
        down_w_ref[:, begin + LANES : begin + FF // 2] = natural(plane, base, slice(0, REST))
    out_w_ref[...] = jnp.concatenate(
        [natural(plane, base, slice(REST, REST + half)) for plane in range(2)], axis=1
    )


def middle_kernel(
    place_ref,
    x_ref,
    attn_ref,
    cot_ref,
    gain_ref,
    part_a_ref,
    part_b_ref,
    part_c_ref,
    part_d_ref,
    block_ref,
    normed_ref,
    hidden_ref,
    dgate_ref,
    dup_ref,
    dattn_ref,
    dout_ref,
    dresid_ref,
    gain_grad_ref,
    out_w_ref,
    gate_w_ref,
    up_w_ref,
    down_w_ref,
    pack_ref,
    sems,
):
    @pl.when(pl.program_id(0) == 0)
    def _():
        parts = (part_a_ref, part_b_ref, part_c_ref, part_d_ref)
        unpack_second(
            place_ref, parts, pack_ref, sems, out_w_ref, gate_w_ref, up_w_ref, down_w_ref
        )

    attn = attn_ref[0]
    cot = cot_ref[0]
    resid = x_ref[0].astype(f32) + dot_nt(attn, out_w_ref[...])
    inv = lax.rsqrt(jnp.mean(resid * resid, axis=-1, keepdims=True) + NORM_EPS)
    hat = resid * inv
    gain = gain_ref[...]
    normed = (hat * gain).astype(bf16)
    normed_ref[0] = normed
    block = resid
    dnormed = jnp.zeros(resid.shape, f32)
    for begin in range(0, FF, FF_CHUNK):
        span = slice(begin, min(begin + FF_CHUNK, FF))
        gate = dot_nt(normed, gate_w_ref[span, :])
        up = dot_nt(normed, up_w_ref[span, :])
        sig = 1.0 / (1.0 + jnp.exp(-gate))
        act = gate * sig
        hidden = (act * up).astype(bf16)
        hidden_ref[0, :, span] = hidden
        block = block + dot_nt(hidden, down_w_ref[:, span])
        dhidden = dot_nn(cot, down_w_ref[:, span])
        dgate = (dhidden * up * (sig * (1.0 + gate * (1.0 - sig)))).astype(bf16)
        dup = (dhidden * act).astype(bf16)
        dgate_ref[0, :, span] = dgate
        dup_ref[0, :, span] = dup
        dnormed = dnormed + dot_nn(dgate, gate_w_ref[span, :]) + dot_nn(dup, up_w_ref[span, :])
    block_ref[0] = block
    gain_grad_ref[0] = jnp.sum(dnormed * hat, axis=0, keepdims=True)
    scaled = dnormed * gain
    dresid = cot.astype(f32) + inv * (scaled - hat * jnp.mean(scaled * hat, axis=-1, keepdims=True))
    dresid_ref[0] = dresid
    dattn = dresid.astype(bf16)
    dattn_ref[0] = dattn
    dout_ref[0] = dot_nn(dattn, out_w_ref[...]).astype(bf16)


def attend_back_kernel(chunks, first, blocks_ref, query_ref, *refs):
    s = first + pl.program_id(0)
    kv_refs = refs[:chunks]
    out_ref, dout_ref, log_ref, cos_ref, sin_ref, dquery_ref = refs[chunks : chunks + 6]
    dkv_refs = refs[chunks + 6 : 2 * chunks + 6]
    sorted_ref, both_ref, flip_ref, delta_ref, dq_ref, dkv_t_ref, dkv_s_ref = refs[2 * chunks + 6 :]
    per, rows = query_ref.shape[1], query_ref.shape[3]
    blk = rows // GROUP
    length = sorted_ref.shape[0]
    sort_blocks(blocks_ref, s, kv_refs, sorted_ref, blk)
    dkv_t_ref[...] = jnp.zeros(dkv_t_ref.shape, f32)
    for b in range(per):
        place = blocks_ref[s, b]
        full = (place * blk) // TILE
        span = slice(b * blk, (b + 1) * blk)
        for j in range(KV_HEADS):
            both_ref[j, :rows] = query_ref[0, b, j]
            for member in range(GROUP):
                head = j * GROUP + member
                lanes = slice(head * HEAD_DIM, (head + 1) * HEAD_DIM)
                dout = dout_ref[0, span, lanes]
                delta = jnp.sum(
                    dout.astype(f32) * out_ref[0, span, lanes].astype(f32), axis=-1, keepdims=True
                )
                here = slice(member * blk, (member + 1) * blk)
                delta_ref[j, here] = jnp.broadcast_to(delta, (blk, PACK))
                both_ref[j, rows + member * blk : rows + (member + 1) * blk] = jnp.concatenate(
                    [jnp.zeros_like(dout), dout], axis=1
                )
            flip_ref[j] = both_ref[j].T
        dq_ref[...] = jnp.zeros(dq_ref.shape, f32)

        def tile_step(t, masked):
            begin = pl.multiple_of(t * TILE, TILE)
            kvs = [
                sorted_ref[pl.ds(begin, TILE), j * PACK : (j + 1) * PACK] for j in range(KV_HEADS)
            ]
            joined = [dot_nt(both_ref[j], kvs[j]) for j in range(KV_HEADS)]
            dscores, joints = [], []
            for j in range(KV_HEADS):
                score, dprob = joined[j][:rows], joined[j][rows:]
                log_total = log_ref[0, b, j]
                delta = delta_ref[j]
                prob = jnp.concatenate(
                    [jnp.exp(score[:, :PACK] - log_total), jnp.exp(score[:, PACK:] - log_total)],
                    axis=1,
                )
                if masked:
                    prob = jnp.where(allowed_mask(place, begin, blk, rows), prob, 0.0)
                dscore = prob * jnp.concatenate(
                    [dprob[:, :PACK] - delta, dprob[:, PACK:] - delta], axis=1
                )
                dscores.append(dscore.astype(bf16))
                joints.append(jnp.concatenate([dscores[j], prob.astype(bf16)], axis=0))
            dqs = [dot_nn(dscores[j], kvs[j]) for j in range(KV_HEADS)]
            dkvs = [dot_nn(flip_ref[j], joints[j]) for j in range(KV_HEADS)]
            for j in range(KV_HEADS):
                dq_ref[j] += dqs[j]
                dkv_t_ref[j * PACK : (j + 1) * PACK, pl.ds(begin, TILE)] += dkvs[j]

        @pl.loop(0, full)
        def _(t):
            tile_step(t, False)

        tile_step(full, True)
        cosine, sine = cos_ref[0, span, :], sin_ref[0, span, :]
        for j in range(KV_HEADS):
            for member in range(GROUP):
                head = j * GROUP + member
                grad = dq_ref[j, member * blk : (member + 1) * blk]
                back = (grad * cosine + turned(grad, False) * sine) * (HEAD_DIM**-0.5)
                dquery_ref[0, span, head * HEAD_DIM : (head + 1) * HEAD_DIM] = back[
                    :, :HEAD_DIM
                ].astype(bf16)
    for begin in range(0, length, TILE):
        dkv_s_ref[begin : begin + TILE, :] = dkv_t_ref[:, begin : begin + TILE].T.astype(bf16)
    for g, dkv_ref in enumerate(dkv_refs):
        for b in range(per):
            place = pl.multiple_of(blocks_ref[s, g * per + b] * blk, blk)
            dkv_ref[0, b * blk : (b + 1) * blk, :] = dkv_s_ref[pl.ds(place, blk), :]


def final_kernel(
    x_ref,
    gain_ref,
    dquery_ref,
    dkv_ref,
    dresid_ref,
    cos_ref,
    sin_ref,
    weight_ref,
    dinput_ref,
    dall_ref,
    gain_grad_ref,
):
    rows = x_ref.shape[1]
    cosine, sine = cos_ref[0], sin_ref[0]
    low_half = lanes_of((rows, PACK)) < HEAD_DIM
    for j in range(KV_HEADS):
        part = dkv_ref[0, :, j * PACK : (j + 1) * PACK].astype(f32)
        back = part * cosine + turned(part, False) * sine
        dall_ref[0, :, j * PACK : (j + 1) * PACK] = jnp.where(low_half, back, part).astype(bf16)
    used = KV_PACKED + QUERY_WIDTH
    dall_ref[0, :, KV_PACKED:used] = dquery_ref[0]
    dall_ref[0, :, used:] = jnp.zeros((rows, INNER - used), bf16)
    dnormed = dot_nn(dall_ref[0, :, :used], weight_ref[...])
    x = x_ref[0].astype(f32)
    inv = lax.rsqrt(jnp.mean(x * x, axis=-1, keepdims=True) + NORM_EPS)
    hat = x * inv
    gain_grad_ref[0] = jnp.sum(dnormed * hat, axis=0, keepdims=True)
    scaled = dnormed * gain_ref[...]
    dinput_ref[0] = dresid_ref[0] + inv * (
        scaled - hat * jnp.mean(scaled * hat, axis=-1, keepdims=True)
    )


def natural_pieces(where_ref, own_ref, other_ref, begin, size):
    zero = where_ref[0] == 0
    pieces = []
    for g in range(own_ref.shape[0]):
        slot = where_ref[1 + g]
        mine = own_ref[slot, begin : begin + size, :].astype(f32)
        theirs = other_ref[slot, begin : begin + size, :].astype(f32)
        pieces.append(jnp.where(zero, mine, theirs))
        pieces.append(jnp.where(zero, theirs, mine))
    return jnp.concatenate(pieces, axis=0).astype(bf16)


def unpack_first_kernel(q_cols, kv_cols, where_ref, own_ref, other_ref, inward_ref):
    width = inward_ref.shape[1]
    query = natural_pieces(where_ref, own_ref, other_ref, 0, q_cols)
    inward_ref[KV_PACKED:, :] = query[:, :width]
    for offset in range(2):
        part = natural_pieces(where_ref, own_ref, other_ref, q_cols + offset * kv_cols, kv_cols)
        for j in range(KV_HEADS):
            begin = j * PACK + offset * HEAD_DIM
            inward_ref[begin : begin + HEAD_DIM, :] = part[
                j * HEAD_DIM : (j + 1) * HEAD_DIM, :width
            ]


def pack_rows(where_ref, own_ref, other_ref, source, begin, size):
    zero = where_ref[0] == 0
    lanes = source.shape[1]
    for g in range(own_ref.shape[0]):
        slot = where_ref[1 + g]
        even = source[2 * g * size : (2 * g + 1) * size]
        odd = source[(2 * g + 1) * size : (2 * g + 2) * size]
        own_ref[slot, begin : begin + size, :lanes] = jnp.where(zero, even, odd).astype(bf16)
        other_ref[slot, begin : begin + size, :lanes] = jnp.where(zero, odd, even).astype(bf16)


def pack_first_kernel(q_cols, kv_cols, parts, where_ref, normed_ref, *refs):
    dall_refs, (gains_ref, own_ref, other_ref, grad_ref) = refs[:parts], refs[parts:]
    width = grad_ref.shape[1]
    seq = 0
    for dall_ref in dall_refs:
        for s in range(dall_ref.shape[0]):
            term = dot_nn(dall_ref[s].T, normed_ref[seq])
            grad_ref[...] = term if seq == 0 else grad_ref[...] + term
            seq += 1
    query = grad_ref[KV_PACKED : KV_PACKED + QUERY_WIDTH, :]
    pack_rows(where_ref, own_ref, other_ref, query, 0, q_cols)
    for offset in range(2):
        part = jnp.concatenate(
            [
                grad_ref[j * PACK + offset * HEAD_DIM : j * PACK + (offset + 1) * HEAD_DIM, :]
                for j in range(KV_HEADS)
            ],
            axis=0,
        )
        pack_rows(where_ref, own_ref, other_ref, part, q_cols + offset * kv_cols, kv_cols)
    begin = q_cols + 2 * kv_cols
    for g in range(own_ref.shape[0]):
        own_ref[g, begin : begin + 2, :width] = gains_ref[...].astype(bf16)
        other_ref[g, begin : begin + 2, :width] = gains_ref[...].astype(bf16)


def pack_second_kernel(
    place_ref, out_g_ref, gate_g_ref, up_g_ref, down_g_ref, a_ref, b_ref, c_ref, d_ref, pack_ref, sems
):
    ctx = pack_ref.shape[1]
    f_cols, o_cols, half = FF // ctx, MODEL_WIDTH // ctx, MODEL_WIDTH // 2
    base = f_cols + o_cols
    for plane in range(2):
        lanes = slice(plane * half, (plane + 1) * half)
        for c in range(ctx):
            here = slice(c * f_cols, (c + 1) * f_cols)
            pack_ref[plane, c, :f_cols, :MODEL_WIDTH] = jnp.concatenate(
                [gate_g_ref[here, lanes], up_g_ref[here, lanes]], axis=1
            )
        begin = plane * (FF // 2)
        first = down_g_ref[:, begin : begin + LANES].astype(f32)
        rest = down_g_ref[:, begin + LANES : begin + FF // 2]
        second = jnp.concatenate([rest, out_g_ref[:, lanes]], axis=1).astype(f32)
        for c in range(ctx):
            here = slice(c * o_cols, (c + 1) * o_cols)
            pack_ref[plane, c, f_cols:base, :] = first[here].astype(bf16)
            pack_ref[plane, c, base : base + o_cols, : REST + half] = second[here].astype(bf16)
    copies = []
    for part, part_ref in enumerate((a_ref, b_ref, c_ref, d_ref)):
        core = jnp.abs(place_ref[0] - part // 2)
        plane = jnp.abs(place_ref[1] - part % 2)
        for k in range(part_ref.shape[0]):
            index = 2 * place_ref[2 + k] + core
            copies.append(
                pltpu.make_async_copy(
                    pack_ref.at[plane, index], part_ref.at[k], sems.at[part, k]
                )
            )
    for copy in copies:
        copy.start()
    for copy in copies:
        copy.wait()


def one(shape):
    rest = tuple(shape[1:])
    return pl.BlockSpec((1,) + rest, lambda s, *_: (s,) + (0,) * len(rest))


def whole(shape):
    return pl.BlockSpec(tuple(shape), lambda s, *_: (0,) * len(shape))


def anywhere(shape):
    return pl.BlockSpec(memory_space=pl.ANY)


def since(first):
    def make(shape):
        rest = tuple(shape[1:])
        return pl.BlockSpec((1,) + rest, lambda s, *_: (first + s,) + (0,) * len(rest))

    return make


def call(kernel, seqs, inputs, outputs, scalars=(), scratch=(), us=1.0, after=()):
    begin = len(scalars) + len(inputs)

    def body_of(*refs):
        kernel(*refs[:begin], *refs[begin + len(after) :])

    in_specs = [make(array.shape) for make, array in inputs]
    in_specs += [anywhere(array.shape) for array in after]
    out_specs = [make(shape) for make, shape, _ in outputs]
    moved = sum(array.size * array.dtype.itemsize for _, array in inputs)
    for _, shape, kind in outputs:
        count = 1
        for size in shape:
            count *= size
        moved += count * jnp.dtype(kind).itemsize
    return pl.pallas_call(
        body_of,
        grid_spec=pltpu.PrefetchScalarGridSpec(
            num_scalar_prefetch=len(scalars),
            grid=(seqs,),
            in_specs=in_specs,
            out_specs=out_specs,
            scratch_shapes=list(scratch),
        ),
        out_shape=[jax.ShapeDtypeStruct(shape, kind) for _, shape, kind in outputs],
        compiler_params=pltpu.CompilerParams(vmem_limit_bytes=VMEM_BYTES),
        cost_estimate=pl.CostEstimate(
            flops=int(us * FLOPS_PER_US), bytes_accessed=int(moved), transcendentals=0
        ),
    )(*scalars, *[array for _, array in inputs], *after)


def join_kernel(*refs):
    del refs


def join(arrays, *after):
    return pl.pallas_call(
        join_kernel,
        in_specs=[pl.BlockSpec(memory_space=pl.ANY)] * (len(arrays) + len(after)),
        out_specs=[pl.BlockSpec(memory_space=pl.ANY)] * len(arrays),
        out_shape=[jax.ShapeDtypeStruct(array.shape, array.dtype) for array in arrays],
        input_output_aliases={i: i for i in range(len(arrays))},
    )(*arrays, *after)


def adam_update(weight, first, second, grad, rate, decay):
    first_next = BETA_ONE * first + (1.0 - BETA_ONE) * grad
    second_next = BETA_TWO * second + (1.0 - BETA_TWO) * grad * grad
    first_fix = first_next / (1.0 - BETA_ONE**STEP)
    second_fix = second_next / (1.0 - BETA_TWO**STEP)
    update = first_fix / (jnp.sqrt(second_fix) + ADAM_EPS) + decay * weight
    return (weight - rate * update, first_next, second_next)


def ring_of(chips):
    if chips == 8:
        return [0, 2, 4, 6, 7, 5, 3, 1]
    return list(range(chips))


def ring_pairs(chips, step):
    ring = ring_of(chips)
    return [
        (2 * ring[p] + core, 2 * ring[(p + step) % chips] + core)
        for p in range(chips)
        for core in range(2)
    ]


def ring_gather(mine, flip, pins=None, trace=None, state=None, until=None):
    chips = lax.axis_size("ctx") // 2
    steps = (chips // 2, (chips - 1) // 2)
    if flip:
        steps = steps[::-1]
    begin, ahead, behind, result = state or (0, mine, mine, [mine] * chips)
    result = list(result)
    for t in range(begin + 1, (until or max(steps)) + 1):
        if pins and t - 1 in pins and t - 1 <= min(steps):
            ahead, behind = join([ahead, behind], *pins[t - 1])
            result[-(t - 1) % chips], result[t - 1] = ahead, behind
        if t <= steps[0]:
            ahead = lax.ppermute(ahead, "ctx", ring_pairs(chips, 1))
            result[-t % chips] = ahead
        if t <= steps[1]:
            behind = lax.ppermute(behind, "ctx", ring_pairs(chips, -1))
            result[t] = behind
        if trace is not None:
            trace.append([ahead, behind])
    return (until, ahead, behind, result) if until else result


def plus(*terms):
    total = terms[0].astype(f32)
    for term in terms[1:]:
        total = total + term.astype(f32)
    return total


def ring_scatter(terms, flip, pin=()):
    chips = lax.axis_size("ctx") // 2
    steps = (chips // 2, (chips - 1) // 2)
    if flip:
        steps = steps[::-1]
    moving = [terms[steps[0]]().astype(bf16), terms[-steps[1] % chips]().astype(bf16)]
    if pin:
        moving = list(join(moving, *pin))
    trace = []
    for t in range(max(steps)):
        for way in range(2):
            left = steps[way] - 1 - t
            if left < 0:
                continue
            sign = 1 - 2 * way
            got = lax.ppermute(moving[way], "ctx", ring_pairs(chips, sign))
            if left:
                got = plus(got, terms[sign * left % chips]()).astype(bf16)
            moving[way] = got
        trace.append(list(moving))
    return plus(terms[0](), moving[0], moving[1]), trace


def rows_gather(part):
    if lax.axis_size("fsdp") != 2:
        return lax.all_gather(part, "fsdp", axis=1, tiled=True)
    first = lax.axis_index("fsdp") == 0
    got = lax.ppermute(part, "fsdp", [(0, 1), (1, 0)])
    return jnp.concatenate([jnp.where(first, part, got), jnp.where(first, got, part)], axis=1)


def rows_scatter(grads):
    fsdp = lax.axis_size("fsdp")
    if fsdp != 2:
        return lax.psum_scatter(
            grads.astype(bf16), "fsdp", scatter_dimension=1, tiled=True
        ).astype(f32)
    first = lax.axis_index("fsdp") == 0
    half = grads.shape[1] // 2
    low, high = grads[:, :half], grads[:, half:]
    got = lax.ppermute(jnp.where(first, high, low).astype(bf16), "fsdp", [(0, 1), (1, 0)])
    return jnp.where(first, low, high) + got.astype(f32)


def widen(array):
    return jnp.pad(array, ((0, 0), (0, LANES - array.shape[1])))


def weight_grad(left, right):
    return lax.dot_general(left, right, (((0, 1), (0, 1)), ((), ())), preferred_element_type=f32)


def body(
    tokens,
    cotangent,
    pair_order,
    query_weight,
    key_master_weight,
    value_master_weight,
    output_weight,
    gate_weight,
    up_weight,
    down_weight,
    norm_gains,
    query_first,
    key_first_moment,
    value_first_moment,
    output_first,
    gate_first,
    up_first,
    down_first,
    gains_first,
    query_second,
    key_second_moment,
    value_second_moment,
    output_second,
    gate_second,
    up_second,
    down_second,
    gains_second,
):
    masters = (
        query_weight,
        key_master_weight,
        value_master_weight,
        output_weight,
        gate_weight,
        up_weight,
        down_weight,
    )
    ctx = lax.axis_size("ctx")
    index = lax.axis_index("ctx")
    chunks = ctx // 2
    core = index % 2
    seqs = tokens.shape[0] // 2
    part_rows = tokens.shape[1]
    rows = 2 * part_rows
    blk = part_rows // 2
    per = rows // blk
    length = part_rows * ctx
    mine, other = core * seqs, (1 - core) * seqs
    partners = [(i, i ^ 1) for i in range(ctx)]

    def take(array):
        own = lax.dynamic_slice_in_dim(array, mine, seqs, 0)
        got = lax.ppermute(lax.dynamic_slice_in_dim(array, other, seqs, 0), "ctx", partners)
        return jnp.concatenate([own, got], axis=1)

    def give(array):
        got = lax.ppermute(array[:, part_rows:], "ctx", partners)
        result = jnp.zeros((2 * seqs, part_rows) + array.shape[2:], array.dtype)
        result = lax.dynamic_update_slice_in_dim(result, array[:, :part_rows], mine, 0)
        return lax.dynamic_update_slice_in_dim(result, got, other, 0)

    ring = ring_of(chunks)
    position_of = [ring.index(g) for g in range(chunks)]
    position = jnp.array(position_of, jnp.int32)[index // 2]
    slots = (jnp.array(position_of, jnp.int32) - position) % chunks
    where = jnp.concatenate([core[None].astype(jnp.int32), slots])
    reached = jnp.array(ring, jnp.int32)[(position + jnp.arange(chunks)) % chunks]
    two_planes = lax.axis_size("fsdp") == 2
    plane = lax.axis_index("fsdp") if two_planes else jnp.zeros((), jnp.int32)
    place = jnp.concatenate([core[None].astype(jnp.int32), plane[None].astype(jnp.int32), reached])
    planes = [(0, 1), (1, 0)]

    turned_low = [matrix.astype(bf16).T for matrix in masters]
    q_cols, kv_cols = QUERY_WIDTH // ctx, KEY_WIDTH // ctx
    o_cols, f_cols = MODEL_WIDTH // ctx, FF // ctx

    def both_packs(pack, flip, pins):
        stack = jnp.stack(ring_gather(pack, flip, pins), axis=0)
        return stack, lax.ppermute(stack, "ctx", partners)

    first_part = rows_gather(jnp.concatenate(turned_low[:3] + [norm_gains.astype(bf16).T], axis=0))
    first_used = first_part.shape[0]
    first_part = jnp.pad(first_part, ((0, -first_used % 16), (0, 0)))
    gains = first_part[q_cols + 2 * kv_cols : first_used].astype(f32)
    gain_one, gain_two = gains[0:1], gains[1:2]
    half = MODEL_WIDTH // 2

    def second_part(gate, up, output, down):
        return jnp.concatenate(
            [
                widen(jnp.concatenate([gate, up], axis=1)),
                down[:, :LANES],
                widen(jnp.concatenate([down[:, LANES:], output], axis=1)),
            ],
            axis=0,
        )

    outer = (turned_low[4], turned_low[5], turned_low[3], turned_low[6])
    second_trace = []
    if two_planes:
        part = join([second_part(*outer)], first_part)[0]
        started = [ring_gather(part, True, trace=second_trace, until=2)]
    else:
        outer = [rows_gather(part) for part in outer]
        started = [
            ring_gather(
                second_part(*[jnp.split(part, 2, axis=1)[side] for part in outer]),
                True,
                trace=second_trace,
                until=2,
            )
            for side in range(2)
        ]
    first_own, first_other = both_packs(widen(first_part), False, {2: second_trace[0]})
    (inward,) = call(
        functools.partial(unpack_first_kernel, q_cols, kv_cols),
        1,
        [(whole, first_own), (whole, first_other)],
        [(whole, (KV_PACKED + QUERY_WIDTH, MODEL_WIDTH), bf16)],
        scalars=(where,),
        us=3.3,
        after=second_trace[0],
    )
    x = take(tokens)
    cot = take(cotangent)
    order = lax.dynamic_slice_in_dim(pair_order, mine, seqs, 0)
    ends = jnp.stack([order, 2 * ctx - 1 - order], axis=2).reshape(seqs, chunks, 2, 2)
    ends = jnp.where(core == 0, ends, ends[:, :, ::-1])
    ends = ends.reshape(seqs, chunks, per)
    blocks = jnp.take(ends, reached, axis=1).reshape(seqs, chunks * per)
    own = blocks[:, :per]
    places = (own[:, :, None] * blk + jnp.arange(blk, dtype=jnp.int32)).reshape(seqs, rows)
    half_dim = HEAD_DIM // 2
    inverse = ROPE_BASE ** (-jnp.arange(half_dim, dtype=f32) * 2.0 / HEAD_DIM)
    angle = places.astype(f32)[..., None] * inverse
    cosine = jnp.tile(jnp.cos(angle), (1, 1, PACK // half_dim))
    sine = jnp.tile(jnp.sin(angle), (1, 1, PACK // half_dim))

    wide = (seqs, rows, MODEL_WIDTH)
    heads = (seqs, per, KV_HEADS, GROUP * blk, PACK)
    normed_one, query, kv = call(
        project_kernel,
        seqs,
        [(one, x), (whole, gain_one), (whole, inward), (one, cosine), (one, sine)],
        [(one, wide, bf16), (one, heads, bf16), (one, (seqs, rows, KV_PACKED), bf16)],
        us=6.2,
        after=second_trace[1],
    )
    load = length / 2048
    tile_rows = (KV_HEADS, GROUP * blk, PACK)
    kv_trace = []
    kv_all = ring_gather(kv, False, trace=kv_trace)
    def later(part):
        return join([part], first_part)[0]

    if two_planes:
        same = jnp.stack(
            ring_gather(None, True, {2: [inward], 3: kv_trace[1]}, None, started[0]), axis=0
        )
        cross = lax.ppermute(same, "fsdp", planes)
    else:
        same, cross = [
            jnp.stack(ring_gather(None, True, state=state), axis=0) for state in started
        ]
    attn, logs = call(
        functools.partial(attend_kernel, chunks),
        seqs,
        [(one, query)] + [(one, chunk) for chunk in kv_all],
        [(one, wide, bf16), (one, heads, f32)],
        scalars=(blocks,),
        scratch=[
            pltpu.VMEM((length, KV_PACKED), bf16),
            pltpu.VMEM((KV_HEADS, length // TILE, GROUP * blk, TILE), f32),
            pltpu.VMEM(tile_rows, f32),
            pltpu.VMEM(tile_rows, f32),
        ],
        us=11.0 * seqs * load,
    )
    (cross,) = join([cross], attn)
    second_parts = [same, cross] + [lax.ppermute(part, "ctx", partners) for part in (same, cross)]
    ff_wide = (seqs, rows, FF)
    (
        block_local,
        normed_two,
        hidden,
        dgate,
        dup,
        dattn,
        dout,
        dresid,
        gain_two_grad,
    ) = call(
        middle_kernel,
        seqs,
        [
            (one, x),
            (one, attn),
            (one, cot),
            (whole, gain_two),
        ]
        + [(anywhere, part) for part in second_parts],
        [
            (one, wide, f32),
            (one, wide, bf16),
            (one, ff_wide, bf16),
            (one, ff_wide, bf16),
            (one, ff_wide, bf16),
            (one, wide, bf16),
            (one, wide, bf16),
            (one, wide, f32),
            (one, (seqs, 1, MODEL_WIDTH), f32),
        ],
        scratch=[
            pltpu.VMEM((MODEL_WIDTH, QUERY_WIDTH), bf16),
            pltpu.VMEM((FF, MODEL_WIDTH), bf16),
            pltpu.VMEM((FF, MODEL_WIDTH), bf16),
            pltpu.VMEM((MODEL_WIDTH, FF), bf16),
            pltpu.VMEM((2, ctx) + same.shape[1:], bf16),
            pltpu.SemaphoreType.DMA((4, chunks)),
        ],
        scalars=(place,),
        us=26.0,
    )
    block_output = give(block_local)
    def reduced_packs(own_packs, other_packs, flip):
        got = lax.ppermute(other_packs, "ctx", partners)
        terms = [lambda k=k: plus(own_packs[k], got[k]) for k in range(chunks)]
        return ring_scatter(terms, flip)

    def outer_sums(earlier):
        behind = traces[-1]
        dattn_, dgate_ = join([dattn, dgate], earlier)
        (dup_,) = join([dup], *behind[0])
        (hidden_,) = join([hidden], *behind[1])
        packs = call(
            pack_second_kernel,
            1,
            [
                (whole, weight_grad(dattn_, attn).astype(bf16)),
                (whole, weight_grad(dgate_, normed_two).astype(bf16)),
                (whole, weight_grad(dup_, normed_two).astype(bf16)),
                (whole, weight_grad(cot, hidden_).astype(bf16)),
            ],
            [(anywhere, same.shape, bf16)] * 4,
            scalars=(place,),
            scratch=[
                pltpu.VMEM((2, ctx) + same.shape[1:], bf16),
                pltpu.SemaphoreType.DMA((4, chunks)),
            ],
            us=7.7,
            after=behind[2],
        )
        got = [lax.ppermute(part, "ctx", partners) for part in packs[2:]]
        if two_planes:
            sent = lax.ppermute(plus(packs[1], got[1]).astype(bf16), "fsdp", planes)
            terms = [lambda k=k: plus(packs[0][k], got[0][k], sent[k]) for k in range(chunks)]
            sums, trace = ring_scatter(terms, True)
            sums, before_last, before_final = [sums], got, [sent]
        else:
            sums = [
                ring_scatter(
                    [lambda k=k, i=i: plus(packs[i][k], got[i][k]) for k in range(chunks)], True
                )[0]
                for i in range(2)
            ]
            before_last, before_final, trace = got, [], [[], []]
        base = f_cols + o_cols
        result = []
        for pick in (
            lambda part: part[base:, REST : REST + half],
            lambda part: part[:f_cols, :half],
            lambda part: part[:f_cols, half:MODEL_WIDTH],
            lambda part: jnp.concatenate([part[f_cols:base], part[base:, :REST]], axis=1),
        ):
            if two_planes:
                result.append(pick(sums[0]))
            else:
                result.append(rows_scatter(jnp.concatenate([pick(part) for part in sums], axis=1)))
        return result, before_last, before_final, trace[1]

    dinputs, dalls, gain_one_grads, traces = [], [], [], []
    last = seqs - 1
    for first, count in ((0, last), (last, 1)):
        these = since(first)
        waits = []
        if first == last:
            outer_reduced, before_last, before_final, before_pack = outer_sums(dquery)
            waits = before_last
        dquery, *dkv = call(
            functools.partial(attend_back_kernel, chunks, first),
            count,
            [(these, query)]
            + [(these, chunk) for chunk in kv_all]
            + [(these, array) for array in (attn, dout, logs, cosine, sine)],
            [(one, (count,) + wide[1:], bf16)] + [(one, (count, rows, KV_PACKED), bf16)] * chunks,
            scalars=(blocks,),
            scratch=[
                pltpu.VMEM((length, KV_PACKED), bf16),
                pltpu.VMEM((KV_HEADS, 2 * GROUP * blk, PACK), bf16),
                pltpu.VMEM((KV_HEADS, PACK, 2 * GROUP * blk), bf16),
                pltpu.VMEM(tile_rows, f32),
                pltpu.VMEM(tile_rows, f32),
                pltpu.VMEM((KV_PACKED, length), f32),
                pltpu.VMEM((length, KV_PACKED), bf16),
            ],
            us=17.0 * count * load,
            after=waits,
        )
        dkv_own, trace = ring_scatter(
            [lambda k=k, dkv=dkv: dkv[k] for k in range(chunks)],
            first > 0,
            traces[-1][-1] if traces else (),
        )
        traces.append(trace)
        dinput, dall, gain_one_grad = call(
            final_kernel,
            count,
            [
                (these, x),
                (whole, gain_one),
                (one, dquery),
                (one, dkv_own),
                (these, dresid),
                (these, cosine),
                (these, sine),
                (whole, inward),
            ],
            [
                (one, (count,) + wide[1:], f32),
                (one, (count, rows, INNER), bf16),
                (one, (count, 1, MODEL_WIDTH), f32),
            ],
            us=2.0 * count,
            after=before_final if first == last else (),
        )
        dinputs.append(dinput)
        dalls.append(dall)
        gain_one_grads.append(jnp.sum(gain_one_grad, axis=0))
    input_gradient = give(jnp.concatenate(dinputs, axis=0))
    gains_grad = jnp.concatenate([sum(gain_one_grads), jnp.sum(gain_two_grad, axis=0)], axis=0)
    packs = (chunks, first_part.shape[0], LANES)
    first_packs = call(
        functools.partial(pack_first_kernel, q_cols, kv_cols, len(dalls)),
        1,
        [(whole, normed_one)] + [(whole, dall) for dall in dalls] + [(whole, gains_grad)],
        [(whole, packs, bf16), (whole, packs, bf16)],
        scalars=(where,),
        scratch=[pltpu.VMEM((INNER, MODEL_WIDTH), f32)],
        us=3.5,
        after=before_pack,
    )
    first_sum = rows_scatter(reduced_packs(*first_packs, False)[0][:, :MODEL_WIDTH])
    reduced = (
        first_sum[:q_cols],
        first_sum[q_cols : q_cols + kv_cols],
        first_sum[q_cols + kv_cols : q_cols + 2 * kv_cols],
        *outer_reduced,
    )
    gains_total = first_sum[q_cols + 2 * kv_cols : first_used].T
    rates = (
        (MODEL_WIDTH // 4) ** (-0.5),
        MODEL_WIDTH ** (-0.5),
        MODEL_WIDTH ** (-0.5),
        (MODEL_WIDTH // 32) ** (-0.5),
        MODEL_WIDTH ** (-0.5),
        MODEL_WIDTH ** (-0.5),
        (FF // 2) ** (-0.5),
    )
    firsts = (
        query_first,
        key_first_moment,
        value_first_moment,
        output_first,
        gate_first,
        up_first,
        down_first,
    )
    seconds = (
        query_second,
        key_second_moment,
        value_second_moment,
        output_second,
        gate_second,
        up_second,
        down_second,
    )
    results = [
        adam_update(
            masters[member], firsts[member], seconds[member], reduced[member].T, rates[member], DECAY
        )
        for member in range(7)
    ]
    results.append(adam_update(norm_gains, gains_first, gains_second, gains_total, GAIN_RATE, 0.0))
    new_weights = [result[0] for result in results]
    new_firsts = [result[1] for result in results]
    new_seconds = [result[2] for result in results]
    return tuple([block_output, input_gradient] + new_weights + new_firsts + new_seconds)


def solution(mesh):
    sequences = P("fsdp", "ctx", None)
    matrix = P("fsdp", "ctx")
    gains = P("fsdp", None)
    state = (matrix,) * 7 + (gains,)
    return jax.shard_map(
        body,
        mesh=mesh,
        in_specs=(sequences, sequences, P("fsdp", None)) + state * 3,
        out_specs=(sequences, sequences) + state * 3,
        check_vma=False,
    )
```
